32 devices in a mesh: dp: 8 (over z, y), section: 4 (over x, core).
Axes of the slice: x: 2, y: 2, z: 4, core: 2. Of those that a mesh axis runs over, the one named last changes fastest.
Arguments:
- inputs: bfloat16 [16, 1024, 512], P('dp'), may hold values from -6 to 6
- lengths: int32 [16], P('dp'), may hold values from 65 to 1024, as said below
- attention_gain: float32 [2, 512], replicated, may hold values from 0.5 to 1.5
- attention_bias: float32 [2, 512], replicated, may hold values from -3 to 3
- project_weight: bfloat16 [2, 512, 1536], replicated, may hold values from -0.25 to 0.25
- output_weight: bfloat16 [2, 512, 512], replicated, may hold values from -0.75 to 0.75
- output_bias: float32 [2, 512], replicated, may hold values from -3 to 3
- feed_gain: float32 [2, 512], replicated, may hold values from 0.5 to 1.5
- feed_bias: float32 [2, 512], replicated, may hold values from -3 to 3
- up_weight: bfloat16 [2, 512, 2048], replicated, may hold values from -0.25 to 0.25
- up_bias: float32 [2, 2048], replicated, may hold values from -3 to 3
- down_weight: bfloat16 [2, 2048, 512], replicated, may hold values from -0.125 to 0.125
- down_bias: float32 [2, 512], replicated, may hold values from -3 to 3
- cotangent: bfloat16 [16, 1024, 512], P('dp'), may hold values from -6 to 6
Outputs:
- outputs: bfloat16 [16, 1024, 512], P('dp', None, 'section')
- input_grad: bfloat16 [16, 1024, 512], P('dp', None, 'section')
- attention_gain_grad: float32 [2, 512], P(None, 'dp')
- attention_bias_grad: float32 [2, 512], P(None, 'dp')
- project_weight_grad: float32 [2, 512, 1536], P(None, 'dp')
- output_weight_grad: float32 [2, 512, 512], P(None, 'dp')
- output_bias_grad: float32 [2, 512], P(None, 'dp')
- feed_gain_grad: float32 [2, 512], P(None, 'dp')
- feed_bias_grad: float32 [2, 512], P(None, 'dp')
- up_weight_grad: float32 [2, 512, 2048], P(None, 'dp')
- up_bias_grad: float32 [2, 2048], P(None, 'dp')
- down_weight_grad: float32 [2, 2048, 512], P(None, 'dp')
- down_bias_grad: float32 [2, 512], P(None, 'dp')
The draws below stay inside these ranges and needn't reach their ends.
Inputs may be any that keep to these rules, and one draw needn't show every extreme that they name: `lengths`: each index of dp holds one sequence of exactly 1024 tokens among its 2.
All inputs are finite; a program needn't handle non-finite values.
Results may differ from the reference program's by a relative error of at most 0.0085.
Values may be sent and summed in bfloat16 or wider, within the bound.
No kernel may reach another device: no remote copies, remote signals or barrier semaphores. Data moves between devices by JAX's collectives and lax.ppermute only.
A program may use at most 256 MiB of HBM per device.

```python
import jax
import jax.numpy as jnp
from jax import lax

D = 512
HEADS = 8
HEAD_DIM = 64
FF = 2048
BLOCK = 16
LAYERS = 2
MICRO = 2
SEQ = 1024
BATCH = 16


def draw_lengths(key, part):
    key = jax.random.fold_in(key, 7)
    key_bucket, key_spread, key_chosen = jax.random.split(key, 3)
    rolled = jax.random.randint(key_bucket, (BATCH,), 0, 8)
    bucket_num = (rolled >= 4).astype(jnp.int32) + (rolled >= 6).astype(jnp.int32) + (rolled >= 7).astype(jnp.int32)
    upper = jnp.where(bucket_num == 0, SEQ, jnp.where(bucket_num == 1, SEQ // 2, jnp.where(bucket_num == 2, SEQ // 4, SEQ // 8)))
    lowest = upper // 2 + 1
    spread = jax.random.randint(key_spread, (BATCH,), 0, SEQ)
    length = lowest + spread % (upper - lowest + 1)
    chosen = jax.random.randint(key_chosen, (BATCH // MICRO, 1), 0, MICRO)
    forced = (jnp.arange(MICRO)[None, :] == chosen).reshape(BATCH)
    return jnp.where(forced, SEQ, length).astype(jnp.int32)


def spiked(values, key, source, target, shards_of, factor):
    def block_of(position):
        return (jnp.arange(values.shape[position]) // (values.shape[position] // shards_of)).reshape((-1,) + (1,) * (values.ndim - 1 - position))

    one_side = jax.random.permutation(key, shards_of)[block_of(target)]
    second = (block_of(target) + shards_of // 2) % shards_of
    return jnp.where((block_of(source) == one_side) | (block_of(source) == second), factor * values, values)


def level_of(rng, shape, pieces, least, largest):
    def one(position, blocks):
        heights = jax.random.uniform(jax.random.fold_in(jax.random.fold_in(rng, 6), position), (blocks,), jnp.float32, least / len(pieces), largest / len(pieces))
        return jnp.repeat(jnp.exp(heights), shape[position] // blocks).reshape((-1,) + (1,) * (len(shape) - position - 1))

    gain = one(*pieces[0])
    for cut in pieces[1:]:
        gain = gain * one(*cut)
    return gain


def bell_draw(rng, dims, width, most, pieces=(), held_as=jnp.bfloat16):
    values = jax.random.normal(rng, dims, jnp.float32) * width
    if len(pieces) > 0:
        values = level_of(rng, dims, pieces, -0.22, 0.18) * values
    return jnp.clip(values, min=-most, max=most).astype(held_as)


def noise_with(key, shape, deviation, most, shards, heavy, kind=jnp.bfloat16):
    values = deviation * jax.random.normal(key, shape, jnp.float32)
    if shards:
        values = values * level_of(key, shape, shards, -0.22, 0.18)
    return jnp.clip(spiked(values, jax.random.fold_in(key, 3), *heavy), -most, most).astype(kind)


def setup_inputs(seed: int = 0) -> dict:
    arg_keys = jax.random.split(jax.random.key(seed), 15)
    inputs = bell_draw(arg_keys[0], (BATCH, SEQ, D), 1.0, 6.0, ((0, 8),))
    lengths = draw_lengths(jax.random.fold_in(arg_keys[14], 71), 0)
    attention_gain = jnp.clip(1.0 + 0.1 * jax.random.normal(arg_keys[2], (LAYERS, D), jnp.float32), 0.5, 1.5)
    attention_bias = bell_draw(arg_keys[3], (LAYERS, D), 0.5, 3.0, (), jnp.float32)
    project_weight = bell_draw(arg_keys[4], (LAYERS, D, 3 * D), D ** -0.5, 0.25)
    output_weight = bell_draw(arg_keys[5], (LAYERS, D, D), (D // 8) ** -0.5, 0.75)
    output_bias = bell_draw(arg_keys[6], (LAYERS, D), 0.5, 3.0, (), jnp.float32)
    feed_gain = jnp.clip(1.0 + 0.1 * jax.random.normal(arg_keys[7], (LAYERS, D), jnp.float32), 0.5, 1.5)
    feed_bias = bell_draw(arg_keys[8], (LAYERS, D), 0.5, 3.0, (), jnp.float32)
    up_weight = bell_draw(arg_keys[9], (LAYERS, D, FF), D ** -0.5, 0.25)
    up_bias = bell_draw(arg_keys[10], (LAYERS, FF), 0.5, 3.0, (), jnp.float32)
    down_weight = bell_draw(arg_keys[11], (LAYERS, FF, D), FF ** -0.5, 0.125)
    down_bias = bell_draw(arg_keys[12], (LAYERS, D), 0.5, 3.0, (), jnp.float32)
    cotangent = noise_with(arg_keys[13], (BATCH, SEQ, D), 1.0, 6.0, ((0, 8),), (0, 2, 8, 2.0))
    return dict(inputs=inputs, lengths=lengths, attention_gain=attention_gain, attention_bias=attention_bias, project_weight=project_weight, output_weight=output_weight, output_bias=output_bias, feed_gain=feed_gain, feed_bias=feed_bias, up_weight=up_weight, up_bias=up_bias, down_weight=down_weight, down_bias=down_bias, cotangent=cotangent)


NORM_EPS = 1e-05
MASK_FILL = -1000000000.0
HIGHEST = lax.Precision.HIGHEST

@jax.custom_vjp
def low(v):
    return lax.optimization_barrier(v.astype(jnp.bfloat16)).astype(jnp.float32)

@jax.custom_vjp
def low_back(v):
    return v

def low_keep(v):
    return (low(v), None)

def low_pass(kept, grad):
    return (grad,)

def back_keep(v):
    return (v, None)

def back_low(kept, grad):
    return (low(grad),)
low.defvjp(low_keep, low_pass)
low_back.defvjp(back_keep, back_low)

def matmul(left, right):
    return jnp.dot(left, right, precision=HIGHEST, preferred_element_type=jnp.float32)

def layer_norm(rows_in, norm_gain, norm_bias):
    average = lax.optimization_barrier(jnp.mean(rows_in, axis=-1, keepdims=True))
    centred = rows_in - average
    variance = lax.optimization_barrier(jnp.mean(centred * centred, axis=-1, keepdims=True))
    return centred * lax.rsqrt(variance + NORM_EPS) * norm_gain + norm_bias

def hier_attention(queries, keys_in, values_in, live_mask):
    seq_total, head_count, head_size = queries.shape
    score_scale = head_size ** (-0.5)
    pair_len = 2 * BLOCK
    groups = seq_total // pair_len
    levels = groups.bit_length() - 1
    grouped_q = queries.reshape(groups, pair_len, head_count, head_size)
    grouped_k = keys_in.reshape(groups, pair_len, head_count, head_size)
    grouped_v = values_in.reshape(groups, pair_len, head_count, head_size)
    near_scores = jnp.einsum('gqhe,gkhe->gqhk', grouped_q, grouped_k, precision=HIGHEST) * score_scale
    near_scores = jnp.where(live_mask.reshape(groups, 1, 1, pair_len) > 0, near_scores, MASK_FILL)
    logits = [near_scores.reshape(seq_total, head_count, pair_len)]
    coarse_values = []
    key_sum = keys_in * live_mask[:, None, None]
    value_sum = values_in * live_mask[:, None, None]
    counts = live_mask
    for level_num in range(1, levels + 1):
        key_sum = key_sum.reshape(-1, 2, head_count, head_size).sum(axis=1)
        value_sum = value_sum.reshape(-1, 2, head_count, head_size).sum(axis=1)
        counts = counts.reshape(-1, 2).sum(axis=1)
        divisor = jnp.maximum(counts, 1.0)[:, None, None]
        span_len = BLOCK * 2 ** level_num
        blocks = seq_total // span_len
        far_keys = (key_sum / divisor).reshape(blocks // 2, 2, BLOCK, head_count, head_size)[:, ::-1]
        far_keys = far_keys.reshape(blocks, BLOCK, head_count, head_size)
        far_values = (value_sum / divisor).reshape(blocks // 2, 2, BLOCK, head_count, head_size)[:, ::-1]
        far_values = far_values.reshape(blocks, BLOCK, head_count, head_size)
        far_counts = counts.reshape(blocks // 2, 2, BLOCK)[:, ::-1].reshape(blocks, BLOCK)
        local_q = queries.reshape(blocks, span_len, head_count, head_size)
        far_scores = jnp.einsum('bqhe,bkhe->bqhk', local_q, far_keys, precision=HIGHEST) * score_scale
        far_scores = far_scores + jnp.log(jnp.maximum(far_counts, 1.0))[:, None, None, :]
        far_scores = jnp.where(far_counts[:, None, None, :] > 0, far_scores, MASK_FILL)
        logits.append(far_scores.reshape(seq_total, head_count, BLOCK))
        coarse_values.append(far_values)
    joined = jnp.concatenate(logits, axis=-1)
    top_score = lax.optimization_barrier(jnp.max(joined, axis=-1, keepdims=True))
    weights = jnp.exp(joined - top_score)
    weights = weights / lax.optimization_barrier(jnp.sum(weights, axis=-1, keepdims=True))
    near_weights = weights[..., :pair_len].reshape(groups, pair_len, head_count, pair_len)
    output = jnp.einsum('gqhk,gkhe->gqhe', near_weights, grouped_v, precision=HIGHEST)
    output = output.reshape(seq_total, head_count, head_size)
    for level_num in range(1, levels + 1):
        span_len = BLOCK * 2 ** level_num
        blocks = seq_total // span_len
        offset = pair_len + BLOCK * (level_num - 1)
        far_weights = weights[..., offset:offset + BLOCK].reshape(blocks, span_len, head_count, BLOCK)
        extra = jnp.einsum('bqhk,bkhe->bqhe', far_weights, coarse_values[level_num - 1], precision=HIGHEST)
        output = output + extra.reshape(seq_total, head_count, head_size)
    return output * live_mask[:, None, None]

def attention_part(stream, live_mask, norm_gain, norm_bias, w_proj, w_back, back_bias):
    seq_total, model_width = stream.shape
    normed = low(layer_norm(stream, norm_gain, norm_bias))
    projected = low_back(low(matmul(normed, w_proj)))
    split_heads = projected.reshape(seq_total, 3, HEADS, HEAD_DIM)
    attended = hier_attention(split_heads[:, 0], split_heads[:, 1], split_heads[:, 2], live_mask)
    attended = low(attended.reshape(seq_total, model_width))
    return stream + matmul(attended, w_back) + back_bias

def feed_part(stream, norm_gain, norm_bias, w_first, first_bias, w_second, second_bias):
    normed = low(layer_norm(stream, norm_gain, norm_bias))
    preact = low_back(matmul(normed, w_first) + first_bias)
    hidden = low(jax.nn.gelu(preact, approximate=True))
    return stream + matmul(hidden, w_second) + second_bias

def passed(values_in):
    return low_back(low(values_in))

def forward(params, stream, live_mask):
    a_gain, a_bias, w_proj, w_back, back_bias, f_gain, f_bias, w_first, first_bias, w_second, second_bias = params
    for layer_num in range(2):
        stream = passed(attention_part(stream, live_mask, a_gain[layer_num], a_bias[layer_num], w_proj[layer_num], w_back[layer_num], back_bias[layer_num]))
        stream = feed_part(stream, f_gain[layer_num], f_bias[layer_num], w_first[layer_num], first_bias[layer_num], w_second[layer_num], second_bias[layer_num])
        if layer_num == 0:
            stream = passed(stream)
    return stream

def reference(inputs, lengths, attention_gain, attention_bias, project_weight, output_weight, output_bias, feed_gain, feed_bias, up_weight, up_bias, down_weight, down_bias, cotangent):
    params = tuple((tensor.astype(jnp.float32) for tensor in (attention_gain, attention_bias, project_weight, output_weight, output_bias, feed_gain, feed_bias, up_weight, up_bias, down_weight, down_bias)))
    positions = jnp.arange(SEQ, dtype=jnp.int32)

    def one_sequence(totals, sequence):
        rows_in, length, grad_rows = sequence
        live_mask = (positions < length).astype(jnp.float32)
        result, pullback = jax.vjp(lambda weights, stream: forward(weights, stream, live_mask), params, rows_in.astype(jnp.float32))
        weight_grads, stream_grad = pullback(grad_rows.astype(jnp.float32))
        totals = jax.tree.map(jnp.add, totals, weight_grads)
        return (totals, (result.astype(jnp.bfloat16), stream_grad.astype(jnp.bfloat16)))
    initial = jax.tree.map(jnp.zeros_like, params)
    totals, (outputs, input_grads) = lax.scan(one_sequence, initial, (inputs, lengths, cotangent))
    return (outputs, input_grads, totals[0], totals[1], totals[2], totals[3], totals[4], totals[5], totals[6], totals[7], totals[8], totals[9], totals[10])
```

```python
import functools

import jax
import jax.numpy as jnp
from jax import lax
from jax.experimental import pallas as pl
from jax.experimental.pallas import tpu as pltpu
from jax.sharding import PartitionSpec as P

FLOAT = jnp.float32
BRAIN = jnp.bfloat16
NORM_EPS = 1e-05
MASK_FILL = -1000000000.0
WIDTH = 512
TOKENS = 512
FF = 2048
GROUP = 32
GROUPS = TOKENS // GROUP
LEVELS = 5
KEYS = GROUP + 16 * LEVELS
HALF = 256
QROWS = 4 * GROUP
LEVEL_AT = (0, 256, 384, 448, 480)
POOLED = 496
MIB = 1024 * 1024

NN = (((1,), (0,)), ((), ()))
NT = (((1,), (1,)), ((), ()))
TN = (((0,), (0,)), ((), ()))


def dot(left, right, dims=NN):
    return lax.dot_general(left, right, dims, preferred_element_type=FLOAT)


def iota(shape, dim):
    return lax.broadcasted_iota(jnp.int32, shape, dim)


def normalise(rows):
    mean = jnp.mean(rows, axis=-1, keepdims=True)
    centred = rows - mean
    scale = lax.rsqrt(jnp.mean(centred * centred, axis=-1, keepdims=True) + NORM_EPS)
    return centred * scale, scale


def norm_into(source, gain, bias, target):
    for start in range(0, TOKENS, 64):
        rows = slice(start, start + 64)
        unit, _ = normalise(source[rows, :].astype(FLOAT))
        target[rows, :] = (unit * gain + bias).astype(BRAIN)


def norm_back(source, gain, grad_ref, through_ref, target, gain_out, bias_out):
    gain_sum = jnp.zeros((1, WIDTH), FLOAT)
    bias_sum = jnp.zeros((1, WIDTH), FLOAT)
    for start in range(0, TOKENS, 64):
        rows = slice(start, start + 64)
        unit, scale = normalise(source[rows, :].astype(FLOAT))
        grad = grad_ref[rows, :]
        gain_sum = gain_sum + jnp.sum(grad * unit, axis=0, keepdims=True)
        bias_sum = bias_sum + jnp.sum(grad, axis=0, keepdims=True)
        inner = grad * gain
        inner_mean = jnp.mean(inner, axis=-1, keepdims=True)
        slope = jnp.mean(inner * unit, axis=-1, keepdims=True)
        back = scale * (inner - inner_mean - unit * slope)
        target[rows, :] = (through_ref[rows, :].astype(FLOAT) + back).astype(BRAIN)
    gain_out[...] = gain_sum
    bias_out[...] = bias_sum


def pool_matrix(level, live):
    shape = (TOKENS >> level, TOKENS)
    key, token = iota(shape, 0), iota(shape, 1)
    inside = (lax.shift_right_logical(token, level) == key) & (token < live)
    return inside.astype(FLOAT).astype(BRAIN)


def pool_matrix_back(level, live):
    shape = (TOKENS, TOKENS >> level)
    token, key = iota(shape, 0), iota(shape, 1)
    inside = (lax.shift_right_logical(token, level) == key) & (token < live)
    return inside.astype(FLOAT).astype(BRAIN)


def counts(level, live, columns):
    key = iota((TOKENS >> level, columns), 0)
    return jnp.clip(live - (key << level), 0, 1 << level)


def project(normed, weight, target, start, stop, target_start=None):
    shift = 0 if target_start is None else target_start - start
    for column in range(start, stop, 256):
        target[:, column + shift : column + shift + 256] = dot(
            normed[...], weight[:, column : column + 256]
        ).astype(BRAIN)


def pool_keys(keyed, first_column, live, levels, coarse, row_at):
    for level in levels:
        matrix = pool_matrix(level, live)
        rows = TOKENS >> level
        inverse = 1.0 / jnp.maximum(counts(level, live, 256), 1).astype(FLOAT)
        at = row_at(level)
        for column in range(0, 1024, 256):
            sums = dot(matrix, keyed[:, first_column + column : first_column + column + 256])
            coarse[at : at + rows, column : column + 256] = (sums * inverse).astype(BRAIN)


def coarse_bias(live, other_live, bias):
    for level in range(1, LEVELS + 1):
        at, rows = LEVEL_AT[level - 1], TOKENS >> level
        of_level = live
        if level == LEVELS:
            at, of_level = POOLED, other_live
        number = counts(level, of_level, 128)
        bias[at : at + rows, :] = jnp.where(
            number > 0, jnp.log(jnp.maximum(number, 1).astype(FLOAT)), MASK_FILL
        )


def head_mask(value):
    shape = (QROWS, HALF)
    return jnp.where(iota(shape, 0) // GROUP == iota(shape, 1) // 64, value, 0.0).astype(BRAIN)


def spread(rows, mask):
    return jnp.concatenate([rows] * 4, axis=0) * mask


def gather_heads(wide):
    left = iota((GROUP, 128), 1) < 64
    low = jnp.where(left, wide[0:32, 0:128], wide[32:64, 0:128])
    high = jnp.where(left, wide[64:96, 128:256], wide[96:128, 128:256])
    return jnp.concatenate([low, high], axis=1)


def group_rows(group):
    at = []
    for level in range(1, LEVELS):
        at.append(LEVEL_AT[level - 1] + ((group >> (level - 1)) ^ 1) * 16)
    at.append(POOLED)
    return at


def aligned(value, multiple):
    return value if isinstance(value, int) else pl.multiple_of(value, multiple)


def key_block(qkv, coarse, group, part, half):
    column = WIDTH * (part + 1) + HALF * half
    coarse_column = WIDTH * part + HALF * half
    pieces = [qkv[pl.ds(aligned(group * GROUP, GROUP), GROUP), column : column + HALF]]
    for at in group_rows(group):
        pieces.append(coarse[pl.ds(aligned(at, 16), 16), coarse_column : coarse_column + HALF])
    return jnp.concatenate(pieces, axis=0)


def hier_forward(qkv, coarse, bias, prob, attended, live, unroll):
    mask = head_mask(0.125)

    def one(group):
        start = aligned(group * GROUP, GROUP)
        token = group * GROUP + iota((GROUP, 128), 0)
        near_bias = jnp.where(token < live, 0.0, MASK_FILL)
        key_bias = jnp.concatenate(
            [near_bias] + [bias[pl.ds(aligned(at, 16), 16), :] for at in group_rows(group)], axis=0
        )
        query_live = (group * GROUP + iota((GROUP, HALF), 0) < live).astype(FLOAT)
        for half in range(2):
            queries = spread(qkv[pl.ds(start, GROUP), half * HALF : (half + 1) * HALF], mask)
            keys = key_block(qkv, coarse, group, 0, half)
            values = key_block(qkv, coarse, group, 1, half)
            scores = dot(keys, queries, NT) + key_bias
            weights = jnp.exp(scores - jnp.max(scores, axis=0, keepdims=True))
            weights = weights * (1.0 / jnp.sum(weights, axis=0, keepdims=True))
            weights = weights.astype(BRAIN)
            prob[group, half, :, :] = weights
            output = gather_heads(dot(weights, values, TN)) * query_live
            attended[pl.ds(start, GROUP), half * HALF : (half + 1) * HALF] = output.astype(BRAIN)

    def body(step, carry):
        for k in range(unroll):
            one(step * unroll + k)
        return carry

    lax.fori_loop(0, GROUPS // unroll, body, 0)


def hier_backward(qkv, coarse, prob, grad_out, grad_q, grad_kv, grad_coarse, unroll):
    mask_q, mask_o = head_mask(0.125), head_mask(1.0)
    grad_coarse[LEVEL_AT[1] :, :] = jnp.zeros((TOKENS - LEVEL_AT[1], 2 * WIDTH), FLOAT)

    def one(group):
        start = aligned(group * GROUP, GROUP)
        at_rows = group_rows(group)
        for half in range(2):
            columns = slice(half * HALF, (half + 1) * HALF)
            queries = spread(qkv[pl.ds(start, GROUP), columns], mask_q)
            grads = spread(grad_out[pl.ds(start, GROUP), columns], mask_o)
            keys = key_block(qkv, coarse, group, 0, half)
            values = key_block(qkv, coarse, group, 1, half)
            weights_low = prob[group, half, :, :]
            weights = weights_low.astype(FLOAT)
            product = weights * dot(values, grads, NT)
            score_grad = product - weights * jnp.sum(product, axis=0, keepdims=True)
            score_grad = score_grad.astype(BRAIN)
            grad_q[pl.ds(start, GROUP), columns] = (
                gather_heads(dot(score_grad, keys, TN)) * 0.125
            ).astype(BRAIN)
            for part, block in enumerate((dot(score_grad, queries), dot(weights_low, grads))):
                to = slice(part * WIDTH + half * HALF, part * WIDTH + (half + 1) * HALF)
                grad_kv[pl.ds(start, GROUP), to] = block[0:GROUP]
                for level, at in enumerate(at_rows):
                    rows = pl.ds(aligned(at, 16), 16)
                    piece = block[GROUP + 16 * level : GROUP + 16 * level + 16]
                    if level == 0:
                        grad_coarse[rows, to] = piece
                    else:
                        grad_coarse[rows, to] += piece

    def body(step, carry):
        for k in range(unroll):
            one(step * unroll + k)
        return carry

    lax.fori_loop(0, GROUPS // unroll, body, 0)


def add_projected(stream, source, weight, bias, target):
    for column in range(0, WIDTH, 256):
        columns = slice(column, column + 256)
        total = dot(source[...], weight[:, columns])
        target[:, columns] = (stream[:, columns].astype(FLOAT) + total + bias[:, columns]).astype(
            BRAIN
        )


def feed_hidden(normed, weight, bias, hidden, slope):
    for column in range(0, FF, 256):
        columns = slice(column, column + 256)
        pre = dot(normed[...], weight[:, columns]) + bias[:, columns]
        square = pre * pre
        bent = jnp.tanh(0.7978845608 * pre * (1.0 + 0.044715 * square))
        half = 0.5 * (1.0 + bent)
        hidden[:, columns] = (pre * half).astype(BRAIN)
        inner = 0.7978845608 + (3 * 0.044715 * 0.7978845608) * square
        slope[:, columns] = (half + 0.5 * pre * (1.0 - bent * bent) * inner).astype(BRAIN)


def fetch(source, target, sem):
    copy = pltpu.make_async_copy(source, target, sem)
    copy.start()
    return copy


ANY = pl.BlockSpec(memory_space=pl.ANY)
VMEM = pl.BlockSpec(memory_space=pltpu.VMEM)
SMEM = pl.BlockSpec(memory_space=pltpu.SMEM)


def shape(dims, dtype=BRAIN):
    return jax.ShapeDtypeStruct(dims, dtype)


def call(body, outs, ins, scratch, limit, flops, name, far_outs=()):
    return pl.pallas_call(
        body,
        out_shape=outs + [shape(dims) for dims in far_outs],
        in_specs=ins,
        out_specs=[VMEM] * len(outs) + [ANY] * len(far_outs),
        scratch_shapes=scratch,
        compiler_params=pltpu.CompilerParams(vmem_limit_bytes=limit * MIB),
        cost_estimate=pl.CostEstimate(flops=flops, bytes_accessed=8 * MIB, transcendentals=0),
        name=name,
    )


def attend_and_feed(live, qkv, coarse, bias, prob, att, stream, w_out, out_bias, mid, gain, shift, normed, w_up, up_bias, hidden, slope):
    hier_forward(qkv, coarse, bias, prob, att, live, 2)
    w_out[1].wait()
    add_projected(stream, att, w_out[0], out_bias, mid)
    norm_into(mid, gain, shift, normed)
    w_up[1].wait()
    feed_hidden(normed, w_up[0], up_bias, hidden, slope)


def first_kernel(info, inputs, ag, ab, ob, fg, fb, ub, db, wp, wo, wu, wd,
                 qkv, coarse, prob, att, mid, hidden, slope, out, qkv_next, coarse_next, pooled,
                 mine, other, wp_at, wo_at, wu_at, wd_at, normed, far, bias, sems):
    seq, half, live, other_live = info[0], info[1], info[2], info[3]
    get_mine = fetch(inputs.at[seq, pl.ds(half * TOKENS, TOKENS)], mine, sems.at[0])
    get_other = fetch(inputs.at[seq, pl.ds((1 - half) * TOKENS, TOKENS)], other, sems.at[1])
    get_wp = fetch(wp.at[0], wp_at.at[0], sems.at[2])
    get_wo = fetch(wo.at[0], wo_at, sems.at[3])
    get_wu = fetch(wu.at[0], wu_at, sems.at[4])
    get_wd = fetch(wd.at[0], wd_at, sems.at[5])
    get_wp1 = fetch(wp.at[1], wp_at.at[1], sems.at[6])
    coarse_bias(live, other_live, bias)
    get_mine.wait()
    norm_into(mine, ag[0:1, :], ab[0:1, :], normed)
    get_wp.wait()
    project(normed, wp_at.at[0], qkv, 0, 3 * WIDTH)
    get_other.wait()
    norm_into(other, ag[0:1, :], ab[0:1, :], normed)
    project(normed, wp_at.at[0], far, WIDTH, 3 * WIDTH, 0)
    pool_keys(qkv, WIDTH, live, range(1, LEVELS + 1), coarse, lambda level: LEVEL_AT[level - 1])
    pool_keys(far, 0, other_live, (LEVELS,), coarse, lambda level: POOLED)
    attend_and_feed(live, qkv, coarse, bias, prob, att, mine, (wo_at, get_wo), ob[0:1, :], mid,
                    fg[0:1, :], fb[0:1, :], normed, (wu_at, get_wu), ub[0:1, :], hidden, slope)
    get_wd.wait()
    add_projected(mid, hidden, wd_at, db[0:1, :], out)
    norm_into(out, ag[1:2, :], ab[1:2, :], normed)
    get_wp1.wait()
    project(normed, wp_at.at[1], qkv_next, 0, 3 * WIDTH)
    pool_keys(qkv_next, WIDTH, live, range(1, LEVELS + 1), coarse_next, lambda level: LEVEL_AT[level - 1])
    coarse_next[POOLED:, :] = jnp.zeros((16, 2 * WIDTH), BRAIN)
    pooled[...] = coarse_next[LEVEL_AT[4] : POOLED, :]


def second_kernel(info, qkv, coarse_in, far, stream, ob, fg, fb, ub, db, wo, wu, wd,
                  coarse, prob, att, mid, hidden, slope, out,
                  wo_at, wu_at, wd_at, normed, bias, sems):
    live, other_live, section = info[2], info[3], info[4]
    get_wo = fetch(wo.at[1], wo_at, sems.at[0])
    get_wu = fetch(wu.at[1], wu_at, sems.at[1])
    get_wd = fetch(wd.at[1], wd_at, sems.at[2])
    coarse_bias(live, other_live, bias)
    coarse[0:POOLED, :] = coarse_in[0:POOLED, :]
    coarse[POOLED:, :] = far[...]
    attend_and_feed(live, qkv, coarse, bias, prob, att, stream, (wo_at, get_wo), ob[1:2, :], mid,
                    fg[1:2, :], fb[1:2, :], normed, (wu_at, get_wu), ub[1:2, :], hidden, slope)
    get_wd.wait()
    for column in range(0, WIDTH, 256):
        total = dot(hidden[...], wd_at[:, column : column + 256])
        for k in range(2):
            columns = slice(column + 128 * k, column + 128 * k + 128)
            final = mid[:, columns].astype(FLOAT) + total[:, 128 * k : 128 * k + 128] + db[1:2, columns]
            out[(column // 128 + k) ^ section, :, :] = final.astype(BRAIN)


def place(info, quarter, shard):
    section, dp = info[4], info[5]
    x, y, core = section >> 1, dp & 1, section & 1
    rel_core = (quarter & 1) ^ core
    rel_x = (quarter >> 1) ^ x
    rel_y = (shard & 1) ^ y
    first = jnp.where((quarter & 1) == 0, rel_x, rel_y)
    second = jnp.where((quarter & 1) == 0, rel_y, rel_x)
    return rel_core, first, second, (shard >> 1) ^ (dp >> 1)


def feed_back_kernel(layer, shards, grad_slice, info, grad_in, stream, hidden, slope, fg, fb, wu, wd,
                     target, sums, keep, send,
                     wu_at, wd_at, grad_at, normed, pre_grad, norm_grad, stage, sems, *more):
    get_wd = fetch(wd.at[layer], wd_at, sems.at[0])
    get_wu = fetch(wu.at[layer], wu_at, sems.at[1])
    if grad_slice:
        source = grad_in.at[info[0], pl.ds(info[1] * TOKENS, TOKENS)]
        fetch(source, grad_at, sems.at[2]).wait()
        grad = grad_at
    else:
        grad = grad_in
    norm_into(stream, fg[layer : layer + 1, :], fb[layer : layer + 1, :], normed)
    rows = FF // shards
    for start in range(0, FF, 256):
        block = dot(hidden[:, start : start + 256], grad[...], TN).astype(BRAIN)
        for at in range(0, 256, rows // 4):
            shard, quarter = (start + at) // rows, ((start + at) % rows) // (rows // 4)
            a, b, c, d = place(info, quarter, shard)
            stage[a, b, c, d, WIDTH // shards :, :] = block[at : at + rows // 4]
    get_wd.wait()
    for column in range(0, FF, 256):
        columns = slice(column, column + 256)
        back = dot(grad[...], wd_at[columns, :], NT) * slope[:, columns].astype(FLOAT)
        back = back.astype(BRAIN)
        pre_grad[:, columns] = back
        sums[3 + column // 512 : 4 + column // 512, column % 512 : column % 512 + 256] = jnp.sum(
            back.astype(FLOAT), axis=0, keepdims=True
        )
    for quarter in range(4):
        for k in range(2):
            at = quarter * 512 + 256 * k
            block = dot(normed[...], pre_grad[:, at : at + 256], TN).astype(BRAIN)
            rows = WIDTH // shards
            for shard in range(shards):
                a, b, c, d = place(info, quarter, shard)
                stage[a, b, c, d, 0:rows, 256 * k : 256 * k + 256] = block[shard * rows : (shard + 1) * rows]
    put_keep = fetch(stage.at[0], keep, sems.at[3])
    put_send = fetch(stage.at[1], send, sems.at[4])
    get_wu.wait()
    for column in range(0, WIDTH, 256):
        norm_grad[:, column : column + 256] = dot(pre_grad[...], wu_at[column : column + 256, :], NT)
    norm_back(stream, fg[layer : layer + 1, :], norm_grad, grad, target, sums.at[0:1, :], sums.at[1:2, :])
    sums[2:3, :] = jnp.sum(grad[...].astype(FLOAT), axis=0, keepdims=True)
    sums[7:8, :] = jnp.zeros((1, WIDTH), FLOAT)
    put_keep.wait()
    put_send.wait()


def attend_back_kernel(layer, info, grad, qkv, coarse, prob, wo,
                       grad_q, grad_kv, grad_coarse, far_grad,
                       wo_at, grad_out, sems):
    live = info[2]
    fetch(wo.at[layer], wo_at, sems.at[0]).wait()
    for column in range(0, WIDTH, 256):
        back = dot(grad[...], wo_at[column : column + 256, :], NT)
        back = back * (iota((TOKENS, 256), 0) < live).astype(FLOAT)
        grad_out[:, column : column + 256] = back.astype(BRAIN)
    hier_backward(qkv, coarse, prob, grad_out, grad_q, grad_kv, grad_coarse, 2)
    far_grad[...] = grad_coarse[POOLED:, :]


def project_back_kernel(layer, shards, slice_in, split_out, info, grad, stream_in, att, grad_q, grad_kv, grad_coarse,
                        far_grad, ag, ab, wp,
                        target, sums, keep, send,
                        wp_at, stream_at, normed, full, norm_grad, low_coarse, stage, sems, *more):
    live, section = info[2], info[4]
    get_wp = fetch(wp.at[layer], wp_at, sems.at[0])
    if slice_in:
        source = stream_in.at[info[0], pl.ds(info[1] * TOKENS, TOKENS)]
        fetch(source, stream_at, sems.at[1]).wait()
        stream = stream_at
    else:
        stream = stream_in
    norm_into(stream, ag[layer : layer + 1, :], ab[layer : layer + 1, :], normed)
    full[:, 0:WIDTH] = grad_q[...]
    for level in range(1, LEVELS + 1):
        at, rows = LEVEL_AT[level - 1], TOKENS >> level
        inverse = 1.0 / jnp.maximum(counts(level, live, 1024), 1).astype(FLOAT)
        source = far_grad[...] if level == LEVELS else grad_coarse[at : at + rows, :]
        low_coarse[at : at + rows, :] = (source * inverse).astype(BRAIN)
    low_coarse[POOLED:, :] = jnp.zeros((16, 2 * WIDTH), BRAIN)
    for column in range(0, 1024, 256):
        columns = slice(column, column + 256)
        total = grad_kv[:, columns]
        for level in range(1, LEVELS + 1):
            at, rows = LEVEL_AT[level - 1], TOKENS >> level
            total = total + dot(pool_matrix(level, live), low_coarse[at : at + rows, columns], TN)
        full[:, WIDTH + column : WIDTH + column + 256] = total.astype(BRAIN)
    rows = WIDTH // shards
    for quarter in range(4):
        left = dot(normed[...], full[:, quarter * 384 : quarter * 384 + 384], TN).astype(BRAIN)
        right = dot(att[...], grad[:, quarter * 128 : quarter * 128 + 128], TN).astype(BRAIN)
        for shard in range(shards):
            a, b, c, d = place(info, quarter, shard)
            stage[a, b, c, d, :, 0:384] = left[shard * rows : (shard + 1) * rows]
            stage[a, b, c, d, :, 384:512] = right[shard * rows : (shard + 1) * rows]
    put_keep = fetch(stage.at[0], keep, sems.at[2])
    put_send = fetch(stage.at[1], send, sems.at[3])
    get_wp.wait()
    for column in range(0, WIDTH, 256):
        norm_grad[:, column : column + 256] = dot(full[...], wp_at[column : column + 256, :], NT)
    result = more[0] if split_out else target
    norm_back(stream, ag[layer : layer + 1, :], norm_grad, grad, result, sums.at[0:1, :], sums.at[1:2, :])
    if split_out:
        for quarter in range(4):
            target[quarter ^ section, :, :] = result[:, quarter * 128 : quarter * 128 + 128]
    sums[2:3, :] = jnp.sum(grad[...].astype(FLOAT), axis=0, keepdims=True)
    sums[3:8, :] = jnp.zeros((5, WIDTH), FLOAT)
    put_keep.wait()
    put_send.wait()


def finish_feed_kernel(layers, shards, info, *refs):
    section = info[4]
    pieces, rest = refs[: 4 * layers], refs[4 * layers :]
    outs, rest = rest[:4], rest[4:]
    up, down, output, sems = rest
    copies = []
    for k in range(4):
        owner = section ^ k
        copies.append(
            fetch(outs[k], output.at[owner >> 1, pl.ds((owner & 1) * TOKENS, TOKENS)], sems.at[k])
        )
    rows = WIDTH // shards
    for layer in range(layers):
        for k in range(4):
            piece = pieces[layer * 4 + k]
            owner = section ^ k
            up[layer, :, pl.ds(pl.multiple_of(owner * 512, 512), 512)] = piece[0:rows, :].astype(FLOAT)
            down[layer, pl.ds(pl.multiple_of(owner * rows, rows), rows), :] = piece[rows:, :].astype(FLOAT)
    for copy in copies:
        copy.wait()


def finish_attend_kernel(layers, shards, info, *refs):
    section, dp = info[4], info[5]
    pieces, rest = refs[: 4 * layers], refs[4 * layers :]
    grads, rest = rest[:4], rest[4:]
    smalls, proj, back, gain_a, bias_a, bias_o, gain_f, bias_f, bias_u, bias_d, input_grad, sems = rest
    copies = []
    for k in range(4):
        owner = section ^ k
        copies.append(
            fetch(grads[k], input_grad.at[owner >> 1, pl.ds((owner & 1) * TOKENS, TOKENS)], sems.at[k])
        )
    for layer in range(layers):
        for k in range(4):
            piece = pieces[layer * 4 + k]
            owner = section ^ k
            proj[layer, :, pl.ds(pl.multiple_of(owner * 384, 128), 384)] = piece[:, 0:384].astype(FLOAT)
            back[layer, :, pl.ds(pl.multiple_of(owner * 128, 128), 128)] = piece[:, 384:].astype(FLOAT)
    width = WIDTH // shards
    pick = (iota((WIDTH, width), 0) == dp * width + iota((WIDTH, width), 1)).astype(FLOAT)
    taken = lax.dot_general(smalls[...], pick, NN, precision=lax.Precision.HIGHEST, preferred_element_type=FLOAT)
    for layer in range(2):
        feed, attend = (16, 24) if layer == 0 else (0, 8)
        gain_f[layer : layer + 1, :] = taken[feed : feed + 1]
        bias_f[layer : layer + 1, :] = taken[feed + 1 : feed + 2]
        bias_d[layer : layer + 1, :] = taken[feed + 2 : feed + 3]
        gain_a[layer : layer + 1, :] = taken[attend : attend + 1]
        bias_a[layer : layer + 1, :] = taken[attend + 1 : attend + 2]
        bias_o[layer : layer + 1, :] = taken[attend + 2 : attend + 3]
    wide = FF // shards
    per_row = WIDTH // wide if wide <= WIDTH else 1
    place_in_row = dp % per_row
    pick = (iota((WIDTH, wide), 0) == place_in_row * wide + iota((WIDTH, wide), 1)).astype(FLOAT)
    taken = lax.dot_general(smalls[...], pick, NN, precision=lax.Precision.HIGHEST, preferred_element_type=FLOAT)
    for layer in range(2):
        feed = 16 if layer == 0 else 0
        row = jnp.zeros((1, wide), FLOAT)
        for k in range(4):
            row = jnp.where(dp // per_row == k, taken[feed + 3 + k : feed + 4 + k], row)
        bias_u[layer : layer + 1, :] = row
    for copy in copies:
        copy.wait()


def swap(block, partner):
    sections = lax.axis_size("section")
    pairs = []
    for dp in range(lax.axis_size("dp")):
        for section in range(sections):
            to_dp, to_section = partner(dp, section)
            pairs.append((dp * sections + section, to_dp * sections + to_section))
    return lax.ppermute(block, ("dp", "section"), pairs)


def over_section(block, bits):
    return swap(block, lambda dp, section: (dp, section ^ bits))


def first_axis(dp, section):
    return (dp, section ^ 2) if section & 1 == 0 else (dp ^ 1, section)


def second_axis(dp, section):
    return (dp ^ 1, section) if section & 1 == 0 else (dp, section ^ 2)


def added(*blocks):
    total = blocks[0].astype(FLOAT)
    for block in blocks[1:]:
        total = total + block.astype(FLOAT)
    return total.astype(blocks[0].dtype)


def scatter_sum(keep, send):
    came = over_section(send, 1)
    give = added(keep[1], came[1])
    came_first = swap(give, first_axis)
    mine = added(keep[0], came[0])
    give = added(mine[1], came_first[1])
    came_second = swap(give, second_axis)
    mine = added(mine[0], came_first[0])
    mine = added(mine, came_second)
    bit = 2
    while mine.shape[0] > 1:
        ways = min(4, mine.shape[0])
        mine = mine.reshape((mine.shape[0] // ways, ways) + mine.shape[1:])
        pieces = [mine[:, 0]]
        for k in range(1, ways):
            pieces.append(swap(mine[:, k], lambda dp, section, k=k, bit=bit: (dp ^ (k * bit), section)))
        mine = added(*pieces)
        bit *= ways
    return mine[0]


def full_sum(block):
    block = block + over_section(block, 1)
    ways = [lambda dp, section: (dp, section ^ 2), lambda dp, section: (dp ^ 1, section),
            lambda dp, section: (dp ^ 1, section ^ 2)]
    block = added(block, *[swap(block, way) for way in ways])
    bit, left = 2, lax.axis_size("dp") // 2
    while left > 1:
        count = min(4, left)
        block = added(block, *[
            swap(block, lambda dp, section, k=k, bit=bit: (dp ^ (k * bit), section)) for k in range(1, count)
        ])
        left //= count
        bit *= count
    return block


def over_all_sections(block):
    return [block] + [over_section(block, k) for k in range(1, 4)]


def exchange_pieces(pieces):
    return [pieces[0]] + [over_section(pieces[k], k) for k in range(1, 4)]


def local(inputs, lengths, ag, ab, wp, wo, ob, fg, fb, wu, ub, wd, db, cotangent):
    shards = lax.axis_size("dp")
    section, dp = lax.axis_index("section"), lax.axis_index("dp")
    seq, half = section // 2, section % 2
    length = lengths[seq]
    live = jnp.clip(length - half * TOKENS, 0, TOKENS)
    other_live = jnp.clip(length - (1 - half) * TOKENS, 0, TOKENS)
    info = jnp.stack([seq, half, live, other_live, section, dp]).astype(jnp.int32)

    rows = shape((TOKENS, WIDTH))
    wide = shape((TOKENS, FF))
    tall = shape((TOKENS, 3 * WIDTH))
    coarse_shape = shape((TOKENS, 2 * WIDTH))
    prob_shape = shape((GROUPS, 2, KEYS, QROWS))
    weights_vmem = [pltpu.VMEM((WIDTH, WIDTH), BRAIN), pltpu.VMEM((WIDTH, FF), BRAIN), pltpu.VMEM((FF, WIDTH), BRAIN)]

    (qkv0, coarse0, prob0, att0, mid0, hidden0, slope0, stream1, qkv1, coarse1, pooled) = call(
        first_kernel,
        [tall, coarse_shape, prob_shape, rows, rows, wide, wide, rows, tall, coarse_shape, shape((16, 2 * WIDTH))],
        [SMEM, ANY] + [VMEM] * 7 + [ANY] * 4,
        [pltpu.VMEM((TOKENS, WIDTH), BRAIN)] * 2
        + [pltpu.VMEM((2, WIDTH, 3 * WIDTH), BRAIN)]
        + weights_vmem
        + [pltpu.VMEM((TOKENS, WIDTH), BRAIN), pltpu.VMEM((TOKENS, 2 * WIDTH), BRAIN),
           pltpu.VMEM((TOKENS, 128), FLOAT), pltpu.SemaphoreType.DMA((7,))],
        48, 12 * 10**9, "layer_zero_forward",
    )(info, inputs, ag, ab, ob, fg, fb, ub, db, wp, wo, wu, wd)
    far = over_section(pooled, 1)
    (coarse1, prob1, att1, mid1, hidden1, slope1, out_pieces) = call(
        second_kernel,
        [coarse_shape, prob_shape, rows, rows, wide, wide, shape((4, TOKENS, 128))],
        [SMEM] + [VMEM] * 9 + [ANY] * 3,
        weights_vmem + [pltpu.VMEM((TOKENS, WIDTH), BRAIN), pltpu.VMEM((TOKENS, 128), FLOAT), pltpu.SemaphoreType.DMA((3,))],
        48, 8 * 10**9, "layer_one_forward",
    )(info, qkv1, coarse1, far, stream1, ob, fg, fb, ub, db, wo, wu, wd)

    half_dims = (2, 2, shards // 2)

    def feed_back(layer, grad, stream, hidden, slope):
        block = half_dims + (WIDTH // shards + FF // shards // 4, WIDTH)
        sliced = grad.ndim == 3
        return call(
            functools.partial(feed_back_kernel, layer, shards, sliced),
            [rows, shape((8, WIDTH), FLOAT)],
            [SMEM, ANY if sliced else VMEM] + [VMEM] * 5 + [ANY] * 2,
            [pltpu.VMEM((WIDTH, FF), BRAIN), pltpu.VMEM((FF, WIDTH), BRAIN), pltpu.VMEM((TOKENS, WIDTH), BRAIN),
             pltpu.VMEM((TOKENS, WIDTH), BRAIN), pltpu.VMEM((TOKENS, FF), BRAIN), pltpu.VMEM((TOKENS, WIDTH), FLOAT),
             pltpu.VMEM((2,) + block, BRAIN), pltpu.SemaphoreType.DMA((5,))],
            48, 6 * 10**9, "feed_back", [block] * 2,
        )(info, grad, stream, hidden, slope, fg, fb, wu, wd)

    def attend_back(layer, grad, qkv, coarse, prob):
        return call(
            functools.partial(attend_back_kernel, layer),
            [rows, shape((TOKENS, 2 * WIDTH), FLOAT), shape((TOKENS, 2 * WIDTH), FLOAT), shape((16, 2 * WIDTH), FLOAT)],
            [SMEM] + [VMEM] * 4 + [ANY],
            [pltpu.VMEM((WIDTH, WIDTH), BRAIN), pltpu.VMEM((TOKENS, WIDTH), BRAIN), pltpu.SemaphoreType.DMA((1,))],
            48, 5 * 10**9, "attend_back",
        )(info, grad, qkv, coarse, prob, wo)

    def project_back(layer, grad, stream, att, grad_q, grad_kv, grad_coarse, far_grad):
        block = half_dims + (WIDTH // shards, WIDTH)
        sliced = stream.ndim == 3
        split = layer == 0
        scratch = [
            pltpu.VMEM((WIDTH, 3 * WIDTH), BRAIN), pltpu.VMEM((TOKENS, WIDTH), BRAIN), pltpu.VMEM((TOKENS, WIDTH), BRAIN),
            pltpu.VMEM((TOKENS, 3 * WIDTH), BRAIN), pltpu.VMEM((TOKENS, WIDTH), FLOAT),
            pltpu.VMEM((TOKENS, 2 * WIDTH), BRAIN), pltpu.VMEM((2,) + block, BRAIN), pltpu.SemaphoreType.DMA((4,)),
        ]
        if split:
            scratch.append(pltpu.VMEM((TOKENS, WIDTH), BRAIN))
        return call(
            functools.partial(project_back_kernel, layer, shards, sliced, split),
            [shape((4, TOKENS, 128)) if split else rows, shape((8, WIDTH), FLOAT)],
            [SMEM, VMEM, ANY if sliced else VMEM] + [VMEM] * 7 + [ANY],
            scratch, 48, 4 * 10**9, "project_back", [block] * 2,
        )(info, grad, stream, att, grad_q, grad_kv, grad_coarse, far_grad, ag, ab, wp)

    grad3, small_f1, keep_f1, send_f1 = feed_back(1, cotangent, mid1, hidden1, slope1)
    out_pieces = exchange_pieces([out_pieces[k] for k in range(4)])
    share_f1 = scatter_sum(keep_f1, send_f1)
    grad_q, grad_kv, grad_coarse, far_grad = attend_back(1, grad3, qkv1, coarse1, prob1)
    far_grad = over_section(far_grad, 1)
    grad2, small_a1, keep_a1, send_a1 = project_back(
        1, grad3, stream1, att1, grad_q, grad_kv, grad_coarse, far_grad)
    share_a1 = scatter_sum(keep_a1, send_a1)
    grad1, small_f0, keep_f0, send_f0 = feed_back(0, grad2, mid0, hidden0, slope0)
    share_f0 = scatter_sum(keep_f0, send_f0)
    grad_q, grad_kv, grad_coarse, far_grad = attend_back(0, grad1, qkv0, coarse0, prob0)
    far_grad = over_section(far_grad, 1)
    grad_pieces, small_a0, keep_a0, send_a0 = project_back(
        0, grad1, inputs, att0, grad_q, grad_kv, grad_coarse, far_grad)
    share_a0 = scatter_sum(keep_a0, send_a0)
    grad_pieces = exchange_pieces([grad_pieces[k] for k in range(4)])
    smalls = full_sum(jnp.concatenate([small_f1, small_a1, small_f0, small_a0], axis=0))

    outputs_shape = shape((2, 2 * TOKENS, 128))
    up_grad, down_grad, outputs = pl.pallas_call(
        functools.partial(finish_feed_kernel, 2, shards),
        out_shape=[shape((2, WIDTH // shards, FF), FLOAT), shape((2, FF // shards, WIDTH), FLOAT), outputs_shape],
        in_specs=[SMEM] + [VMEM] * 8 + [ANY] * 4,
        out_specs=[VMEM, VMEM, ANY],
        scratch_shapes=[pltpu.SemaphoreType.DMA((4,))],
        compiler_params=pltpu.CompilerParams(vmem_limit_bytes=16 * MIB),
        name="finish_feed",
    )(info, *over_all_sections(share_f0), *over_all_sections(share_f1), *out_pieces)
    vector = shape((2, WIDTH // shards), FLOAT)
    finished = pl.pallas_call(
        functools.partial(finish_attend_kernel, 2, shards),
        out_shape=[shape((2, WIDTH // shards, 3 * WIDTH), FLOAT), shape((2, WIDTH // shards, WIDTH), FLOAT),
                   vector, vector, vector, vector, vector, shape((2, FF // shards), FLOAT), vector, outputs_shape],
        in_specs=[SMEM] + [VMEM] * 8 + [ANY] * 4 + [VMEM],
        out_specs=[VMEM] * 9 + [ANY],
        scratch_shapes=[pltpu.SemaphoreType.DMA((4,))],
        compiler_params=pltpu.CompilerParams(vmem_limit_bytes=16 * MIB),
        name="finish_attend",
    )(info, *over_all_sections(share_a0), *over_all_sections(share_a1), *grad_pieces, smalls)
    proj_grad, back_grad, gain_a, bias_a, bias_o, gain_f, bias_f, bias_u, bias_d, input_grad = finished
    return (outputs, input_grad, gain_a, bias_a, proj_grad, back_grad, bias_o, gain_f, bias_f, up_grad, bias_u,
            down_grad, bias_d)


def solution(mesh):
    batch = P("dp", None, None)
    split = P("dp", None, "section")
    vector, matrix = P(None, "dp"), P(None, "dp", None)
    return jax.shard_map(
        local,
        mesh=mesh,
        in_specs=(batch, P("dp")) + (P(),) * 11 + (batch,),
        out_specs=(split, split, vector, vector, matrix, matrix, vector, vector, vector, matrix, vector, matrix, vector),
        check_vma=False,
    )
```

```python
import functools

import jax
import jax.numpy as jnp
from jax import lax
from jax.experimental import pallas as pl
from jax.experimental.pallas import tpu as pltpu
from jax.sharding import PartitionSpec as P

FLOAT = jnp.float32
BRAIN = jnp.bfloat16
NORM_EPS = 1e-05
MASK_FILL = -1000000000.0
WIDTH = 512
TOKENS = 512
FF = 2048
GROUP = 32
GROUPS = TOKENS // GROUP
LEVELS = 5
KEYS = GROUP + 16 * LEVELS
HALF = 256
QROWS = 4 * GROUP
TILE = 256
TILES = TOKENS // TILE
LEVEL_AT = (0, 128, 192, 224, 240)
USED = 248
MIB = 1024 * 1024

NN = (((1,), (0,)), ((), ()))
NT = (((1,), (1,)), ((), ()))
TN = (((0,), (0,)), ((), ()))


def dot(left, right, dims=NN):
    return lax.dot_general(left, right, dims, preferred_element_type=FLOAT)


def iota(shape, dim):
    return lax.broadcasted_iota(jnp.int32, shape, dim)


def normalise(rows):
    mean = jnp.mean(rows, axis=-1, keepdims=True)
    centred = rows - mean
    scale = lax.rsqrt(jnp.mean(centred * centred, axis=-1, keepdims=True) + NORM_EPS)
    return centred * scale, scale


def norm_into(source, gain, bias, target):
    for start in range(0, TOKENS, 64):
        rows = slice(start, start + 64)
        unit, _ = normalise(source[rows, :].astype(FLOAT))
        target[rows, :] = (unit * gain + bias).astype(BRAIN)


def norm_back(source, gain, grad_ref, through_ref, target, gain_out, bias_out):
    gain_sum = jnp.zeros((1, WIDTH), FLOAT)
    bias_sum = jnp.zeros((1, WIDTH), FLOAT)
    for start in range(0, TOKENS, 64):
        rows = slice(start, start + 64)
        unit, scale = normalise(source[rows, :].astype(FLOAT))
        grad = grad_ref[rows, :]
        gain_sum = gain_sum + jnp.sum(grad * unit, axis=0, keepdims=True)
        bias_sum = bias_sum + jnp.sum(grad, axis=0, keepdims=True)
        inner = grad * gain
        inner_mean = jnp.mean(inner, axis=-1, keepdims=True)
        slope = jnp.mean(inner * unit, axis=-1, keepdims=True)
        back = scale * (inner - inner_mean - unit * slope)
        target[rows, :] = (through_ref[rows, :].astype(FLOAT) + back).astype(BRAIN)
    gain_out[...] = gain_sum
    bias_out[...] = bias_sum


def span_of(row):
    level = 1 + sum((row >= at).astype(jnp.int32) for at in LEVEL_AT[1:])
    at = sum(jnp.where(level == k + 1, at, 0) for k, at in enumerate(LEVEL_AT))
    return level, (row - at) << level


def pool_matrix(tile, live, transposed):
    dims = (TILE, TILE)
    row, token = iota(dims, int(transposed)), iota(dims, 1 - int(transposed))
    level, first = span_of(row)
    inside = (token >= first) & (token < first + (1 << level)) & (token < live - tile * TILE) & (row < USED)
    return inside.astype(FLOAT).astype(BRAIN)


def counts(tile, live, columns):
    level, first = span_of(iota((TILE, columns), 0))
    return jnp.clip(live - tile * TILE - first, 0, 1 << level)


def far_counts(live, columns):
    return jnp.clip(live - (iota((16, columns), 0) << LEVELS), 0, 1 << LEVELS)


def inverse(number):
    return 1.0 / jnp.maximum(number, 1).astype(FLOAT)


def log_count(number):
    return jnp.where(number > 0, jnp.log(jnp.maximum(number, 1).astype(FLOAT)), MASK_FILL)


def project(normed, weight, target, start, stop, target_start=None):
    shift = 0 if target_start is None else target_start - start
    for column in range(start, stop, 256):
        target[:, column + shift : column + shift + 256] = dot(
            normed[...], weight[:, column : column + 256]
        ).astype(BRAIN)


def pool_keys(qkv, live, coarse, pooled):
    matrix = [pool_matrix(tile, live, False) for tile in range(TILES)]
    share = [inverse(counts(tile, live, TILE)) for tile in range(TILES)]
    for column in range(0, 2 * WIDTH, TILE):
        columns = slice(column, column + TILE)
        last = []
        for tile in range(TILES):
            rows = slice(tile * TILE, (tile + 1) * TILE)
            mean = dot(matrix[tile], qkv[rows, WIDTH + column : WIDTH + column + TILE]) * share[tile]
            coarse[rows, columns] = mean.astype(BRAIN)
            last.append(mean[LEVEL_AT[4] : USED])
        pooled[:, columns] = jnp.concatenate(last, axis=0).astype(BRAIN)


def pool_far(keyed, live, pooled):
    key, token = iota((16, TOKENS), 0), iota((16, TOKENS), 1)
    matrix = ((token >> LEVELS == key) & (token < live)).astype(FLOAT).astype(BRAIN)
    share = inverse(far_counts(live, TILE))
    for column in range(0, 2 * WIDTH, TILE):
        columns = slice(column, column + TILE)
        pooled[:, columns] = (dot(matrix, keyed[:, columns]) * share).astype(BRAIN)


def key_bias(live, other_live, bias):
    for tile in range(TILES):
        bias[tile * TILE : (tile + 1) * TILE, :] = log_count(counts(tile, live, 128))
    bias[TOKENS:, :] = log_count(far_counts(other_live, 128))


def head_mask(value):
    shape = (QROWS, HALF)
    return jnp.where(iota(shape, 0) // GROUP == iota(shape, 1) // 64, value, 0.0).astype(BRAIN)


def spread(rows, mask):
    return jnp.concatenate([rows] * 4, axis=0) * mask


def gather_heads(wide):
    left = iota((GROUP, 128), 1) < 64
    low = jnp.where(left, wide[0:32, 0:128], wide[32:64, 0:128])
    high = jnp.where(left, wide[64:96, 128:256], wide[96:128, 128:256])
    return jnp.concatenate([low, high], axis=1)


def group_rows(group):
    at = []
    for level in range(1, LEVELS):
        block = (group >> (level - 1)) ^ 1
        per_tile = TILE // (16 << level)
        at.append(block // per_tile * TILE + LEVEL_AT[level - 1] + block % per_tile * 16)
    return at


def key_block(qkv, coarse, far, group, part, half):
    column = WIDTH * (part + 1) + HALF * half
    columns = slice(WIDTH * part + HALF * half, WIDTH * part + HALF * (half + 1))
    pieces = [qkv[group * GROUP : (group + 1) * GROUP, column : column + HALF]]
    pieces += [coarse[at : at + 16, columns] for at in group_rows(group)]
    return jnp.concatenate(pieces + [far[:, columns]], axis=0)


def hier_forward(qkv, coarse, far, bias, prob, attended, live):
    mask = head_mask(0.125)
    for group in range(GROUPS):
        rows = slice(group * GROUP, (group + 1) * GROUP)
        near_bias = jnp.where(group * GROUP + iota((GROUP, 128), 0) < live, 0.0, MASK_FILL)
        added_bias = jnp.concatenate(
            [near_bias] + [bias[at : at + 16, :] for at in group_rows(group)] + [bias[TOKENS:, :]], axis=0
        )
        query_live = (group * GROUP + iota((GROUP, HALF), 0) < live).astype(FLOAT)
        for half in range(2):
            columns = slice(half * HALF, (half + 1) * HALF)
            queries = spread(qkv[rows, columns], mask)
            scores = dot(key_block(qkv, coarse, far, group, 0, half), queries, NT) + added_bias
            weights = jnp.exp(scores - jnp.max(scores, axis=0, keepdims=True))
            weights = weights * (1.0 / jnp.sum(weights, axis=0, keepdims=True))
            weights = weights.astype(BRAIN)
            prob[group, half, :, :] = weights
            output = dot(weights, key_block(qkv, coarse, far, group, 1, half), TN)
            attended[rows, columns] = (gather_heads(output) * query_live).astype(BRAIN)


def hier_backward(qkv, coarse, far, prob, grad_out, grad_q, grad_kv, grad_coarse, grad_far):
    mask_q, mask_o = head_mask(0.125), head_mask(1.0)
    for group in range(GROUPS):
        own = slice(group * GROUP, (group + 1) * GROUP)
        for half in range(2):
            columns = slice(half * HALF, (half + 1) * HALF)
            queries = spread(qkv[own, columns], mask_q)
            grads = spread(grad_out[own, columns], mask_o)
            keys = key_block(qkv, coarse, far, group, 0, half)
            values = key_block(qkv, coarse, far, group, 1, half)
            weights_low = prob[group, half, :, :]
            weights = weights_low.astype(FLOAT)
            product = weights * dot(values, grads, NT)
            score_grad = product - weights * jnp.sum(product, axis=0, keepdims=True)
            score_grad = score_grad.astype(BRAIN)
            grad_q[own, columns] = (gather_heads(dot(score_grad, keys, TN)) * 0.125).astype(BRAIN)
            for part, block in enumerate((dot(score_grad, queries), dot(weights_low, grads))):
                to = slice(part * WIDTH + half * HALF, part * WIDTH + (half + 1) * HALF)
                grad_kv[own, to] = block[0:GROUP]
                for level, at in enumerate(group_rows(group)):
                    piece = block[GROUP + 16 * level : GROUP + 16 * level + 16]
                    if group % (1 << level) == 0:
                        grad_coarse[at : at + 16, to] = piece
                    else:
                        grad_coarse[at : at + 16, to] += piece
                if group == 0:
                    grad_far[:, to] = block[KEYS - 16 :]
                else:
                    grad_far[:, to] += block[KEYS - 16 :]


def add_projected(stream, source, weight, bias, target):
    for column in range(0, WIDTH, 256):
        columns = slice(column, column + 256)
        total = dot(source[...], weight[:, columns])
        target[:, columns] = (stream[:, columns].astype(FLOAT) + total + bias[:, columns]).astype(
            BRAIN
        )


def feed_hidden(normed, weight, bias, hidden, slope):
    for column in range(0, FF, 256):
        columns = slice(column, column + 256)
        pre = dot(normed[...], weight[:, columns]) + bias[:, columns]
        square = pre * pre
        bent = jnp.tanh(0.7978845608 * pre * (1.0 + 0.044715 * square))
        half = 0.5 * (1.0 + bent)
        hidden[:, columns] = (pre * half).astype(BRAIN)
        inner = 0.7978845608 + (3 * 0.044715 * 0.7978845608) * square
        slope[:, columns] = (half + 0.5 * pre * (1.0 - bent * bent) * inner).astype(BRAIN)


def projected_grad(qkv_grad, grad_kv, grad_coarse, grad_far, live):
    for tile in range(TILES):
        rows = slice(tile * TILE, (tile + 1) * TILE)
        matrix = pool_matrix(tile, live, True)
        share = inverse(counts(tile, live, TILE))
        for column in range(0, 2 * WIDTH, TILE):
            columns = slice(column, column + TILE)
            spans = jnp.concatenate(
                [grad_coarse[tile * TILE : tile * TILE + LEVEL_AT[4], columns],
                 grad_far[8 * tile : 8 * tile + 8, columns], jnp.zeros((8, TILE), FLOAT)], axis=0)
            total = grad_kv[rows, columns] + dot(matrix, (spans * share).astype(BRAIN))
            qkv_grad[rows, WIDTH + column : WIDTH + column + TILE] = total.astype(BRAIN)


def fetch(source, target, sem):
    copy = pltpu.make_async_copy(source, target, sem)
    copy.start()
    return copy


def reversed_bits(value, bits):
    return sum(((value >> k) & 1) << (bits - 1 - k) for k in range(bits))


def block_index(info, owner_core, rel_x, shard, bits):
    rest = reversed_bits(shard, bits) ^ info[6]
    return jnp.where(owner_core == 0, (rel_x << bits) | rest, (rest << 1) | rel_x)


def pair_columns(ref, section, rel_core, width):
    both = []
    for rel_x in range(2):
        quarter = section ^ (2 * rel_x + rel_core)
        both.append(ref[:, pl.ds(pl.multiple_of(quarter * width, 128), width)])
    return jnp.concatenate(both, axis=1)


def feed_weight_grads(info, rel_core, normed, pre_grad, hidden, grad, blocks, shards):
    bits = shards.bit_length() - 1
    section = info[4]
    owner = (section & 1) ^ rel_core
    rows = WIDTH // shards
    wide = FF // shards
    where = [[block_index(info, owner, rel_x, shard, bits) for shard in range(shards)] for rel_x in range(2)]
    for rel_x in range(2):
        quarter = section ^ (2 * rel_x + rel_core)
        for part in range(2):
            at = pl.multiple_of(quarter * 512 + 256 * part, 256)
            block = dot(normed[...], pre_grad[:, pl.ds(at, 256)], TN).astype(BRAIN)
            for shard in range(shards):
                blocks[where[rel_x][shard], 0:rows, 256 * part : 256 * part + 256] = block[shard * rows : (shard + 1) * rows]
    some_grad = pair_columns(grad, section, rel_core, 128)
    for start in range(0, FF, 256):
        block = dot(hidden[:, start : start + 256], some_grad, TN).astype(BRAIN)
        for at in range(0, 256, rows):
            shard, part = (start + at) // wide, (start + at) % wide // rows
            for rel_x in range(2):
                blocks[where[rel_x][shard], rows:, 128 * part : 128 * part + 128] = block[
                    at : at + rows, 128 * rel_x : 128 * rel_x + 128]


def attend_weight_grads(info, rel_core, normed, qkv_grad, att, grad, blocks, shards):
    bits = shards.bit_length() - 1
    section = info[4]
    owner = (section & 1) ^ rel_core
    rows = WIDTH // shards
    left = dot(normed[...], pair_columns(qkv_grad, section, rel_core, 384), TN).astype(BRAIN)
    right = dot(att[...], pair_columns(grad, section, rel_core, 128), TN).astype(BRAIN)
    for rel_x in range(2):
        for shard in range(shards):
            where = block_index(info, owner, rel_x, shard, bits)
            mine = slice(shard * rows, (shard + 1) * rows)
            blocks[where, :, 0:384] = left[mine, 384 * rel_x : 384 * rel_x + 384]
            blocks[where, :, 384:512] = right[mine, 128 * rel_x : 128 * rel_x + 128]


ANY = pl.BlockSpec(memory_space=pl.ANY)
VMEM = pl.BlockSpec(memory_space=pltpu.VMEM)
SMEM = pl.BlockSpec(memory_space=pltpu.SMEM)


def shape(dims, dtype=BRAIN):
    return jax.ShapeDtypeStruct(dims, dtype)


def call(body, outs, args, scratch, flops, name, limit=16, after=()):
    count = len(args)

    def kernel(*refs):
        body(*refs[:count], *refs[count + len(after):])

    return pl.pallas_call(
        kernel,
        out_shape=outs,
        in_specs=[spec for spec, _ in args] + [ANY] * len(after),
        out_specs=[VMEM] * len(outs),
        scratch_shapes=scratch,
        compiler_params=pltpu.CompilerParams(vmem_limit_bytes=limit * MIB),
        cost_estimate=pl.CostEstimate(flops=flops, bytes_accessed=MIB, transcendentals=0),
        name=name,
    )(*[array for _, array in args], *after)


def first_kernel(info, inputs, hag, hab, hob, hfg, hfb, hub, hdb, hwp, hwo, hwu, hwd,
                 ag, ab, ob, fg, fb, ub, db, wp, wo, wu, wd,
                 qkv, coarse, far, prob, att, mine, mid, hidden, slope, out, qkv_next, coarse_next, pooled,
                 other, normed, keyed, bias, sems):
    seq, half, live, other_live = info[0], info[1], info[2], info[3]
    get_mine = fetch(inputs.at[seq, pl.ds(half * TOKENS, TOKENS)], mine, sems.at[0])
    small = [fetch(source, target, sems.at[2 + k]) for k, (source, target) in enumerate(
        ((hag, ag), (hab, ab), (hob, ob), (hfg, fg), (hfb, fb), (hub, ub), (hdb, db)))]
    get_wp = fetch(hwp.at[0], wp.at[0], sems.at[9])
    get_other = fetch(inputs.at[seq, pl.ds((1 - half) * TOKENS, TOKENS)], other, sems.at[1])
    large = [fetch(source.at[0], target.at[0], sems.at[10 + k]) for k, (source, target) in enumerate(
        ((hwo, wo), (hwu, wu), (hwd, wd)))]
    later = [fetch(source.at[1], target.at[1], sems.at[13 + k]) for k, (source, target) in enumerate(
        ((hwp, wp), (hwo, wo), (hwu, wu), (hwd, wd)))]
    key_bias(live, other_live, bias)
    for copy in small:
        copy.wait()
    get_mine.wait()
    norm_into(mine, ag[0:1, :], ab[0:1, :], normed)
    get_wp.wait()
    project(normed, wp.at[0], qkv, 0, 3 * WIDTH)
    get_other.wait()
    norm_into(other, ag[0:1, :], ab[0:1, :], normed)
    project(normed, wp.at[0], keyed, WIDTH, 3 * WIDTH, 0)
    pool_far(keyed, other_live, far)
    pool_keys(qkv, live, coarse, pooled)
    hier_forward(qkv, coarse, far, bias, prob, att, live)
    large[0].wait()
    add_projected(mine, att, wo.at[0], ob[0:1, :], mid)
    norm_into(mid, fg[0:1, :], fb[0:1, :], normed)
    large[1].wait()
    feed_hidden(normed, wu.at[0], ub[0:1, :], hidden, slope)
    large[2].wait()
    add_projected(mid, hidden, wd.at[0], db[0:1, :], out)
    norm_into(out, ag[1:2, :], ab[1:2, :], normed)
    later[0].wait()
    project(normed, wp.at[1], qkv_next, 0, 3 * WIDTH)
    pool_keys(qkv_next, live, coarse_next, pooled)
    for copy in later[1:]:
        copy.wait()


def second_kernel(info, qkv, coarse, far, stream, ob, fg, fb, ub, wo, wu,
                  prob, att, mid, normed, hidden, slope, bias):
    live, other_live = info[2], info[3]
    key_bias(live, other_live, bias)
    hier_forward(qkv, coarse, far, bias, prob, att, live)
    add_projected(stream, att, wo.at[1], ob[1:2, :], mid)
    norm_into(mid, fg[1:2, :], fb[1:2, :], normed)
    feed_hidden(normed, wu.at[1], ub[1:2, :], hidden, slope)


def feed_back_send(layer, shards, take_grad, take_norm, info, *refs):
    refs = list(refs)
    source = refs.pop(0)
    hidden, slope, wd = refs[:3]
    del refs[:3]
    if take_norm:
        stream, gain, shift = refs[:3]
        del refs[:3]
    else:
        normed = refs.pop(0)
    pre_grad, sums, send = refs[:3]
    del refs[:3]
    if take_grad:
        grad = refs.pop(0)
    if take_norm:
        normed = refs.pop(0)
    if take_grad:
        copy = fetch(source.at[info[0], pl.ds(info[1] * TOKENS, TOKENS)], grad, refs[0].at[0])
        copy.wait()
    else:
        grad = source
    if take_norm:
        norm_into(stream, gain[layer : layer + 1, :], shift[layer : layer + 1, :], normed)
    for column in range(0, FF, 256):
        columns = slice(column, column + 256)
        back = dot(grad[...], wd[layer, columns, :], NT) * slope[:, columns].astype(FLOAT)
        back = back.astype(BRAIN)
        pre_grad[:, columns] = back
        sums[3 + column // 512 : 4 + column // 512, column % 512 : column % 512 + 256] = jnp.sum(
            back.astype(FLOAT), axis=0, keepdims=True
        )
    feed_weight_grads(info, 1, normed, pre_grad, hidden, grad, send, shards)
    sums[0:2, :] = jnp.zeros((2, WIDTH), FLOAT)
    sums[2:3, :] = jnp.sum(grad[...].astype(FLOAT), axis=0, keepdims=True)
    sums[7:8, :] = jnp.zeros((1, WIDTH), FLOAT)


def feed_back_keep(layer, shards, info, grad, normed, pre_grad, hidden, stream, gain, wu, sums_in,
                   target, sums, keep, norm_grad):
    feed_weight_grads(info, 0, normed, pre_grad, hidden, grad, keep, shards)
    for column in range(0, WIDTH, 256):
        norm_grad[:, column : column + 256] = dot(pre_grad[...], wu[layer, column : column + 256, :], NT)
    sums[...] = sums_in[...]
    norm_back(stream, gain[layer : layer + 1, :], norm_grad, grad, target, sums.at[0:1, :], sums.at[1:2, :])


def attend_back(layer, finish, info, grad, qkv, coarse, far, prob, wo, *refs):
    live, section = info[2], info[4]
    refs = list(refs)
    if finish:
        mid, hidden, wd, db = refs[:4]
        del refs[:4]
    grad_q, grad_kv, grad_coarse, grad_far = refs[:4]
    del refs[:4]
    if finish:
        out = refs.pop(0)
        for column in range(0, WIDTH, 256):
            total = dot(hidden[...], wd[layer, :, column : column + 256])
            for k in range(2):
                columns = slice(column + 128 * k, column + 128 * k + 128)
                final = mid[:, columns].astype(FLOAT) + total[:, 128 * k : 128 * k + 128] + db[layer : layer + 1, columns]
                out[(column // 128 + k) ^ section, :, :] = final.astype(BRAIN)
    grad_out = refs.pop(0)
    for column in range(0, WIDTH, 256):
        back = dot(grad[...], wo[layer, column : column + 256, :], NT)
        back = back * (iota((TOKENS, 256), 0) < live).astype(FLOAT)
        grad_out[:, column : column + 256] = back.astype(BRAIN)
    hier_backward(qkv, coarse, far, prob, grad_out, grad_q, grad_kv, grad_coarse, grad_far)


def project_back_send(layer, shards, info, grad, stream, att, grad_q, grad_kv, grad_coarse, grad_far, gain, shift,
                      qkv_grad, normed, send):
    norm_into(stream, gain[layer : layer + 1, :], shift[layer : layer + 1, :], normed)
    qkv_grad[:, 0:WIDTH] = grad_q[...]
    projected_grad(qkv_grad, grad_kv, grad_coarse, grad_far, info[2])
    attend_weight_grads(info, 1, normed, qkv_grad, att, grad, send, shards)


def project_back_keep(layer, shards, split, info, grad, stream, att, normed, qkv_grad, gain, wp,
                      target, sums, keep, norm_grad, *more):
    section = info[4]
    attend_weight_grads(info, 0, normed, qkv_grad, att, grad, keep, shards)
    for column in range(0, WIDTH, 256):
        norm_grad[:, column : column + 256] = dot(qkv_grad[...], wp[layer, column : column + 256, :], NT)
    result = more[0] if split else target
    norm_back(stream, gain[layer : layer + 1, :], norm_grad, grad, result, sums.at[0:1, :], sums.at[1:2, :])
    if split:
        for quarter in range(4):
            target[quarter ^ section, :, :] = result[:, quarter * 128 : quarter * 128 + 128]
    sums[2:3, :] = jnp.sum(grad[...].astype(FLOAT), axis=0, keepdims=True)
    sums[3:8, :] = jnp.zeros((5, WIDTH), FLOAT)


def finish_feed_kernel(layers, shards, info, *refs):
    section = info[4]
    pieces, rest = refs[: 4 * layers], refs[4 * layers :]
    outs, rest = rest[:4], rest[4:]
    up, down, output, sems = rest
    copies = []
    for k in range(4):
        owner = section ^ k
        copies.append(
            fetch(outs[k], output.at[owner >> 1, pl.ds((owner & 1) * TOKENS, TOKENS)], sems.at[k])
        )
    rows = WIDTH // shards
    for layer in range(layers):
        for k in range(4):
            piece = pieces[layer * 4 + k]
            owner = section ^ k
            up[layer, :, pl.ds(pl.multiple_of(owner * 512, 512), 512)] = piece[0:rows, :].astype(FLOAT)
            for part in range(FF // WIDTH):
                down[layer, part * rows : (part + 1) * rows, pl.ds(pl.multiple_of(owner * 128, 128), 128)] = piece[
                    rows:, 128 * part : 128 * part + 128].astype(FLOAT)
    for copy in copies:
        copy.wait()


def finish_attend_kernel(layers, shards, info, *refs):
    section, dp = info[4], info[5]
    pieces, rest = refs[: 4 * layers], refs[4 * layers :]
    grads, rest = rest[:4], rest[4:]
    smalls, proj, back, gain_a, bias_a, bias_o, gain_f, bias_f, bias_u, bias_d, input_grad, sems = rest
    copies = []
    for k in range(4):
        owner = section ^ k
        copies.append(
            fetch(grads[k], input_grad.at[owner >> 1, pl.ds((owner & 1) * TOKENS, TOKENS)], sems.at[k])
        )
    for layer in range(layers):
        for k in range(4):
            piece = pieces[layer * 4 + k]
            owner = section ^ k
            proj[layer, :, pl.ds(pl.multiple_of(owner * 384, 128), 384)] = piece[:, 0:384].astype(FLOAT)
            back[layer, :, pl.ds(pl.multiple_of(owner * 128, 128), 128)] = piece[:, 384:].astype(FLOAT)
    width = WIDTH // shards
    pick = (iota((WIDTH, width), 0) == dp * width + iota((WIDTH, width), 1)).astype(FLOAT)
    taken = lax.dot_general(smalls[...], pick, NN, precision=lax.Precision.HIGHEST, preferred_element_type=FLOAT)
    for layer in range(2):
        feed, attend = (16, 24) if layer == 0 else (0, 8)
        gain_f[layer : layer + 1, :] = taken[feed : feed + 1]
        bias_f[layer : layer + 1, :] = taken[feed + 1 : feed + 2]
        bias_d[layer : layer + 1, :] = taken[feed + 2 : feed + 3]
        gain_a[layer : layer + 1, :] = taken[attend : attend + 1]
        bias_a[layer : layer + 1, :] = taken[attend + 1 : attend + 2]
        bias_o[layer : layer + 1, :] = taken[attend + 2 : attend + 3]
    wide = FF // shards
    per_row = WIDTH // wide if wide <= WIDTH else 1
    place_in_row = dp % per_row
    pick = (iota((WIDTH, wide), 0) == place_in_row * wide + iota((WIDTH, wide), 1)).astype(FLOAT)
    taken = lax.dot_general(smalls[...], pick, NN, precision=lax.Precision.HIGHEST, preferred_element_type=FLOAT)
    for layer in range(2):
        feed = 16 if layer == 0 else 0
        row = jnp.zeros((1, wide), FLOAT)
        for k in range(4):
            row = jnp.where(dp // per_row == k, taken[feed + 3 + k : feed + 4 + k], row)
        bias_u[layer : layer + 1, :] = row
    for copy in copies:
        copy.wait()


def swap(block, partner):
    sections = lax.axis_size("section")
    pairs = []
    for dp in range(lax.axis_size("dp")):
        for section in range(sections):
            to_dp, to_section = partner(dp, section)
            pairs.append((dp * sections + section, to_dp * sections + to_section))
    return lax.ppermute(block, ("dp", "section"), pairs)


def over_section(block, bits):
    return swap(block, lambda dp, section: (dp, section ^ bits))


def added(*blocks):
    total = blocks[0].astype(FLOAT)
    for block in blocks[1:]:
        total = total + block.astype(FLOAT)
    return total.astype(blocks[0].dtype)


class Reduction:
    def __init__(self, send):
        self.bits = lax.axis_size("dp").bit_length() - 1
        self.came = over_section(send, 1)
        self.done = 0

    def partner(self, dp, section):
        step, core = self.done, section & 1
        over_x = step == 0 if core == 0 else step == self.bits
        if over_x:
            return dp, section ^ 2
        return dp ^ (1 << (step - 1 + core)), section

    def keep(self, blocks):
        self.mine = blocks

    def step(self):
        if self.done > self.bits:
            if self.came is not None:
                self.mine, self.came = added(self.mine, self.came), None
            return self.mine
        count = self.mine.shape[0] // 2
        give = added(self.mine[count:], self.came[count:])
        self.mine = added(self.mine[:count], self.came[:count])
        self.came = swap(give, self.partner)
        self.done += 1
        return give

    def finish(self):
        while self.done <= self.bits:
            self.step()
        self.step()
        return self.mine[0]


def full_sum(block):
    block = block + over_section(block, 1)
    ways = [lambda dp, section: (dp, section ^ 2), lambda dp, section: (dp ^ 1, section),
            lambda dp, section: (dp ^ 1, section ^ 2)]
    block = added(block, *[swap(block, way) for way in ways])
    bit, left = 2, lax.axis_size("dp") // 2
    while left > 1:
        count = min(4, left)
        block = added(block, *[
            swap(block, lambda dp, section, k=k, bit=bit: (dp ^ (k * bit), section)) for k in range(1, count)
        ])
        left //= count
        bit *= count
    return block


def over_all_sections(block):
    return [block] + [over_section(block, k) for k in range(1, 4)]


def exchange_pieces(pieces):
    return [pieces[0]] + [over_section(pieces[k], k) for k in range(1, 4)]


def vmem(dims, dtype=BRAIN):
    return pltpu.VMEM(dims, dtype)


def in_hbm(array):
    return (ANY, pltpu.with_memory_space_constraint(array, pltpu.HBM))


def local(inputs, lengths, ag, ab, wp, wo, ob, fg, fb, wu, ub, wd, db, cotangent):
    shards = lax.axis_size("dp")
    bits = shards.bit_length() - 1
    section, dp = lax.axis_index("section"), lax.axis_index("dp")
    seq, half = section // 2, section % 2
    length = jnp.where(seq == 0, lengths[0], lengths[1])
    live = jnp.clip(length - half * TOKENS, 0, TOKENS)
    other_live = jnp.clip(length - (1 - half) * TOKENS, 0, TOKENS)
    info = jnp.stack([seq, half, live, other_live, section, dp, reversed_bits(dp, bits)]).astype(jnp.int32)
    here = (SMEM, info)

    def there(*arrays):
        return [(VMEM, array) for array in arrays]

    rows, wide, tall = vmem((TOKENS, WIDTH)), vmem((TOKENS, FF)), vmem((TOKENS, 3 * WIDTH))
    rows_float = vmem((TOKENS, WIDTH), FLOAT)
    coarse_shape, far_shape = vmem((TOKENS, 2 * WIDTH)), vmem((16, 2 * WIDTH))
    prob_shape = vmem((GROUPS, 2, KEYS, QROWS))
    bias_shape = vmem((TOKENS + 16, 128), FLOAT)
    sums_shape = vmem((8, WIDTH), FLOAT)
    params = (ag, ab, ob, fg, fb, ub, db, wp, wo, wu, wd)
    (ag, ab, ob, fg, fb, ub, db, wp, wo, wu, wd,
     qkv0, coarse0, far0, prob0, att0, stream0, mid0, hidden0, slope0, stream1, qkv1, coarse1, pooled) = call(
        first_kernel,
        [vmem(array.shape, array.dtype) for array in params]
        + [tall, coarse_shape, far_shape, prob_shape, rows, rows, rows, wide, wide, rows, tall, coarse_shape, far_shape],
        [here, in_hbm(inputs)] + [in_hbm(array) for array in params],
        [rows, rows, vmem((TOKENS, 2 * WIDTH)), bias_shape, pltpu.SemaphoreType.DMA((17,))],
        12 * 10**9, "layer_zero_forward",
    )
    far1 = over_section(pooled, 1)
    prob1, att1, mid1, normed1, hidden1, slope1 = call(
        second_kernel, [prob_shape, rows, rows, rows, wide, wide],
        [here] + there(qkv1, coarse1, far1, stream1, ob, fg, fb, ub, wo, wu), [bias_shape],
        6 * 10**9, "layer_one_forward",
    )

    feed_blocks = vmem((2 * shards, WIDTH // shards + FF // shards // 4, WIDTH))
    attend_blocks = vmem((2 * shards, WIDTH // shards, WIDTH))
    sem = pltpu.SemaphoreType.DMA((1,))

    pre_grad, sums_f1, send_f1, grad_last = call(
        functools.partial(feed_back_send, 1, shards, True, False), [wide, sums_shape, feed_blocks, rows],
        [here, in_hbm(cotangent)] + there(hidden1, slope1, wd, normed1), [sem], 3 * 10**9, "feed_back_send_1",
    )
    red_f1 = Reduction(send_f1)
    grad3, sums_f1, keep_f1 = call(
        functools.partial(feed_back_keep, 1, shards), [rows, sums_shape, feed_blocks],
        [here] + there(grad_last, normed1, pre_grad, hidden1, mid1, fg, wu, sums_f1), [rows_float],
        3 * 10**9, "feed_back_keep_1",
    )
    red_f1.keep(keep_f1)
    ready = [red_f1.step()]
    grad_q, grad_kv, grad_coarse, grad_far, out_pieces = call(
        functools.partial(attend_back, 1, True),
        [rows, vmem((TOKENS, 2 * WIDTH), FLOAT), vmem((TOKENS, 2 * WIDTH), FLOAT), vmem((16, 2 * WIDTH), FLOAT),
         vmem((4, TOKENS, 128))],
        [here] + there(grad3, qkv1, coarse1, far1, prob1, wo, mid1, hidden1, wd, db), [rows],
        8 * 10**9, "attend_back_1", after=ready,
    )
    grad_far = over_section(grad_far, 1)
    ready = [red_f1.step()]
    qkv_grad, normed, send_a1 = call(
        functools.partial(project_back_send, 1, shards), [tall, rows, attend_blocks],
        [here] + there(grad3, stream1, att1, grad_q, grad_kv, grad_coarse, grad_far, ag, ab), [],
        3 * 10**9, "project_back_send_1", after=ready,
    )
    red_a1 = Reduction(send_a1)
    grad2, sums_a1, keep_a1 = call(
        functools.partial(project_back_keep, 1, shards, False), [rows, sums_shape, attend_blocks],
        [here] + there(grad3, stream1, att1, normed, qkv_grad, ag, wp), [rows_float],
        3 * 10**9, "project_back_keep_1",
    )
    red_a1.keep(keep_a1)
    ready = [red_f1.step(), red_a1.step()]
    pre_grad, sums_f0, send_f0, normed = call(
        functools.partial(feed_back_send, 0, shards, False, True), [wide, sums_shape, feed_blocks, rows],
        [here] + there(grad2, hidden0, slope0, wd, mid0, fg, fb), [], 3 * 10**9, "feed_back_send_0", after=ready,
    )
    red_f0 = Reduction(send_f0)
    grad1, sums_f0, keep_f0 = call(
        functools.partial(feed_back_keep, 0, shards), [rows, sums_shape, feed_blocks],
        [here] + there(grad2, normed, pre_grad, hidden0, mid0, fg, wu, sums_f0), [rows_float],
        3 * 10**9, "feed_back_keep_0",
    )
    red_f0.keep(keep_f0)
    ready = [red_f0.step(), red_f1.step(), red_a1.step()]
    grad_q, grad_kv, grad_coarse, grad_far = call(
        functools.partial(attend_back, 0, False),
        [rows, vmem((TOKENS, 2 * WIDTH), FLOAT), vmem((TOKENS, 2 * WIDTH), FLOAT), vmem((16, 2 * WIDTH), FLOAT)],
        [here] + there(grad1, qkv0, coarse0, far0, prob0, wo), [rows],
        8 * 10**9, "attend_back_0", after=ready,
    )
    grad_far = over_section(grad_far, 1)
    ready = [red_f1.step(), red_a1.step()]
    qkv_grad, normed, send_a0 = call(
        functools.partial(project_back_send, 0, shards), [tall, rows, attend_blocks],
        [here] + there(grad1, stream0, att0, grad_q, grad_kv, grad_coarse, grad_far, ag, ab), [],
        3 * 10**9, "project_back_send_0", after=ready,
    )
    red_a0 = Reduction(send_a0)
    ready = [red_f0.step(), red_a1.step()]
    grad_pieces, sums_a0, keep_a0 = call(
        functools.partial(project_back_keep, 0, shards, True), [vmem((4, TOKENS, 128)), sums_shape, attend_blocks],
        [here] + there(grad1, stream0, att0, normed, qkv_grad, ag, wp), [rows_float, rows],
        3 * 10**9, "project_back_keep_0", after=ready,
    )
    red_a0.keep(keep_a0)
    red_a0.step()
    grad_pieces = exchange_pieces([grad_pieces[k] for k in range(4)])
    out_pieces = exchange_pieces([out_pieces[k] for k in range(4)])
    smalls = full_sum(jnp.concatenate([sums_f1, sums_a1, sums_f0, sums_a0], axis=0))
    share_f1, share_a1 = red_f1.finish(), red_a1.finish()
    share_f0, share_a0 = red_f0.finish(), red_a0.finish()

    outputs_shape = shape((2, 2 * TOKENS, 128))
    up_grad, down_grad, outputs = pl.pallas_call(
        functools.partial(finish_feed_kernel, 2, shards),
        out_shape=[shape((2, WIDTH // shards, FF), FLOAT), shape((2, FF // shards, WIDTH), FLOAT), outputs_shape],
        in_specs=[SMEM] + [VMEM] * 8 + [ANY] * 4,
        out_specs=[VMEM, VMEM, ANY],
        scratch_shapes=[pltpu.SemaphoreType.DMA((4,))],
        compiler_params=pltpu.CompilerParams(vmem_limit_bytes=16 * MIB),
        name="finish_feed",
    )(info, *over_all_sections(share_f0), *over_all_sections(share_f1), *out_pieces)
    vector = shape((2, WIDTH // shards), FLOAT)
    finished = pl.pallas_call(
        functools.partial(finish_attend_kernel, 2, shards),
        out_shape=[shape((2, WIDTH // shards, 3 * WIDTH), FLOAT), shape((2, WIDTH // shards, WIDTH), FLOAT),
                   vector, vector, vector, vector, vector, shape((2, FF // shards), FLOAT), vector, outputs_shape],
        in_specs=[SMEM] + [VMEM] * 8 + [ANY] * 4 + [VMEM],
        out_specs=[VMEM] * 9 + [ANY],
        scratch_shapes=[pltpu.SemaphoreType.DMA((4,))],
        compiler_params=pltpu.CompilerParams(vmem_limit_bytes=16 * MIB),
        name="finish_attend",
    )(info, *over_all_sections(share_a0), *over_all_sections(share_a1), *grad_pieces, smalls)
    proj_grad, back_grad, gain_a, bias_a, bias_o, gain_f, bias_f, bias_u, bias_d, input_grad = finished
    return (outputs, input_grad, gain_a, bias_a, proj_grad, back_grad, bias_o, gain_f, bias_f, up_grad, bias_u,
            down_grad, bias_d)


def solution(mesh):
    batch = P("dp", None, None)
    split = P("dp", None, "section")
    vector, matrix = P(None, "dp"), P(None, "dp", None)
    return jax.shard_map(
        local,
        mesh=mesh,
        in_specs=(batch, P("dp")) + (P(),) * 11 + (batch,),
        out_specs=(split, split, vector, vector, matrix, matrix, vector, vector, vector, matrix, vector, matrix, vector),
        check_vma=False,
    )
```

```python
import functools

import jax
import jax.numpy as jnp
from jax import lax
from jax.experimental import pallas as pl
from jax.experimental.pallas import tpu as pltpu
from jax.sharding import PartitionSpec as P

FLOAT = jnp.float32
BRAIN = jnp.bfloat16
NORM_EPS = 1e-05
MASK_FILL = -1000000000.0
WIDTH = 512
TOKENS = 512
FF = 2048
GROUP = 64
GROUPS = TOKENS // GROUP
LEVELS = 5
KEYS = GROUP + 32 + 16 * (LEVELS - 1)
HALF = 256
QROWS = 4 * GROUP
TILE = 256
TILES = TOKENS // TILE
LEVEL_AT = (0, 128, 192, 224, 240)
USED = 248
MIB = 1024 * 1024
COST = 1 * 10**9

NN = (((1,), (0,)), ((), ()))
NT = (((1,), (1,)), ((), ()))
TN = (((0,), (0,)), ((), ()))


def dot(left, right, dims=NN):
    return lax.dot_general(left, right, dims, preferred_element_type=FLOAT)


def iota(shape, dim):
    return lax.broadcasted_iota(jnp.int32, shape, dim)


def normalise(rows):
    mean = jnp.mean(rows, axis=-1, keepdims=True)
    centred = rows - mean
    scale = lax.rsqrt(jnp.mean(centred * centred, axis=-1, keepdims=True) + NORM_EPS)
    return centred * scale, scale


def norm_into(source, gain, bias, target):
    for start in range(0, TOKENS, 64):
        rows = slice(start, start + 64)
        unit, _ = normalise(source[rows, :].astype(FLOAT))
        target[rows, :] = (unit * gain + bias).astype(BRAIN)


def norm_back(source, gain, grad_ref, through_ref, target, gain_out, bias_out):
    gain_sum = jnp.zeros((1, WIDTH), FLOAT)
    bias_sum = jnp.zeros((1, WIDTH), FLOAT)
    for start in range(0, TOKENS, 64):
        rows = slice(start, start + 64)
        unit, scale = normalise(source[rows, :].astype(FLOAT))
        grad = grad_ref[rows, :]
        gain_sum = gain_sum + jnp.sum(grad * unit, axis=0, keepdims=True)
        bias_sum = bias_sum + jnp.sum(grad, axis=0, keepdims=True)
        inner = grad * gain
        inner_mean = jnp.mean(inner, axis=-1, keepdims=True)
        slope = jnp.mean(inner * unit, axis=-1, keepdims=True)
        back = scale * (inner - inner_mean - unit * slope)
        target[rows, :] = (through_ref[rows, :].astype(FLOAT) + back).astype(BRAIN)
    gain_out[...] = gain_sum
    bias_out[...] = bias_sum


def span_of(row):
    level = 1 + sum((row >= at).astype(jnp.int32) for at in LEVEL_AT[1:])
    at = sum(jnp.where(level == k + 1, at, 0) for k, at in enumerate(LEVEL_AT))
    return level, (row - at) << level


def pool_matrix(tile, live, transposed):
    dims = (TILE, TILE)
    row, token = iota(dims, int(transposed)), iota(dims, 1 - int(transposed))
    level, first = span_of(row)
    inside = (token >= first) & (token < first + (1 << level)) & (token < live - tile * TILE) & (row < USED)
    return inside.astype(FLOAT).astype(BRAIN)


def counts(tile, live, columns):
    level, first = span_of(iota((TILE, columns), 0))
    return jnp.clip(live - tile * TILE - first, 0, 1 << level)


def far_counts(live, columns):
    return jnp.clip(live - (iota((16, columns), 0) << LEVELS), 0, 1 << LEVELS)


def inverse(number):
    return 1.0 / jnp.maximum(number, 1).astype(FLOAT)


def log_count(number):
    return jnp.where(number > 0, jnp.log(jnp.maximum(number, 1).astype(FLOAT)), MASK_FILL)


def project(normed, weight, target, start, stop, target_start=None):
    shift = 0 if target_start is None else target_start - start
    for column in range(start, stop, 256):
        target[:, column + shift : column + shift + 256] = dot(
            normed[...], weight[:, column : column + 256]
        ).astype(BRAIN)


def pool_keys(qkv, live, coarse, pooled):
    matrix = [pool_matrix(tile, live, False) for tile in range(TILES)]
    share = [inverse(counts(tile, live, TILE)) for tile in range(TILES)]
    for column in range(0, 2 * WIDTH, TILE):
        columns = slice(column, column + TILE)
        last = []
        for tile in range(TILES):
            rows = slice(tile * TILE, (tile + 1) * TILE)
            mean = dot(matrix[tile], qkv[rows, WIDTH + column : WIDTH + column + TILE]) * share[tile]
            coarse[rows, columns] = mean.astype(BRAIN)
            last.append(mean[LEVEL_AT[4] : USED])
        pooled[:, columns] = jnp.concatenate(last, axis=0).astype(BRAIN)


def pool_far(keyed, live, pooled):
    key, token = iota((16, TOKENS), 0), iota((16, TOKENS), 1)
    matrix = ((token >> LEVELS == key) & (token < live)).astype(FLOAT).astype(BRAIN)
    share = inverse(far_counts(live, TILE))
    for column in range(0, 2 * WIDTH, TILE):
        columns = slice(column, column + TILE)
        pooled[:, columns] = (dot(matrix, keyed[:, columns]) * share).astype(BRAIN)


def key_bias(live, other_live, bias):
    for tile in range(TILES):
        bias[tile * TILE : (tile + 1) * TILE, :] = log_count(counts(tile, live, 128))
    bias[TOKENS:, :] = log_count(far_counts(other_live, 128))


def head_mask(value):
    dims = (QROWS, HALF)
    return jnp.where(iota(dims, 0) // GROUP == iota(dims, 1) // 64, value, 0.0).astype(BRAIN)


def pair_mask():
    own_key, own_query = iota((GROUP, QROWS), 0) // 32, iota((GROUP, QROWS), 1) % GROUP // 32
    near_key, near_query = iota((32, QROWS), 0) // 16, iota((32, QROWS), 1) % GROUP // 32
    own = jnp.where(own_key == own_query, 0.0, MASK_FILL)
    near = jnp.where(near_key != near_query, 0.0, MASK_FILL)
    return jnp.concatenate([own, near], axis=0)


def spread(rows, mask):
    return jnp.concatenate([rows] * 4, axis=0) * mask


def gather_heads(wide):
    left = iota((GROUP, 128), 1) < 64
    pairs = [wide[k * GROUP : (k + 1) * GROUP, k // 2 * 128 : k // 2 * 128 + 128] for k in range(4)]
    return jnp.concatenate([jnp.where(left, pairs[0], pairs[1]), jnp.where(left, pairs[2], pairs[3])], axis=1)


def group_rows(group):
    at = [(group // 4 * TILE + group % 4 * 32, 32)]
    for level in range(2, LEVELS):
        block = (group >> (level - 2)) ^ 1
        per_tile = TILE // (16 << level)
        at.append((block // per_tile * TILE + LEVEL_AT[level - 1] + block % per_tile * 16, 16))
    return at


def key_block(qkv, coarse, far, group, part, half):
    column = WIDTH * (part + 1) + HALF * half
    columns = slice(WIDTH * part + HALF * half, WIDTH * part + HALF * (half + 1))
    pieces = [qkv[group * GROUP : (group + 1) * GROUP, column : column + HALF]]
    pieces += [coarse[at : at + size, columns] for at, size in group_rows(group)]
    return jnp.concatenate(pieces + [far[:, columns]], axis=0)


def hier_forward(qkv, coarse, far, bias, prob, attended, live):
    mask = head_mask(0.125)
    pairs = pair_mask()
    for group in range(GROUPS):
        rows = slice(group * GROUP, (group + 1) * GROUP)
        own_bias = jnp.where(group * GROUP + iota((GROUP, QROWS), 0) < live, 0.0, MASK_FILL)
        coarse_bias = jnp.concatenate(
            [bias[at : at + size, :] for at, size in group_rows(group)] + [bias[TOKENS:, :]], axis=0
        )
        added_bias = jnp.concatenate([own_bias, jnp.concatenate([coarse_bias] * 2, axis=1)], axis=0)
        added_bias = jnp.concatenate([added_bias[: GROUP + 32] + pairs, added_bias[GROUP + 32 :]], axis=0)
        query_live = (group * GROUP + iota((GROUP, HALF), 0) < live).astype(FLOAT)
        for half in range(2):
            columns = slice(half * HALF, (half + 1) * HALF)
            queries = spread(qkv[rows, columns], mask)
            scores = dot(key_block(qkv, coarse, far, group, 0, half), queries, NT) + added_bias
            weights = jnp.exp(scores - jnp.max(scores, axis=0, keepdims=True))
            weights = weights * (1.0 / jnp.sum(weights, axis=0, keepdims=True))
            weights = weights.astype(BRAIN)
            prob[group, half, :, :] = weights
            output = dot(weights, key_block(qkv, coarse, far, group, 1, half), TN)
            attended[rows, columns] = (gather_heads(output) * query_live).astype(BRAIN)


def far_backward(qkv, far, prob, attended, grad_out, grad_far, dots):
    weights = []
    for half in range(2):
        for head in range(4):
            parts = [prob[g, half, KEYS - 16 :, head * 64 : head * 64 + 64] for g in range(GROUPS)]
            weights.append(jnp.concatenate(parts, axis=1))
    weights = jnp.concatenate(weights, axis=0)
    dims = (128, WIDTH)
    mask = jnp.where(iota(dims, 0) // 16 == iota(dims, 1) // 64, 1.0, 0.0).astype(BRAIN)
    values = jnp.concatenate([far[:, WIDTH:]] * 8, axis=0) * mask
    both = (attended[...].astype(FLOAT) * grad_out[...].astype(FLOAT)).astype(BRAIN)
    total = dot(mask, both, NT)
    score_grad = (weights.astype(FLOAT) * (dot(values, grad_out[...], NT) - total)).astype(BRAIN)
    left = iota((16, 128), 1) < 64
    for part, wide in enumerate((dot(score_grad, qkv[:, 0:WIDTH]) * 0.125, dot(weights, grad_out[...]))):
        for pair in range(4):
            block = wide[32 * pair : 32 * pair + 32, 128 * pair : 128 * pair + 128]
            to = part * WIDTH + 128 * pair
            grad_far[:, to : to + 128] = jnp.where(left, block[0:16], block[16:32])
    for group in range(GROUPS):
        for half in range(2):
            rows = [half * 64 + head * 16 for head in range(4)]
            dots[group, half, 0:1, :] = jnp.concatenate(
                [total[row : row + 1, group * GROUP : (group + 1) * GROUP] for row in rows], axis=1)


def hier_backward(qkv, coarse, far, prob, grad_out, dots, grad_q, grad_kv, grad_coarse):
    mask_q, mask_o = head_mask(0.125), head_mask(1.0)
    for group in range(GROUPS):
        own = slice(group * GROUP, (group + 1) * GROUP)
        for half in range(2):
            columns = slice(half * HALF, (half + 1) * HALF)
            queries = spread(qkv[own, columns], mask_q)
            grads = spread(grad_out[own, columns], mask_o)
            keys = key_block(qkv, coarse, far, group, 0, half)
            values = key_block(qkv, coarse, far, group, 1, half)
            weights = prob[group, half, :, :]
            score_grad = weights.astype(FLOAT) * (dot(values, grads, NT) - dots[group, half, 0:1, :])
            score_grad = score_grad.astype(BRAIN)
            grad_q[own, columns] = (gather_heads(dot(score_grad, keys, TN)) * 0.125).astype(BRAIN)
            for part, block in enumerate((dot(score_grad, queries), dot(weights, grads))):
                to = slice(part * WIDTH + half * HALF, part * WIDTH + (half + 1) * HALF)
                grad_kv[own, to] = block[0:GROUP]
                start = GROUP
                for level, (at, size) in enumerate(group_rows(group)):
                    piece = block[start : start + size]
                    start += size
                    if level < 2 or group % (1 << (level - 1)) == 0:
                        grad_coarse[at : at + size, to] = piece
                    else:
                        grad_coarse[at : at + size, to] += piece


def add_projected(stream, source, weight, bias, target):
    for column in range(0, WIDTH, 256):
        columns = slice(column, column + 256)
        total = dot(source[...], weight[:, columns])
        target[:, columns] = (stream[:, columns].astype(FLOAT) + total + bias[:, columns]).astype(
            BRAIN
        )


def feed_hidden(normed, weight, bias, hidden, slope):
    scale, cubic = 0.7978845608, 0.7978845608 * 0.044715
    for start in range(0, TOKENS, 256):
        rows = slice(start, start + 256)
        for column in range(0, FF, 256):
            columns = slice(column, column + 256)
            pre = dot(normed[rows, :], weight[:, columns]) + bias[:, columns]
            square = pre * pre
            share = 0.5 * jnp.tanh(pre * (scale + cubic * square)) + 0.5
            value = pre * share
            hidden[rows, columns] = value.astype(BRAIN)
            slope[rows, columns] = (
                share + value * ((1.0 - share) * (2 * scale + 6 * cubic * square))
            ).astype(BRAIN)


def projected_grad(qkv_grad, grad_kv, grad_coarse, grad_far, live):
    for tile in range(TILES):
        rows = slice(tile * TILE, (tile + 1) * TILE)
        matrix = pool_matrix(tile, live, True)
        share = inverse(counts(tile, live, TILE))
        for column in range(0, 2 * WIDTH, TILE):
            columns = slice(column, column + TILE)
            spans = jnp.concatenate(
                [grad_coarse[tile * TILE : tile * TILE + LEVEL_AT[4], columns],
                 grad_far[8 * tile : 8 * tile + 8, columns], jnp.zeros((8, TILE), FLOAT)], axis=0)
            total = grad_kv[rows, columns] + dot(matrix, (spans * share).astype(BRAIN))
            qkv_grad[rows, WIDTH + column : WIDTH + column + TILE] = total.astype(BRAIN)


def fetch(source, target, sem):
    copy = pltpu.make_async_copy(source, target, sem)
    copy.start()
    return copy


def reversed_bits(value, bits):
    return sum(((value >> k) & 1) << (bits - 1 - k) for k in range(bits))


def block_index(info, owner_core, rel_x, shard, bits, turned):
    rest = reversed_bits(shard, bits) ^ info[6]
    other = rest
    if turned and bits > 1:
        top, next_top = rest >> (bits - 1), (rest >> (bits - 2)) & 1
        other = (rest & ((1 << (bits - 2)) - 1)) | (next_top << (bits - 1)) | (top << (bits - 2))
    return jnp.where(owner_core == 0, (rel_x << bits) | rest, (other << 1) | rel_x)


def pair_columns(ref, section, rel_core, width):
    both = []
    for rel_x in range(2):
        quarter = section ^ (2 * rel_x + rel_core)
        both.append(ref[:, pl.ds(pl.multiple_of(quarter * width, 128), width)])
    return jnp.concatenate(both, axis=1)


def feed_weight_grads(info, rel_core, normed, pre_grad, hidden, grad, blocks, shards):
    bits = shards.bit_length() - 1
    section = info[4]
    owner = (section & 1) ^ rel_core
    rows = WIDTH // shards
    wide = FF // shards
    where = [[block_index(info, owner, rel_x, shard, bits, False) for shard in range(shards)] for rel_x in range(2)]
    for rel_x in range(2):
        quarter = section ^ (2 * rel_x + rel_core)
        for part in range(2):
            at = pl.multiple_of(quarter * 512 + 256 * part, 256)
            block = dot(normed[...], pre_grad[:, pl.ds(at, 256)], TN).astype(BRAIN)
            for shard in range(shards):
                blocks[where[rel_x][shard], 0:rows, 256 * part : 256 * part + 256] = block[shard * rows : (shard + 1) * rows]
    some_grad = pair_columns(grad, section, rel_core, 128)
    for start in range(0, FF, 256):
        block = dot(hidden[:, start : start + 256], some_grad, TN).astype(BRAIN)
        for at in range(0, 256, rows):
            shard, part = (start + at) // wide, (start + at) % wide // rows
            for rel_x in range(2):
                blocks[where[rel_x][shard], rows:, 128 * part : 128 * part + 128] = block[
                    at : at + rows, 128 * rel_x : 128 * rel_x + 128]


def attend_weight_grads(info, rel_core, normed, qkv_grad, att, grad, blocks, shards):
    bits = shards.bit_length() - 1
    section = info[4]
    owner = (section & 1) ^ rel_core
    rows = WIDTH // shards
    left = dot(normed[...], pair_columns(qkv_grad, section, rel_core, 384), TN).astype(BRAIN)
    right = dot(att[...], pair_columns(grad, section, rel_core, 128), TN).astype(BRAIN)
    for rel_x in range(2):
        for shard in range(shards):
            where = block_index(info, owner, rel_x, shard, bits, True)
            mine = slice(shard * rows, (shard + 1) * rows)
            blocks[where, :, 0:384] = left[mine, 384 * rel_x : 384 * rel_x + 384]
            blocks[where, :, 384:512] = right[mine, 128 * rel_x : 128 * rel_x + 128]


ANY = pl.BlockSpec(memory_space=pl.ANY)
VMEM = pl.BlockSpec(memory_space=pltpu.VMEM)
SMEM = pl.BlockSpec(memory_space=pltpu.SMEM)


def shape(dims, dtype=BRAIN):
    return jax.ShapeDtypeStruct(dims, dtype)


def vmem(dims, dtype=BRAIN):
    return pltpu.VMEM(dims, dtype)


def facts(ids, lengths, shards):
    section, dp = ids[0], ids[1]
    seq, half = section >> 1, section & 1
    length = lengths[seq]

    def inside(value):
        return jnp.minimum(jnp.maximum(value, 0), TOKENS)

    reverse = reversed_bits(dp, shards.bit_length() - 1)
    return seq, half, inside(length - half * TOKENS), inside(length - (1 - half) * TOKENS), section, dp, reverse


class Line:
    def __init__(self):
        self.known, self.last, self.pinned = None, None, []

    def pin(self, array):
        self.pinned.append(array)

    def call(self, body, outs, args, scratch, us, name, limit=16, out_specs=None, aliases=None):
        known = [] if self.known is None else [pltpu.with_memory_space_constraint(self.known, pltpu.SMEM)]
        first = len(known)
        count = first + len(args)
        after = there(*([] if self.last is None else [self.last]), *self.pinned)
        self.pinned = []

        def kernel(*refs):
            info = [refs[0][k] for k in range(7)] if known else None
            body(info, *refs[first:count], *refs[count + len(after) :])

        result = pl.pallas_call(
            kernel,
            out_shape=outs,
            in_specs=[SMEM] * first + [spec for spec, _ in args + after],
            out_specs=out_specs or [VMEM] * len(outs),
            scratch_shapes=scratch,
            input_output_aliases={first + k: v for k, v in (aliases or {}).items()},
            compiler_params=pltpu.CompilerParams(vmem_limit_bytes=limit * MIB),
            cost_estimate=pl.CostEstimate(flops=int(us * COST), bytes_accessed=1024, transcendentals=0),
            name=name,
        )(*known, *[array for _, array in args + after])
        if out_specs is None:
            self.last = result[-1]
        return result


def first_kernel(shards, _info, ids, lengths, inputs, hag, hab, hob, hfg, hfb, hub, hdb, hwp, hwo, hwu, hwd,
                 ag, ab, ob, fg, fb, ub, db, wp, wo, wu, wd,
                 qkv, coarse, far, prob, att, mine, mid, hidden, slope, out, qkv_next, coarse_next, info_out, pooled,
                 other, normed, keyed, bias, sems):
    info = facts(ids, lengths, shards)
    for k, value in enumerate(info):
        info_out[k] = value
    seq, half, live, other_live = info[0], info[1], info[2], info[3]
    get_mine = fetch(inputs.at[seq, pl.ds(half * TOKENS, TOKENS)], mine, sems.at[0])
    small = [fetch(source, target, sems.at[2 + k]) for k, (source, target) in enumerate(
        ((hag, ag), (hab, ab), (hob, ob), (hfg, fg), (hfb, fb), (hub, ub), (hdb, db)))]
    get_wp = fetch(hwp.at[0], wp.at[0], sems.at[9])
    get_other = fetch(inputs.at[seq, pl.ds((1 - half) * TOKENS, TOKENS)], other, sems.at[1])
    large = [fetch(source.at[0], target.at[0], sems.at[10 + k]) for k, (source, target) in enumerate(
        ((hwo, wo), (hwu, wu), (hwd, wd)))]
    later = [fetch(source.at[1], target.at[1], sems.at[13 + k]) for k, (source, target) in enumerate(
        ((hwp, wp), (hwo, wo), (hwu, wu), (hwd, wd)))]
    key_bias(live, other_live, bias)
    for copy in small:
        copy.wait()
    get_mine.wait()
    norm_into(mine, ag[0:1, :], ab[0:1, :], normed)
    get_wp.wait()
    project(normed, wp.at[0], qkv, 0, 3 * WIDTH)
    get_other.wait()
    norm_into(other, ag[0:1, :], ab[0:1, :], normed)
    project(normed, wp.at[0], keyed, WIDTH, 3 * WIDTH, 0)
    pool_far(keyed, other_live, far)
    pool_keys(qkv, live, coarse, pooled)
    hier_forward(qkv, coarse, far, bias, prob, att, live)
    large[0].wait()
    add_projected(mine, att, wo.at[0], ob[0:1, :], mid)
    norm_into(mid, fg[0:1, :], fb[0:1, :], normed)
    large[1].wait()
    feed_hidden(normed, wu.at[0], ub[0:1, :], hidden, slope)
    large[2].wait()
    add_projected(mid, hidden, wd.at[0], db[0:1, :], out)
    norm_into(out, ag[1:2, :], ab[1:2, :], normed)
    later[0].wait()
    project(normed, wp.at[1], qkv_next, 0, 3 * WIDTH)
    pool_keys(qkv_next, live, coarse_next, pooled)
    for copy in later[1:]:
        copy.wait()


def second_kernel(info, qkv, coarse, far, stream, ob, fg, fb, ub, wo, wu,
                  prob, att, mid, normed, hidden, slope, bias):
    live, other_live = info[2], info[3]
    key_bias(live, other_live, bias)
    hier_forward(qkv, coarse, far, bias, prob, att, live)
    add_projected(stream, att, wo.at[1], ob[1:2, :], mid)
    norm_into(mid, fg[1:2, :], fb[1:2, :], normed)
    feed_hidden(normed, wu.at[1], ub[1:2, :], hidden, slope)


def feed_back_send(layer, shards, take_grad, take_norm, info, *refs):
    refs = list(refs)
    source = refs.pop(0)
    hidden, slope, wd = refs[:3]
    del refs[:3]
    if take_norm:
        stream, gain, shift = refs[:3]
        del refs[:3]
    else:
        normed = refs.pop(0)
    pre_grad, sums, send = refs[:3]
    del refs[:3]
    if take_grad:
        grad = refs.pop(0)
    if take_norm:
        normed = refs.pop(0)
    if take_grad:
        copy = fetch(source.at[info[0], pl.ds(info[1] * TOKENS, TOKENS)], grad, refs[0].at[0])
        copy.wait()
    else:
        grad = source
    if take_norm:
        norm_into(stream, gain[layer : layer + 1, :], shift[layer : layer + 1, :], normed)
    for column in range(0, FF, 256):
        columns = slice(column, column + 256)
        back = dot(grad[...], wd[layer, columns, :], NT) * slope[:, columns].astype(FLOAT)
        back = back.astype(BRAIN)
        pre_grad[:, columns] = back
        sums[3 + column // 512 : 4 + column // 512, column % 512 : column % 512 + 256] = jnp.sum(
            back.astype(FLOAT), axis=0, keepdims=True
        )
    feed_weight_grads(info, 1, normed, pre_grad, hidden, grad, send, shards)
    sums[0:2, :] = jnp.zeros((2, WIDTH), FLOAT)
    sums[2:3, :] = jnp.sum(grad[...].astype(FLOAT), axis=0, keepdims=True)
    sums[7:8, :] = jnp.zeros((1, WIDTH), FLOAT)


def feed_back_keep(layer, shards, info, grad, normed, pre_grad, hidden, stream, gain, wu, sums_in, wo, qkv, far, prob, att,
                   target, sums, keep, grad_out, dots, grad_far, norm_grad):
    feed_weight_grads(info, 0, normed, pre_grad, hidden, grad, keep, shards)
    for column in range(0, WIDTH, 256):
        norm_grad[:, column : column + 256] = dot(pre_grad[...], wu[layer, column : column + 256, :], NT)
    sums[...] = sums_in[...]
    norm_back(stream, gain[layer : layer + 1, :], norm_grad, grad, target, sums.at[0:1, :], sums.at[1:2, :])
    for column in range(0, WIDTH, 256):
        back = dot(target[...], wo[layer, column : column + 256, :], NT)
        back = back * (iota((TOKENS, 256), 0) < info[2]).astype(FLOAT)
        grad_out[:, column : column + 256] = back.astype(BRAIN)
    far_backward(qkv, far, prob, att, grad_out, grad_far, dots)


def split_pieces(rows, section, own, far, near):
    targets = {0: own, 2: far}
    for k in range(4):
        piece = rows[:, pl.ds(pl.multiple_of((section ^ k) * 128, 128), 128)]
        if k % 2 == 0:
            targets[k][...] = piece
        else:
            near[k // 2, :, :] = piece


def last_output(layer, info, mid, hidden, wd, db, own, far, near, final):
    for column in range(0, WIDTH, 256):
        columns = slice(column, column + 256)
        total = dot(hidden[...], wd[layer, :, columns])
        final[:, columns] = (mid[:, columns].astype(FLOAT) + total + db[layer : layer + 1, columns]).astype(BRAIN)
    split_pieces(final, info[4], own, far, near)


def attend_back(info, qkv, coarse, far, prob, grad_out, dots, grad_q, grad_kv, grad_coarse):
    hier_backward(qkv, coarse, far, prob, grad_out, dots, grad_q, grad_kv, grad_coarse)


def project_back(layer, shards, info, grad, stream, att, grad_q, grad_kv, grad_coarse, grad_far, gain, shift,
                 qkv_grad, send, keep, normed):
    norm_into(stream, gain[layer : layer + 1, :], shift[layer : layer + 1, :], normed)
    qkv_grad[:, 0:WIDTH] = grad_q[...]
    projected_grad(qkv_grad, grad_kv, grad_coarse, grad_far, info[2])
    attend_weight_grads(info, 1, normed, qkv_grad, att, grad, send, shards)
    attend_weight_grads(info, 0, normed, qkv_grad, att, grad, keep, shards)


def project_back_norm(layer, last, info, grad, stream, qkv_grad, gain, wp, *refs):
    section = info[4]
    refs = list(refs)
    if last:
        earlier = refs[:3]
        del refs[:3]
        own, far, near, small, norm_grad, target, sums = refs
    else:
        mid, hidden, wd, db, target, sums, own, far, near, norm_grad, final = refs
        last_output(layer, info, mid, hidden, wd, db, own, far, near, final)
    for column in range(0, WIDTH, 256):
        norm_grad[:, column : column + 256] = dot(qkv_grad[...], wp[layer, column : column + 256, :], NT)
    norm_back(stream, gain[layer : layer + 1, :], norm_grad, grad, target, sums.at[0:1, :], sums.at[1:2, :])
    if last:
        split_pieces(target, section, own, far, near)
    sums[2:3, :] = jnp.sum(grad[...].astype(FLOAT), axis=0, keepdims=True)
    sums[3:8, :] = jnp.zeros((5, WIDTH), FLOAT)
    if last:
        feed_one, attend_one, feed_zero = earlier
        for k, sublayer in enumerate((sums, feed_zero, attend_one, feed_one)):
            up = feed_zero if k < 2 else feed_one
            small[k, 0:3, :] = sublayer[0:3, :]
            small[k, 3:5, :] = up[3 + k % 2 * 2 : 5 + k % 2 * 2, :]
            small[k, 5:, :] = jnp.zeros((11, WIDTH), FLOAT)


def add_halves(info, *refs):
    *pairs, give, kept = refs
    half = give.shape[0]

    def body(k, carry):
        row = 0
        for mine, came in zip(pairs[::2], pairs[1::2]):
            rows = slice(row, row + mine.shape[1])
            row += mine.shape[1]
            give[k, rows, :] = mine[half + k] + came[half + k]
            kept[k, rows, :] = mine[k] + came[k]
        return carry

    lax.fori_loop(0, half, body, 0)


def add_last(info, *refs):
    *pairs, total = refs
    row = 0
    for mine, came in zip(pairs[::2], pairs[1::2]):
        rows = slice(row, row + mine.shape[1])
        row += mine.shape[1]
        total[rows, :] = mine[0] + came[0]


def add_first(info, mine, came, small, small_came, give, kept):
    half, rows = give.shape[0], mine.shape[1]
    core, bits = info[4] & 1, half.bit_length() - 1

    def body(k, carry):
        for target, block in ((give, half + k), (kept, k)):
            target[k, 0:rows, :] = mine[block] + came[block]
            rel_x = jnp.where(core == 0, block >> bits, block & 1)
            quarter = info[4] ^ (2 * rel_x)
            target[k, rows:, :] = (small[quarter] + small_came[quarter]).astype(BRAIN)
        return carry

    lax.fori_loop(0, half, body, 0)


def place_shares(layer, shards, section, pieces, outs, stages, sems):
    up, down, proj, back = stages
    rows = WIDTH // shards
    for k in range(4):
        owner = section ^ k
        piece = pieces[k]
        up[:, pl.ds(pl.multiple_of(owner * 512, 512), 512)] = piece[0:rows, :].astype(FLOAT)
        for part in range(FF // WIDTH):
            down[part * rows : (part + 1) * rows, pl.ds(pl.multiple_of(owner * 128, 128), 128)] = piece[
                rows : 2 * rows, 128 * part : 128 * part + 128].astype(FLOAT)
        proj[:, pl.ds(pl.multiple_of(owner * 384, 128), 384)] = piece[2 * rows : 3 * rows, 0:384].astype(FLOAT)
        back[:, pl.ds(pl.multiple_of(owner * 128, 128), 128)] = piece[2 * rows : 3 * rows, 384:].astype(FLOAT)
    return [fetch(stage, out.at[layer], sems.at[k]) for k, (stage, out) in enumerate(zip(stages, outs))]


def finish_tokens(info, own, near, across, target, done, sems):
    section = info[4]
    copies = []
    for k, piece in enumerate((own, near.at[0], across.at[0], across.at[1])):
        owner = section ^ k
        to = target.at[owner >> 1, pl.ds(pl.multiple_of((owner & 1) * TOKENS, TOKENS), TOKENS)]
        copies.append(fetch(piece, to, sems.at[k]))
    done[...] = jnp.zeros((8, 128), FLOAT)
    for copy in copies:
        copy.wait()


def finish_one(shards, info, own, near, across, beyond, up, down, proj, back, *scratch):
    section, sems = info[4], scratch[-1]
    copies = place_shares(1, shards, section, (own, near, across, beyond), (up, down, proj, back), scratch[:4], sems)
    for copy in copies:
        copy.wait()


def finish_zero(shards, info, own, near, across, beyond, _up, _down, _proj, _back,
                up, down, proj, back, gain_a, bias_a, bias_o, gain_f, bias_f, bias_u, bias_d, *scratch):
    section, dp, small, sems = info[4], info[5], scratch[-2], scratch[-1]
    pieces = (own, near, across, beyond)
    copies = place_shares(0, shards, section, pieces, (up, down, proj, back), scratch[:4], sems)
    width = WIDTH // shards
    for k in range(4):
        small[section ^ k, :, :] = pieces[k][3 * width :, :].astype(FLOAT)
    total = jnp.concatenate([small[k, 0:8, :] for k in range(4)], axis=0)

    def taken(start, columns):
        pick = (iota((WIDTH, columns), 0) == start + iota((WIDTH, columns), 1)).astype(FLOAT)
        return lax.dot_general(total, pick, NN, precision=lax.Precision.HIGHEST, preferred_element_type=FLOAT)

    part = taken(dp * width, width)
    for layer in range(2):
        attend, feed = 16 * layer, 16 * layer + 8
        for start, outs in ((attend, (gain_a, bias_a, bias_o)), (feed, (gain_f, bias_f, bias_d))):
            for k, out in enumerate(outs):
                out[layer : layer + 1, :] = part[start + k : start + k + 1]
    wide = FF // shards
    per_row = WIDTH // wide
    part = taken(dp % per_row * wide, wide)
    for layer in range(2):
        row = part[16 * layer + 3 : 16 * layer + 4]
        for k in range(1, 4):
            at = 16 * layer + 8 * (k // 2) + 3 + k % 2
            row = jnp.where(dp // per_row == k, part[at : at + 1], row)
        bias_u[layer : layer + 1, :] = row
    for copy in copies:
        copy.wait()


def swap(block, partner):
    sections = lax.axis_size("section")
    pairs = []
    for dp in range(lax.axis_size("dp")):
        for section in range(sections):
            to_dp, to_section = partner(dp, section)
            pairs.append((dp * sections + section, to_dp * sections + to_section))
    return lax.ppermute(block, ("dp", "section"), pairs)


def over_section(block, bits):
    return swap(block, lambda dp, section: (dp, section ^ bits))


def there(*arrays):
    return [(VMEM, pltpu.with_memory_space_constraint(array, pltpu.VMEM)) for array in arrays]


def in_hbm(*arrays):
    return [(ANY, pltpu.with_memory_space_constraint(array, pltpu.HBM)) for array in arrays]


class Reduction:
    def __init__(self, line, name, send, turned):
        self.line, self.name, self.turned = line, name, turned
        self.bits = lax.axis_size("dp").bit_length() - 1
        self.came = over_section(send, 1)
        self.done = 0

    def partner(self, dp, section):
        step, core = self.done, section & 1
        over_x = step == 0 if core == 0 else step == self.bits
        if over_x:
            return dp, section ^ 2
        bit = step - 1 + core
        if core == 1 and self.turned and self.bits > 1 and step < 2:
            bit = 1 - step
        return dp ^ (1 << bit), section

    def keep(self, blocks):
        self.mine = blocks

    def step(self, other=None, small=None):
        pairs = there(self.mine) + there(self.came)
        dims = list(self.mine.shape)
        if other is not None:
            pairs += there(other.mine) + there(other.came)
            dims[1] += other.mine.shape[1]
        dims[0] //= 2
        body = add_halves
        if small is not None:
            body = add_first
            pairs += there(small, over_section(small, 1))
            dims[1] += small.shape[1]
        give, self.mine = self.line.call(body, [vmem(dims)] * 2, pairs, [], 0.2, self.name + str(self.done))
        self.came = swap(give, self.partner)
        self.done += 1

    def last(self, other=None):
        while self.done <= self.bits:
            self.step(other)
            other = None
        pairs = there(self.mine) + there(self.came)
        rows = self.mine.shape[1]
        if other is not None:
            pairs += there(other.mine) + there(other.came)
            rows += other.mine.shape[1]
        (total,) = self.line.call(add_last, [vmem((rows, WIDTH))], pairs, [], 0.1, self.name + "_last")
        return total


def over_all_sections(share):
    across = over_section(share, 2)
    return share, over_section(share, 1), across, over_section(across, 1)


def exchange_pieces(own, far, near):
    came = over_section(near, 1)
    across = over_section(jnp.concatenate([far[None], came[1:]], axis=0), 2)
    return own, came, across


def finish_rows(line, pieces, name):
    outs = [shape((2, 2 * TOKENS, 128)), vmem((8, 128), FLOAT)]
    target, line.last = line.call(
        finish_tokens, outs, [(ANY, array) for array in exchange_pieces(*pieces)],
        [pltpu.SemaphoreType.DMA((4,))], 1.2, name, out_specs=[ANY, VMEM],
    )
    return target


def local(inputs, lengths, ag, ab, wp, wo, ob, fg, fb, wu, ub, wd, db, cotangent):
    shards = lax.axis_size("dp")
    ids = jnp.stack([lax.axis_index("section"), lax.axis_index("dp")]).astype(jnp.int32)
    line = Line()

    rows, wide, tall = vmem((TOKENS, WIDTH)), vmem((TOKENS, FF)), vmem((TOKENS, 3 * WIDTH))
    rows_float, double_float = vmem((TOKENS, WIDTH), FLOAT), vmem((TOKENS, 2 * WIDTH), FLOAT)
    coarse_shape, far_shape = vmem((TOKENS, 2 * WIDTH)), vmem((16, 2 * WIDTH))
    prob_shape = vmem((GROUPS, 2, KEYS, QROWS))
    bias_shape = vmem((TOKENS + 16, 128), FLOAT)
    sums_shape = vmem((8, WIDTH), FLOAT)
    piece, two_pieces = vmem((TOKENS, 128)), vmem((2, TOKENS, 128))
    params = (ag, ab, ob, fg, fb, ub, db, wp, wo, wu, wd)
    (ag, ab, ob, fg, fb, ub, db, wp, wo, wu, wd,
     qkv0, coarse0, far0, prob0, att0, stream0, mid0, hidden0, slope0, stream1, qkv1, coarse1, info, pooled) = line.call(
        functools.partial(first_kernel, shards),
        [vmem(array.shape, array.dtype) for array in params]
        + [tall, coarse_shape, far_shape, prob_shape, rows, rows, rows, wide, wide, rows, tall, coarse_shape,
           pltpu.SMEM((8,), jnp.int32), far_shape],
        [(SMEM, ids), (SMEM, lengths)] + in_hbm(inputs, *params),
        [rows, rows, coarse_shape, bias_shape, pltpu.SemaphoreType.DMA((17,))],
        13.5, "layer_zero_forward", out_specs=[VMEM] * 23 + [SMEM, VMEM],
    )
    line.known, line.last = info, pooled
    far1 = over_section(pooled, 1)
    prob1, att1, mid1, normed1, hidden1, slope1 = line.call(
        second_kernel, [prob_shape, rows, rows, rows, wide, wide],
        there(qkv1, coarse1, far1, stream1, ob, fg, fb, ub, wo, wu), [bias_shape],
        6.8, "layer_one_forward",
    )

    feed_blocks = vmem((2 * shards, WIDTH // shards + FF // shards // 4, WIDTH))
    attend_blocks = vmem((2 * shards, WIDTH // shards, WIDTH))
    sem = pltpu.SemaphoreType.DMA((1,))

    dots_shape = vmem((GROUPS, 2, 8, QROWS), FLOAT)
    far_float = vmem((16, 2 * WIDTH), FLOAT)

    pre_grad, sums_f1, send, grad_last = line.call(
        functools.partial(feed_back_send, 1, shards, True, False), [wide, sums_shape, feed_blocks, rows],
        in_hbm(cotangent) + there(hidden1, slope1, wd, normed1), [sem], 4.5, "feed_back_send_1",
    )
    feed_one = Reduction(line, "feed_one_", send, False)
    grad3, sums_f1, keep, grad_out, dots, grad_far = line.call(
        functools.partial(feed_back_keep, 1, shards), [rows, sums_shape, feed_blocks, rows, dots_shape, far_float],
        there(grad_last, normed1, pre_grad, hidden1, mid1, fg, wu, sums_f1, wo, qkv1, far1, prob1, att1), [rows_float],
        5.5, "feed_back_keep_1",
    )
    grad_far = over_section(grad_far, 1)
    feed_one.keep(keep)
    feed_one.step()
    grad_q, grad_kv, grad_coarse = line.call(
        attend_back, [rows, double_float, double_float],
        there(qkv1, coarse1, far1, prob1, grad_out, dots), [], 4.3, "attend_back_1",
    )
    qkv_grad, send, keep = line.call(
        functools.partial(project_back, 1, shards), [tall, attend_blocks, attend_blocks],
        there(grad3, stream1, att1, grad_q, grad_kv, grad_coarse, grad_far, ag, ab), [rows], 3.4, "project_back_1",
    )
    attend_one = Reduction(line, "attend_one_", send, True)
    attend_one.keep(keep)
    grad2, sums_a1, *out_pieces = line.call(
        functools.partial(project_back_norm, 1, False), [rows, sums_shape, piece, piece, two_pieces],
        there(grad3, stream1, qkv_grad, ag, wp, mid1, hidden1, wd, db), [rows_float, rows], 3.0, "project_back_norm_1",
    )
    feed_one.step()
    attend_one.step()
    pre_grad, sums_f0, send, normed = line.call(
        functools.partial(feed_back_send, 0, shards, False, True), [wide, sums_shape, feed_blocks, rows],
        there(grad2, hidden0, slope0, wd, mid0, fg, fb), [], 3.7, "feed_back_send_0",
    )
    feed_zero = Reduction(line, "feed_zero_", send, False)
    grad1, sums_f0, keep, grad_out, dots, grad_far = line.call(
        functools.partial(feed_back_keep, 0, shards), [rows, sums_shape, feed_blocks, rows, dots_shape, far_float],
        there(grad2, normed, pre_grad, hidden0, mid0, fg, wu, sums_f0, wo, qkv0, far0, prob0, att0), [rows_float],
        5.5, "feed_back_keep_0",
    )
    grad_far = over_section(grad_far, 1)
    feed_zero.keep(keep)
    feed_zero.step()
    grad_q, grad_kv, grad_coarse = line.call(
        attend_back, [rows, double_float, double_float],
        there(qkv0, coarse0, far0, prob0, grad_out, dots), [], 4.3, "attend_back_0",
    )
    attend_one.step()
    line.pin(feed_one.came)
    qkv_grad, send, keep = line.call(
        functools.partial(project_back, 0, shards), [tall, attend_blocks, attend_blocks],
        there(grad1, stream0, att0, grad_q, grad_kv, grad_coarse, grad_far, ag, ab), [rows], 3.4, "project_back_0",
    )
    attend_zero = Reduction(line, "attend_zero_", send, True)
    attend_zero.keep(keep)
    *grad_pieces, small = line.call(
        functools.partial(project_back_norm, 0, True), [piece, piece, two_pieces, vmem((4, 16, WIDTH), FLOAT)],
        there(grad1, stream0, qkv_grad, ag, wp, sums_f1, sums_a1, sums_f0), [rows_float, rows, sums_shape], 2.3,
        "project_back_norm_0",
    )
    feed_zero.step()
    attend_zero.step(small=small)
    feed_one.step(attend_one)
    attend_zero.step()
    feed_one.step()
    feed_zero.step(attend_zero)
    outputs = finish_rows(line, out_pieces, "finish_outputs")
    share_one = feed_one.last()
    feed_zero.step()
    input_grad = finish_rows(line, grad_pieces, "finish_input_grad")
    share_zero = feed_zero.last()

    weight_grads = [
        shape((2, WIDTH // shards, FF), FLOAT), shape((2, FF // shards, WIDTH), FLOAT),
        shape((2, WIDTH // shards, 3 * WIDTH), FLOAT), shape((2, WIDTH // shards, WIDTH), FLOAT),
    ]
    stages = [vmem(out.shape[1:], FLOAT) for out in weight_grads]
    stages += [vmem((4, 16, WIDTH), FLOAT), pltpu.SemaphoreType.DMA((4,))]
    weight_first = line.call(
        functools.partial(finish_one, shards), weight_grads, there(*over_all_sections(share_one)),
        stages, 1.9, "finish_one", out_specs=[ANY] * 4,
    )
    vector = shape((2, WIDTH // shards), FLOAT)
    vectors = [vector] * 5 + [shape((2, FF // shards), FLOAT), vector]
    finished = line.call(
        functools.partial(finish_zero, shards), weight_grads + vectors,
        there(*over_all_sections(share_zero)) + [(ANY, array) for array in weight_first],
        stages, 3.0, "finish_zero", out_specs=[ANY] * 4 + [VMEM] * 7, aliases={4 + k: k for k in range(4)},
    )
    up_grad, down_grad, proj_grad, back_grad, gain_a, bias_a, bias_o, gain_f, bias_f, bias_u, bias_d = finished
    return (outputs, input_grad, gain_a, bias_a, proj_grad, back_grad, bias_o, gain_f, bias_f, up_grad, bias_u,
            down_grad, bias_d)


def solution(mesh):
    batch = P("dp", None, None)
    split = P("dp", None, "section")
    vector, matrix = P(None, "dp"), P(None, "dp", None)
    return jax.shard_map(
        local,
        mesh=mesh,
        in_specs=(batch, P("dp")) + (P(),) * 11 + (batch,),
        out_specs=(split, split, vector, vector, matrix, matrix, vector, vector, vector, matrix, vector, matrix, vector),
        check_vma=False,
    )
```

```python
import functools

import jax
import jax.numpy as jnp
from jax import lax
from jax.experimental import pallas as pl
from jax.experimental.pallas import tpu as pltpu
from jax.sharding import PartitionSpec as P

FLOAT = jnp.float32
BRAIN = jnp.bfloat16
NORM_EPS = 1e-05
MASK_FILL = -1000000000.0
WIDTH = 512
TOKENS = 512
FF = 2048
GROUP = 64
GROUPS = TOKENS // GROUP
LEVELS = 5
KEYS = GROUP + 32 + 16 * (LEVELS - 1)
HALF = 256
QROWS = 4 * GROUP
TILE = 256
TILES = TOKENS // TILE
LEVEL_AT = (0, 128, 192, 224, 240)
USED = 248
MIB = 1024 * 1024
FEED_ORDERS = ((("x", 1, 0, 2), (1, 0, "x", 2)), (("x", 0, 1, 2), (0, 1, 2, "x")))
ATTEND_ORDERS = ((("x", 0, 1, 2), (0, "x", 1, 2)), (("x", 0, 1, 2), (1, 0, 2, "x")))
COST = 1 * 10**9

NN = (((1,), (0,)), ((), ()))
NT = (((1,), (1,)), ((), ()))
TN = (((0,), (0,)), ((), ()))


def dot(left, right, dims=NN):
    return lax.dot_general(left, right, dims, preferred_element_type=FLOAT)


def iota(shape, dim):
    return lax.broadcasted_iota(jnp.int32, shape, dim)


def normalise(rows):
    mean = jnp.mean(rows, axis=-1, keepdims=True)
    centred = rows - mean
    scale = lax.rsqrt(jnp.mean(centred * centred, axis=-1, keepdims=True) + NORM_EPS)
    return centred * scale, scale


def norm_into(source, gain, bias, target):
    for start in range(0, TOKENS, 64):
        rows = slice(start, start + 64)
        unit, _ = normalise(source[rows, :].astype(FLOAT))
        target[rows, :] = (unit * gain + bias).astype(BRAIN)


def norm_back(source, gain, grad_ref, through_ref, target, gain_out, bias_out):
    gain_sum = jnp.zeros((1, WIDTH), FLOAT)
    bias_sum = jnp.zeros((1, WIDTH), FLOAT)
    for start in range(0, TOKENS, 64):
        rows = slice(start, start + 64)
        unit, scale = normalise(source[rows, :].astype(FLOAT))
        grad = grad_ref[rows, :]
        gain_sum = gain_sum + jnp.sum(grad * unit, axis=0, keepdims=True)
        bias_sum = bias_sum + jnp.sum(grad, axis=0, keepdims=True)
        inner = grad * gain
        inner_mean = jnp.mean(inner, axis=-1, keepdims=True)
        slope = jnp.mean(inner * unit, axis=-1, keepdims=True)
        back = scale * (inner - inner_mean - unit * slope)
        target[rows, :] = (through_ref[rows, :].astype(FLOAT) + back).astype(BRAIN)
    gain_out[...] = gain_sum
    bias_out[...] = bias_sum


def span_of(row):
    level = 1 + sum((row >= at).astype(jnp.int32) for at in LEVEL_AT[1:])
    at = sum(jnp.where(level == k + 1, at, 0) for k, at in enumerate(LEVEL_AT))
    return level, (row - at) << level


def pool_matrix(tile, live, transposed):
    dims = (TILE, TILE)
    row, token = iota(dims, int(transposed)), iota(dims, 1 - int(transposed))
    level, first = span_of(row)
    inside = (token >= first) & (token < first + (1 << level)) & (token < live - tile * TILE) & (row < USED)
    return inside.astype(FLOAT).astype(BRAIN)


def counts(tile, live, columns):
    level, first = span_of(iota((TILE, columns), 0))
    return jnp.clip(live - tile * TILE - first, 0, 1 << level)


def far_counts(live, columns):
    return jnp.clip(live - (iota((16, columns), 0) << LEVELS), 0, 1 << LEVELS)


def inverse(number):
    return 1.0 / jnp.maximum(number, 1).astype(FLOAT)


def log_count(number):
    return jnp.where(number > 0, jnp.log(jnp.maximum(number, 1).astype(FLOAT)), MASK_FILL)


def project(normed, weight, target, start, stop, target_start=None):
    shift = 0 if target_start is None else target_start - start
    for column in range(start, stop, 256):
        target[:, column + shift : column + shift + 256] = dot(
            normed[...], weight[:, column : column + 256]
        ).astype(BRAIN)


def pool_keys(qkv, live, coarse, pooled):
    matrix = [pool_matrix(tile, live, False) for tile in range(TILES)]
    share = [inverse(counts(tile, live, TILE)) for tile in range(TILES)]
    for column in range(0, 2 * WIDTH, TILE):
        columns = slice(column, column + TILE)
        last = []
        for tile in range(TILES):
            rows = slice(tile * TILE, (tile + 1) * TILE)
            mean = dot(matrix[tile], qkv[rows, WIDTH + column : WIDTH + column + TILE]) * share[tile]
            coarse[rows, columns] = mean.astype(BRAIN)
            last.append(mean[LEVEL_AT[4] : USED])
        pooled[:, columns] = jnp.concatenate(last, axis=0).astype(BRAIN)


def project_far(normed, weight, live, pooled):
    key, token = iota((16, TOKENS), 0), iota((16, TOKENS), 1)
    matrix = ((token >> LEVELS == key) & (token < live)).astype(FLOAT).astype(BRAIN)
    mean = dot(matrix, normed[...]) * inverse(far_counts(live, WIDTH))
    high = mean.astype(BRAIN)
    both = jnp.concatenate([high, (mean - high.astype(FLOAT)).astype(BRAIN)], axis=0)
    for column in range(0, 2 * WIDTH, 256):
        product = dot(both, weight[:, WIDTH + column : WIDTH + column + 256])
        pooled[:, column : column + 256] = (product[0:16] + product[16:32]).astype(BRAIN)


def key_bias(live, other_live, bias):
    for tile in range(TILES):
        bias[tile * TILE : (tile + 1) * TILE, :] = log_count(counts(tile, live, 128))
    bias[TOKENS:, :] = log_count(far_counts(other_live, 128))


def head_mask(value):
    dims = (QROWS, HALF)
    return jnp.where(iota(dims, 0) // GROUP == iota(dims, 1) // 64, value, 0.0).astype(BRAIN)


def pair_mask():
    own_key, own_query = iota((GROUP, QROWS), 0) // 32, iota((GROUP, QROWS), 1) % GROUP // 32
    near_key, near_query = iota((32, QROWS), 0) // 16, iota((32, QROWS), 1) % GROUP // 32
    own = jnp.where(own_key == own_query, 0.0, MASK_FILL)
    near = jnp.where(near_key != near_query, 0.0, MASK_FILL)
    return jnp.concatenate([own, near], axis=0)


def spread(rows, mask):
    return jnp.concatenate([rows] * 4, axis=0) * mask


def gather_heads(wide):
    left = iota((GROUP, 128), 1) < 64
    pairs = [wide[k * GROUP : (k + 1) * GROUP, k // 2 * 128 : k // 2 * 128 + 128] for k in range(4)]
    return jnp.concatenate([jnp.where(left, pairs[0], pairs[1]), jnp.where(left, pairs[2], pairs[3])], axis=1)


def group_rows(group):
    at = [(group // 4 * TILE + group % 4 * 32, 32)]
    for level in range(2, LEVELS):
        block = (group >> (level - 2)) ^ 1
        per_tile = TILE // (16 << level)
        at.append((block // per_tile * TILE + LEVEL_AT[level - 1] + block % per_tile * 16, 16))
    return at


def key_block(qkv, coarse, far, group, part, half):
    column = WIDTH * (part + 1) + HALF * half
    columns = slice(WIDTH * part + HALF * half, WIDTH * part + HALF * (half + 1))
    pieces = [qkv[group * GROUP : (group + 1) * GROUP, column : column + HALF]]
    pieces += [coarse[at : at + size, columns] for at, size in group_rows(group)]
    return jnp.concatenate(pieces + [far[:, columns]], axis=0)


def hier_forward(qkv, coarse, far, bias, prob, attended, live):
    mask = head_mask(0.125)
    pairs = pair_mask()
    for group in range(GROUPS):
        rows = slice(group * GROUP, (group + 1) * GROUP)
        own_bias = jnp.where(group * GROUP + iota((GROUP, QROWS), 0) < live, 0.0, MASK_FILL)
        coarse_bias = jnp.concatenate(
            [bias[at : at + size, :] for at, size in group_rows(group)] + [bias[TOKENS:, :]], axis=0
        )
        added_bias = jnp.concatenate([own_bias, jnp.concatenate([coarse_bias] * 2, axis=1)], axis=0)
        added_bias = jnp.concatenate([added_bias[: GROUP + 32] + pairs, added_bias[GROUP + 32 :]], axis=0)
        query_live = (group * GROUP + iota((GROUP, HALF), 0) < live).astype(FLOAT)
        for half in range(2):
            columns = slice(half * HALF, (half + 1) * HALF)
            queries = spread(qkv[rows, columns], mask)
            scores = dot(key_block(qkv, coarse, far, group, 0, half), queries, NT) + added_bias
            weights = jnp.exp(scores - jnp.max(scores, axis=0, keepdims=True))
            weights = weights * (1.0 / jnp.sum(weights, axis=0, keepdims=True))
            weights = weights.astype(BRAIN)
            prob[group, half, :, :] = weights
            output = dot(weights, key_block(qkv, coarse, far, group, 1, half), TN)
            attended[rows, columns] = (gather_heads(output) * query_live).astype(BRAIN)


def far_backward(qkv, far, prob, attended, grad_out, grad_far, dots):
    weights = []
    for half in range(2):
        for head in range(4):
            parts = [prob[g, half, KEYS - 16 :, head * 64 : head * 64 + 64] for g in range(GROUPS)]
            weights.append(jnp.concatenate(parts, axis=1))
    weights = jnp.concatenate(weights, axis=0)
    dims = (128, WIDTH)
    mask = jnp.where(iota(dims, 0) // 16 == iota(dims, 1) // 64, 1.0, 0.0).astype(BRAIN)
    values = jnp.concatenate([far[:, WIDTH:]] * 8, axis=0) * mask
    both = (attended[...].astype(FLOAT) * grad_out[...].astype(FLOAT)).astype(BRAIN)
    total = dot(mask, both, NT)
    score_grad = (weights.astype(FLOAT) * (dot(values, grad_out[...], NT) - total)).astype(BRAIN)
    left = iota((16, 128), 1) < 64
    for part, wide in enumerate((dot(score_grad, qkv[:, 0:WIDTH]) * 0.125, dot(weights, grad_out[...]))):
        for pair in range(4):
            block = wide[32 * pair : 32 * pair + 32, 128 * pair : 128 * pair + 128]
            to = part * WIDTH + 128 * pair
            grad_far[:, to : to + 128] = jnp.where(left, block[0:16], block[16:32])
    for group in range(GROUPS):
        for half in range(2):
            rows = [half * 64 + head * 16 for head in range(4)]
            dots[group, half, 0:1, :] = jnp.concatenate(
                [total[row : row + 1, group * GROUP : (group + 1) * GROUP] for row in rows], axis=1)


def hier_backward(qkv, coarse, far, prob, grad_out, dots, grad_q, grad_kv, grad_coarse):
    mask_q, mask_o = head_mask(0.125), head_mask(1.0)
    for group in range(GROUPS):
        own = slice(group * GROUP, (group + 1) * GROUP)
        for half in range(2):
            columns = slice(half * HALF, (half + 1) * HALF)
            queries = spread(qkv[own, columns], mask_q)
            grads = spread(grad_out[own, columns], mask_o)
            keys = key_block(qkv, coarse, far, group, 0, half)
            values = key_block(qkv, coarse, far, group, 1, half)
            weights = prob[group, half, :, :]
            score_grad = weights.astype(FLOAT) * (dot(values, grads, NT) - dots[group, half, 0:1, :])
            score_grad = score_grad.astype(BRAIN)
            grad_q[own, columns] = (gather_heads(dot(score_grad, keys, TN)) * 0.125).astype(BRAIN)
            for part, block in enumerate((dot(score_grad, queries), dot(weights, grads))):
                to = slice(part * WIDTH + half * HALF, part * WIDTH + (half + 1) * HALF)
                grad_kv[own, to] = block[0:GROUP]
                start = GROUP
                for level, (at, size) in enumerate(group_rows(group)):
                    piece = block[start : start + size]
                    start += size
                    if level < 2 or group % (1 << (level - 1)) == 0:
                        grad_coarse[at : at + size, to] = piece
                    else:
                        grad_coarse[at : at + size, to] += piece


def add_projected(stream, source, weight, bias, target):
    for column in range(0, WIDTH, 256):
        columns = slice(column, column + 256)
        total = dot(source[...], weight[:, columns])
        target[:, columns] = (stream[:, columns].astype(FLOAT) + total + bias[:, columns]).astype(
            BRAIN
        )


def feed_hidden(normed, weight, bias, hidden, slope):
    scale, cubic = 0.7978845608, 0.7978845608 * 0.044715
    for start in range(0, TOKENS, 256):
        rows = slice(start, start + 256)
        for column in range(0, FF, 256):
            columns = slice(column, column + 256)
            pre = dot(normed[rows, :], weight[:, columns]) + bias[:, columns]
            square = pre * pre
            share = 0.5 * jnp.tanh(pre * (scale + cubic * square)) + 0.5
            value = pre * share
            hidden[rows, columns] = value.astype(BRAIN)
            slope[rows, columns] = (
                share + value * ((1.0 - share) * (2 * scale + 6 * cubic * square))
            ).astype(BRAIN)


def projected_grad(qkv_grad, grad_kv, grad_coarse, grad_far, live):
    for tile in range(TILES):
        rows = slice(tile * TILE, (tile + 1) * TILE)
        matrix = pool_matrix(tile, live, True)
        share = inverse(counts(tile, live, TILE))
        for column in range(0, 2 * WIDTH, TILE):
            columns = slice(column, column + TILE)
            spans = jnp.concatenate(
                [grad_coarse[tile * TILE : tile * TILE + LEVEL_AT[4], columns],
                 grad_far[8 * tile : 8 * tile + 8, columns], jnp.zeros((8, TILE), FLOAT)], axis=0)
            total = grad_kv[rows, columns] + dot(matrix, (spans * share).astype(BRAIN))
            qkv_grad[rows, WIDTH + column : WIDTH + column + TILE] = total.astype(BRAIN)


def fetch(source, target, sem):
    copy = pltpu.make_async_copy(source, target, sem)
    copy.start()
    return copy


def reversed_bits(value, bits):
    return sum(((value >> k) & 1) << (bits - 1 - k) for k in range(bits))


def axes_of(order, bits):
    known = [axis for axis in order if axis == "x" or axis < bits]
    return known + [bit for bit in range(bits) if bit not in known]


def block_index(info, owner_core, rel_x, shard, bits, orders):
    index = []
    for order in orders:
        total = 0
        for axis in axes_of(order, bits):
            rel = rel_x if axis == "x" else ((shard >> axis) & 1) ^ ((info[5] >> axis) & 1)
            total = total * 2 + rel
        index.append(total)
    return jnp.where(owner_core == 0, index[0], index[1])


def pair_columns(ref, section, rel_core, width):
    both = []
    for rel_x in range(2):
        quarter = section ^ (2 * rel_x + rel_core)
        both.append(ref[:, pl.ds(pl.multiple_of(quarter * width, 128), width)])
    return jnp.concatenate(both, axis=1)


def feed_weight_grads(info, orders, rel_core, normed, pre_grad, hidden, grad, up, down, shards):
    bits = shards.bit_length() - 1
    section = info[4]
    owner = (section & 1) ^ rel_core
    rows = WIDTH // shards
    wide = FF // shards
    where = [[block_index(info, owner, rel_x, shard, bits, orders) for shard in range(shards)] for rel_x in range(2)]
    for rel_x in range(2):
        quarter = section ^ (2 * rel_x + rel_core)
        for part in range(2):
            at = pl.multiple_of(quarter * 512 + 256 * part, 256)
            block = dot(normed[...], pre_grad[:, pl.ds(at, 256)], TN).astype(BRAIN)
            for shard in range(shards):
                up[where[rel_x][shard], :, 256 * part : 256 * part + 256] = block[shard * rows : (shard + 1) * rows]
    some_grad = pair_columns(grad, section, rel_core, 128)
    for start in range(0, FF, 256):
        block = dot(hidden[:, start : start + 256], some_grad, TN).astype(BRAIN)
        for at in range(0, 256, rows):
            shard, part = (start + at) // wide, (start + at) % wide // rows
            for rel_x in range(2):
                down[where[rel_x][shard], :, 128 * part : 128 * part + 128] = block[
                    at : at + rows, 128 * rel_x : 128 * rel_x + 128]


def attend_weight_grads(info, orders, rel_core, normed, qkv_grad, att, grad, first, second, shards):
    bits = shards.bit_length() - 1
    section = info[4]
    owner = (section & 1) ^ rel_core
    rows = WIDTH // shards
    left = dot(normed[...], pair_columns(qkv_grad, section, rel_core, 384), TN).astype(BRAIN)
    right = dot(att[...], pair_columns(grad, section, rel_core, 128), TN).astype(BRAIN)
    for rel_x in range(2):
        for shard in range(shards):
            where = block_index(info, owner, rel_x, shard, bits, orders)
            mine = slice(shard * rows, (shard + 1) * rows)
            first[where, :, :] = left[mine, 384 * rel_x : 384 * rel_x + 256]
            second[where, :, 0:128] = left[mine, 384 * rel_x + 256 : 384 * rel_x + 384]
            second[where, :, 128:256] = right[mine, 128 * rel_x : 128 * rel_x + 128]


ANY = pl.BlockSpec(memory_space=pl.ANY)
VMEM = pl.BlockSpec(memory_space=pltpu.VMEM)
SMEM = pl.BlockSpec(memory_space=pltpu.SMEM)


def shape(dims, dtype=BRAIN):
    return jax.ShapeDtypeStruct(dims, dtype)


def vmem(dims, dtype=BRAIN):
    return pltpu.VMEM(dims, dtype)


def facts(ids, lengths, shards):
    section, dp = ids[0], ids[1]
    seq, half = section >> 1, section & 1
    length = lengths[seq]

    def inside(value):
        return jnp.minimum(jnp.maximum(value, 0), TOKENS)

    reverse = reversed_bits(dp, shards.bit_length() - 1)
    return seq, half, inside(length - half * TOKENS), inside(length - (1 - half) * TOKENS), section, dp, reverse


class Line:
    def __init__(self):
        self.known, self.last, self.pinned = None, None, []

    def pin(self, *arrays):
        self.pinned += arrays

    def call(self, body, outs, args, scratch, us, name, limit=16, out_specs=None, aliases=None):
        known = [] if self.known is None else [pltpu.with_memory_space_constraint(self.known, pltpu.SMEM)]
        first = len(known)
        count = first + len(args)
        after = there(*([] if self.last is None else [self.last]), *self.pinned)
        self.pinned = []

        def kernel(*refs):
            info = [refs[0][k] for k in range(7)] if known else None
            body(info, *refs[first:count], *refs[count + len(after) :])

        result = pl.pallas_call(
            kernel,
            out_shape=outs,
            in_specs=[SMEM] * first + [spec for spec, _ in args + after],
            out_specs=out_specs or [VMEM] * len(outs),
            scratch_shapes=scratch,
            input_output_aliases={first + k: v for k, v in (aliases or {}).items()},
            compiler_params=pltpu.CompilerParams(vmem_limit_bytes=limit * MIB),
            cost_estimate=pl.CostEstimate(flops=int(us * COST), bytes_accessed=1024, transcendentals=0),
            name=name,
        )(*known, *[array for _, array in args + after])
        if out_specs is None:
            self.last = result[-1]
        return result


def first_kernel(shards, _info, ids, lengths_in, inputs, hag, hab, hob, hfg, hfb, hub, hdb, hwp, hwo, hwu, hwd,
                 ag, ab, ob, fg, fb, ub, db, wp, wo, wu, wd,
                 qkv, coarse, far, prob, att, mine, mid, hidden, slope, out, qkv_next, coarse_next, info_out, pooled,
                 other, normed, bias, lengths, sems):
    seq, half = ids[0] >> 1, ids[0] & 1
    get_lengths = fetch(lengths_in, lengths, sems.at[17])
    get_mine = fetch(inputs.at[seq, pl.ds(half * TOKENS, TOKENS)], mine, sems.at[0])
    small = [fetch(source, target, sems.at[2 + k]) for k, (source, target) in enumerate(
        ((hag, ag), (hab, ab), (hob, ob), (hfg, fg), (hfb, fb), (hub, ub), (hdb, db)))]
    get_wp = fetch(hwp.at[0], wp.at[0], sems.at[9])
    get_other = fetch(inputs.at[seq, pl.ds((1 - half) * TOKENS, TOKENS)], other, sems.at[1])
    large = [fetch(source.at[0], target.at[0], sems.at[10 + k]) for k, (source, target) in enumerate(
        ((hwo, wo), (hwu, wu), (hwd, wd)))]
    later = [fetch(source.at[1], target.at[1], sems.at[13 + k]) for k, (source, target) in enumerate(
        ((hwp, wp), (hwo, wo), (hwu, wu), (hwd, wd)))]
    get_lengths.wait()
    info = facts(ids, lengths, shards)
    for k, value in enumerate(info):
        info_out[k] = value
    live, other_live = info[2], info[3]
    key_bias(live, other_live, bias)
    for copy in small:
        copy.wait()
    get_mine.wait()
    norm_into(mine, ag[0:1, :], ab[0:1, :], normed)
    get_wp.wait()
    project(normed, wp.at[0], qkv, 0, 3 * WIDTH)
    get_other.wait()
    norm_into(other, ag[0:1, :], ab[0:1, :], normed)
    project_far(normed, wp.at[0], other_live, far)
    pool_keys(qkv, live, coarse, pooled)
    hier_forward(qkv, coarse, far, bias, prob, att, live)
    large[0].wait()
    add_projected(mine, att, wo.at[0], ob[0:1, :], mid)
    norm_into(mid, fg[0:1, :], fb[0:1, :], normed)
    large[1].wait()
    feed_hidden(normed, wu.at[0], ub[0:1, :], hidden, slope)
    large[2].wait()
    add_projected(mid, hidden, wd.at[0], db[0:1, :], out)
    norm_into(out, ag[1:2, :], ab[1:2, :], normed)
    later[0].wait()
    project(normed, wp.at[1], qkv_next, 0, 3 * WIDTH)
    pool_keys(qkv_next, live, coarse_next, pooled)
    for copy in later[1:]:
        copy.wait()


def second_kernel(info, cotangent, qkv, coarse, far, stream, ob, fg, fb, ub, wo, wu,
                  prob, att, mid, normed, hidden, slope, grad, bias, sem):
    live, other_live = info[2], info[3]
    get_grad = fetch(cotangent.at[info[0], pl.ds(pl.multiple_of(info[1] * TOKENS, TOKENS), TOKENS)], grad, sem)
    key_bias(live, other_live, bias)
    hier_forward(qkv, coarse, far, bias, prob, att, live)
    add_projected(stream, att, wo.at[1], ob[1:2, :], mid)
    norm_into(mid, fg[1:2, :], fb[1:2, :], normed)
    feed_hidden(normed, wu.at[1], ub[1:2, :], hidden, slope)
    get_grad.wait()


def feed_back_send(layer, shards, take_norm, info, grad, hidden, slope, wd, *refs):
    if take_norm:
        stream, gain, shift, pre_grad, sums, send_up, send_down, normed = refs
        norm_into(stream, gain[layer : layer + 1, :], shift[layer : layer + 1, :], normed)
    else:
        normed, pre_grad, sums, send_up, send_down = refs
    for column in range(0, FF, 256):
        columns = slice(column, column + 256)
        back = dot(grad[...], wd[layer, columns, :], NT) * slope[:, columns].astype(FLOAT)
        back = back.astype(BRAIN)
        pre_grad[:, columns] = back
        sums[3 + column // 512 : 4 + column // 512, column % 512 : column % 512 + 256] = jnp.sum(
            back.astype(FLOAT), axis=0, keepdims=True
        )
    feed_weight_grads(info, FEED_ORDERS[layer], 1, normed, pre_grad, hidden, grad, send_up, send_down, shards)
    sums[0:2, :] = jnp.zeros((2, WIDTH), FLOAT)
    sums[2:3, :] = jnp.sum(grad[...].astype(FLOAT), axis=0, keepdims=True)
    sums[7:8, :] = jnp.zeros((1, WIDTH), FLOAT)


def feed_back_keep(layer, shards, info, grad, normed, pre_grad, hidden, stream, gain, wu, sums_in, wo, qkv, far, prob, att,
                   target, sums, keep_up, keep_down, grad_out, dots, grad_far, norm_grad):
    feed_weight_grads(info, FEED_ORDERS[layer], 0, normed, pre_grad, hidden, grad, keep_up, keep_down, shards)
    for column in range(0, WIDTH, 256):
        norm_grad[:, column : column + 256] = dot(pre_grad[...], wu[layer, column : column + 256, :], NT)
    sums[...] = sums_in[...]
    norm_back(stream, gain[layer : layer + 1, :], norm_grad, grad, target, sums.at[0:1, :], sums.at[1:2, :])
    for column in range(0, WIDTH, 256):
        back = dot(target[...], wo[layer, column : column + 256, :], NT)
        back = back * (iota((TOKENS, 256), 0) < info[2]).astype(FLOAT)
        grad_out[:, column : column + 256] = back.astype(BRAIN)
    far_backward(qkv, far, prob, att, grad_out, grad_far, dots)


def split_pieces(rows, section, own, far, near):
    targets = {0: own, 2: far}
    for k in range(4):
        piece = rows[:, pl.ds(pl.multiple_of((section ^ k) * 128, 128), 128)]
        if k % 2 == 0:
            targets[k][...] = piece
        else:
            near[k // 2, :, :] = piece


def last_output(layer, info, mid, hidden, wd, db, own, far, near, final):
    for column in range(0, WIDTH, 256):
        columns = slice(column, column + 256)
        total = dot(hidden[...], wd[layer, :, columns])
        final[:, columns] = (mid[:, columns].astype(FLOAT) + total + db[layer : layer + 1, columns]).astype(BRAIN)
    split_pieces(final, info[4], own, far, near)


def attend_back(info, qkv, coarse, far, prob, grad_out, dots, grad_q, grad_kv, grad_coarse):
    hier_backward(qkv, coarse, far, prob, grad_out, dots, grad_q, grad_kv, grad_coarse)


def project_back(layer, shards, info, grad, stream, att, grad_q, grad_kv, grad_coarse, grad_far, gain, shift,
                 qkv_grad, send, send_more, keep, keep_more, normed):
    norm_into(stream, gain[layer : layer + 1, :], shift[layer : layer + 1, :], normed)
    qkv_grad[:, 0:WIDTH] = grad_q[...]
    projected_grad(qkv_grad, grad_kv, grad_coarse, grad_far, info[2])
    attend_weight_grads(info, ATTEND_ORDERS[layer], 1, normed, qkv_grad, att, grad, send, send_more, shards)
    attend_weight_grads(info, ATTEND_ORDERS[layer], 0, normed, qkv_grad, att, grad, keep, keep_more, shards)


def project_back_norm(layer, last, info, grad, stream, qkv_grad, gain, wp, *refs):
    section = info[4]
    refs = list(refs)
    if last:
        earlier = refs[:3]
        del refs[:3]
        own, far, near, small, norm_grad, target, sums = refs
    else:
        mid, hidden, wd, db, target, sums, own, far, near, norm_grad, final = refs
        last_output(layer, info, mid, hidden, wd, db, own, far, near, final)
    for column in range(0, WIDTH, 256):
        norm_grad[:, column : column + 256] = dot(qkv_grad[...], wp[layer, column : column + 256, :], NT)
    norm_back(stream, gain[layer : layer + 1, :], norm_grad, grad, target, sums.at[0:1, :], sums.at[1:2, :])
    if last:
        split_pieces(target, section, own, far, near)
    sums[2:3, :] = jnp.sum(grad[...].astype(FLOAT), axis=0, keepdims=True)
    sums[3:8, :] = jnp.zeros((5, WIDTH), FLOAT)
    if last:
        feed_one, attend_one, feed_zero = earlier
        for k, sublayer in enumerate((sums, feed_zero, attend_one, feed_one)):
            up = feed_zero if k < 2 else feed_one
            small[k, 0:3, :] = sublayer[0:3, :]
            small[k, 3:5, :] = up[3 + k % 2 * 2 : 5 + k % 2 * 2, :]
            small[k, 5:, :] = jnp.zeros((11, WIDTH), FLOAT)


def beside(pairs):
    row = column = 0
    for mine, came in zip(pairs[::2], pairs[1::2]):
        rows, columns = mine.shape[1:]
        yield mine, came, slice(row, row + rows), slice(column, column + columns)
        column = (column + columns) % WIDTH
        row += rows if column == 0 else 0


def add_halves(info, *refs):
    *pairs, give, kept = refs
    half = give.shape[0]

    def body(k, carry):
        for mine, came, rows, columns in beside(pairs):
            give[k, rows, columns] = mine[half + k] + came[half + k]
            kept[k, rows, columns] = mine[k] + came[k]
        return carry

    lax.fori_loop(0, half, body, 0)


def add_last(info, *refs):
    *pairs, total = refs
    for mine, came, rows, columns in beside(pairs):
        total[rows, columns] = mine[0] + came[0]


def add_first(x_bits, info, *refs):
    *pairs, small, small_came, give, kept = refs
    half, height = give.shape[0], give.shape[1] - small.shape[1]
    core = info[4] & 1

    def body(k, carry):
        for target, block in ((give, half + k), (kept, k)):
            for mine, came, rows, columns in beside(pairs):
                target[k, rows, columns] = mine[block] + came[block]
            rel_x = (block >> jnp.where(core == 0, x_bits[0], x_bits[1])) & 1
            quarter = info[4] ^ (2 * rel_x)
            target[k, height:, :] = (small[quarter] + small_came[quarter]).astype(BRAIN)
        return carry

    lax.fori_loop(0, half, body, 0)


def place_shares(layer, shards, section, pieces, outs, stages, sems):
    up, down, proj, back = stages
    rows = WIDTH // shards
    for k in range(4):
        owner = section ^ k
        piece = pieces[k]
        up[:, pl.ds(pl.multiple_of(owner * 512, 512), 512)] = piece[0:rows, :].astype(FLOAT)
        for part in range(FF // WIDTH):
            down[part * rows : (part + 1) * rows, pl.ds(pl.multiple_of(owner * 128, 128), 128)] = piece[
                rows : 2 * rows, 128 * part : 128 * part + 128].astype(FLOAT)
        proj[:, pl.ds(pl.multiple_of(owner * 384, 128), 384)] = piece[2 * rows : 3 * rows, 0:384].astype(FLOAT)
        back[:, pl.ds(pl.multiple_of(owner * 128, 128), 128)] = piece[2 * rows : 3 * rows, 384:].astype(FLOAT)
    return [fetch(stage, out.at[layer], sems.at[k]) for k, (stage, out) in enumerate(zip(stages, outs))]


def finish_tokens(info, own, near, across, target, done, sems):
    section = info[4]
    copies = []
    for k, piece in enumerate((own, near.at[0], across.at[0], across.at[1])):
        owner = section ^ k
        to = target.at[owner >> 1, pl.ds(pl.multiple_of((owner & 1) * TOKENS, TOKENS), TOKENS)]
        copies.append(fetch(piece, to, sems.at[k]))
    done[...] = jnp.zeros((8, 128), FLOAT)
    for copy in copies:
        copy.wait()


def finish_one(shards, info, own, near, across, beyond, up, down, proj, back, *scratch):
    section, sems = info[4], scratch[-1]
    copies = place_shares(1, shards, section, (own, near, across, beyond), (up, down, proj, back), scratch[:4], sems)
    for copy in copies:
        copy.wait()


def finish_zero(shards, info, own, near, across, beyond, _up, _down, _proj, _back,
                up, down, proj, back, gain_a, bias_a, bias_o, gain_f, bias_f, bias_u, bias_d, *scratch):
    section, dp, small, sems = info[4], info[5], scratch[-2], scratch[-1]
    pieces = (own, near, across, beyond)
    copies = place_shares(0, shards, section, pieces, (up, down, proj, back), scratch[:4], sems)
    width = WIDTH // shards
    for k in range(4):
        small[section ^ k, :, :] = pieces[k][3 * width :, :].astype(FLOAT)
    total = jnp.concatenate([small[k, 0:8, :] for k in range(4)], axis=0)

    def taken(start, columns):
        pick = (iota((WIDTH, columns), 0) == start + iota((WIDTH, columns), 1)).astype(FLOAT)
        return lax.dot_general(total, pick, NN, precision=lax.Precision.HIGHEST, preferred_element_type=FLOAT)

    part = taken(dp * width, width)
    for layer in range(2):
        attend, feed = 16 * layer, 16 * layer + 8
        for start, outs in ((attend, (gain_a, bias_a, bias_o)), (feed, (gain_f, bias_f, bias_d))):
            for k, out in enumerate(outs):
                out[layer : layer + 1, :] = part[start + k : start + k + 1]
    wide = FF // shards
    per_row = WIDTH // wide
    part = taken(dp % per_row * wide, wide)
    for layer in range(2):
        row = part[16 * layer + 3 : 16 * layer + 4]
        for k in range(1, 4):
            at = 16 * layer + 8 * (k // 2) + 3 + k % 2
            row = jnp.where(dp // per_row == k, part[at : at + 1], row)
        bias_u[layer : layer + 1, :] = row
    for copy in copies:
        copy.wait()


def swap(block, partner):
    sections = lax.axis_size("section")
    pairs = []
    for dp in range(lax.axis_size("dp")):
        for section in range(sections):
            to_dp, to_section = partner(dp, section)
            pairs.append((dp * sections + section, to_dp * sections + to_section))
    return lax.ppermute(block, ("dp", "section"), pairs)


def over_section(block, bits):
    return swap(block, lambda dp, section: (dp, section ^ bits))


def there(*arrays):
    return [(VMEM, pltpu.with_memory_space_constraint(array, pltpu.VMEM)) for array in arrays]


def in_hbm(*arrays):
    return [(ANY, pltpu.with_memory_space_constraint(array, pltpu.HBM)) for array in arrays]


class Reduction:
    def __init__(self, line, name, orders, *send):
        self.line, self.name = line, name
        self.bits = lax.axis_size("dp").bit_length() - 1
        self.orders = [axes_of(order, self.bits) for order in orders]
        self.came = [over_section(part, 1) for part in send]
        self.done = 0

    def partner(self, dp, section):
        axis = self.orders[section & 1][self.done]
        return (dp, section ^ 2) if axis == "x" else (dp ^ (1 << axis), section)

    def keep(self, *blocks):
        self.mine = list(blocks)

    def height(self, other):
        arrays = self.mine + (other.mine if other is not None else [])
        return sum(array.shape[1] * array.shape[2] for array in arrays) // WIDTH

    def pairs(self):
        return [pair for mine, came in zip(self.mine, self.came) for pair in there(mine, came)]

    def step(self, other=None, small=None):
        pairs = self.pairs() + (other.pairs() if other is not None else [])
        dims = [self.mine[0].shape[0] // 2, self.height(other), WIDTH]
        body = add_halves
        if small is not None:
            body = functools.partial(add_first, [self.bits - order.index("x") for order in self.orders])
            pairs += there(small, over_section(small, 1))
            dims[1] += small.shape[1]
        give, mine = self.line.call(body, [vmem(dims)] * 2, pairs, [], 0.2, self.name + str(self.done))
        self.mine, self.came = [mine], [swap(give, self.partner)]
        self.done += 1

    def last(self, other=None):
        while self.done <= self.bits:
            self.step(other)
            other = None
        pairs = self.pairs() + (other.pairs() if other is not None else [])
        rows = self.height(other)
        (total,) = self.line.call(add_last, [vmem((rows, WIDTH))], pairs, [], 0.1, self.name + "_last")
        return total


def over_all_sections(share):
    across = over_section(share, 2)
    return share, over_section(share, 1), across, over_section(across, 1)


def exchange_near(own, far, near):
    came = over_section(near, 1)
    return own, came, jnp.concatenate([far[None], came[1:]], axis=0)


def finish_rows(line, own, near, across, name):
    outs = [shape((2, 2 * TOKENS, 128)), vmem((8, 128), FLOAT)]
    target, line.last = line.call(
        finish_tokens, outs, [(ANY, array) for array in (own, near, across)],
        [pltpu.SemaphoreType.DMA((4,))], 1.2, name, out_specs=[ANY, VMEM],
    )
    return target


def local(inputs, lengths, ag, ab, wp, wo, ob, fg, fb, wu, ub, wd, db, cotangent):
    shards = lax.axis_size("dp")
    ids = jnp.stack([lax.axis_index("section"), lax.axis_index("dp")]).astype(jnp.int32)
    line = Line()

    rows, wide, tall = vmem((TOKENS, WIDTH)), vmem((TOKENS, FF)), vmem((TOKENS, 3 * WIDTH))
    rows_float, double_float = vmem((TOKENS, WIDTH), FLOAT), vmem((TOKENS, 2 * WIDTH), FLOAT)
    coarse_shape, far_shape = vmem((TOKENS, 2 * WIDTH)), vmem((16, 2 * WIDTH))
    prob_shape = vmem((GROUPS, 2, KEYS, QROWS))
    bias_shape = vmem((TOKENS + 16, 128), FLOAT)
    sums_shape = vmem((8, WIDTH), FLOAT)
    piece, two_pieces = vmem((TOKENS, 128)), vmem((2, TOKENS, 128))
    params = (ag, ab, ob, fg, fb, ub, db, wp, wo, wu, wd)
    (ag, ab, ob, fg, fb, ub, db, wp, wo, wu, wd,
     qkv0, coarse0, far0, prob0, att0, stream0, mid0, hidden0, slope0, stream1, qkv1, coarse1, info, pooled) = line.call(
        functools.partial(first_kernel, shards),
        [vmem(array.shape, array.dtype) for array in params]
        + [tall, coarse_shape, far_shape, prob_shape, rows, rows, rows, wide, wide, rows, tall, coarse_shape,
           pltpu.SMEM((8,), jnp.int32), far_shape],
        [(SMEM, ids)] + in_hbm(lengths, inputs, *params),
        [rows, rows, bias_shape, pltpu.SMEM((2,), jnp.int32), pltpu.SemaphoreType.DMA((18,))],
        13.5, "layer_zero_forward", out_specs=[VMEM] * 23 + [SMEM, VMEM],
    )
    line.known, line.last = info, pooled
    far1 = over_section(pooled, 1)
    prob1, att1, mid1, normed1, hidden1, slope1, grad_last = line.call(
        second_kernel, [prob_shape, rows, rows, rows, wide, wide, rows],
        in_hbm(cotangent) + there(qkv1, coarse1, far1, stream1, ob, fg, fb, ub, wo, wu),
        [bias_shape, pltpu.SemaphoreType.DMA],
        6.8, "layer_one_forward",
    )

    blocks = vmem((2 * shards, WIDTH // shards, WIDTH))

    dots_shape = vmem((GROUPS, 2, 8, QROWS), FLOAT)
    far_float = vmem((16, 2 * WIDTH), FLOAT)

    pre_grad, sums_f1, send_up, send_down = line.call(
        functools.partial(feed_back_send, 1, shards, False), [wide, sums_shape, blocks, blocks],
        there(grad_last, hidden1, slope1, wd, normed1), [], 3.2, "feed_back_send_1",
    )
    feed_one = Reduction(line, "feed_one_", FEED_ORDERS[1], send_up, send_down)
    grad3, sums_f1, keep_up, keep_down, grad_out, dots, grad_far = line.call(
        functools.partial(feed_back_keep, 1, shards),
        [rows, sums_shape, blocks, blocks, rows, dots_shape, far_float],
        there(grad_last, normed1, pre_grad, hidden1, mid1, fg, wu, sums_f1, wo, qkv1, far1, prob1, att1), [rows_float],
        5.5, "feed_back_keep_1",
    )
    grad_far = over_section(grad_far, 1)
    feed_one.keep(keep_up, keep_down)
    feed_one.step()
    grad_q, grad_kv, grad_coarse = line.call(
        attend_back, [rows, double_float, double_float],
        there(qkv1, coarse1, far1, prob1, grad_out, dots), [], 4.3, "attend_back_1",
    )
    qkv_grad, *both = line.call(
        functools.partial(project_back, 1, shards), [tall] + [vmem((2 * shards, WIDTH // shards, WIDTH // 2))] * 4,
        there(grad3, stream1, att1, grad_q, grad_kv, grad_coarse, grad_far, ag, ab), [rows], 3.4, "project_back_1",
    )
    attend_one = Reduction(line, "attend_one_", ATTEND_ORDERS[1], *both[:2])
    attend_one.keep(*both[2:])
    grad2, sums_a1, *out_pieces = line.call(
        functools.partial(project_back_norm, 1, False), [rows, sums_shape, piece, piece, two_pieces],
        there(grad3, stream1, qkv_grad, ag, wp, mid1, hidden1, wd, db), [rows_float, rows], 3.0, "project_back_norm_1",
    )
    out_own, out_near, out_give = exchange_near(*out_pieces)
    out_across = over_section(out_give, 2)
    pre_grad, sums_f0, send_up, send_down, normed = line.call(
        functools.partial(feed_back_send, 0, shards, True), [wide, sums_shape, blocks, blocks, rows],
        there(grad2, hidden0, slope0, wd, mid0, fg, fb), [], 3.7, "feed_back_send_0",
    )
    feed_zero = Reduction(line, "feed_zero_", FEED_ORDERS[0], send_up, send_down)
    line.pin(out_near)
    feed_one.step()
    attend_one.step()
    grad1, sums_f0, keep_up, keep_down, grad_out, dots, grad_far = line.call(
        functools.partial(feed_back_keep, 0, shards),
        [rows, sums_shape, blocks, blocks, rows, dots_shape, far_float],
        there(grad2, normed, pre_grad, hidden0, mid0, fg, wu, sums_f0, wo, qkv0, far0, prob0, att0), [rows_float],
        5.5, "feed_back_keep_0",
    )
    grad_far = over_section(grad_far, 1)
    feed_zero.keep(keep_up, keep_down)
    line.pin(out_across)
    feed_zero.step()
    grad_q, grad_kv, grad_coarse = line.call(
        attend_back, [rows, double_float, double_float],
        there(qkv0, coarse0, far0, prob0, grad_out, dots), [], 4.3, "attend_back_0",
    )
    attend_one.step()
    line.pin(*feed_one.came)
    qkv_grad, *both = line.call(
        functools.partial(project_back, 0, shards), [tall] + [vmem((2 * shards, WIDTH // shards, WIDTH // 2))] * 4,
        there(grad1, stream0, att0, grad_q, grad_kv, grad_coarse, grad_far, ag, ab), [rows], 3.4, "project_back_0",
    )
    attend_zero = Reduction(line, "attend_zero_", ATTEND_ORDERS[0], *both[:2])
    attend_zero.keep(*both[2:])
    line.pin(*attend_one.came)
    *grad_pieces, small = line.call(
        functools.partial(project_back_norm, 0, True), [piece, piece, two_pieces, vmem((4, 16, WIDTH), FLOAT)],
        there(grad1, stream0, qkv_grad, ag, wp, sums_f1, sums_a1, sums_f0), [rows_float, rows, sums_shape], 2.3,
        "project_back_norm_0",
    )
    grad_own, grad_near, grad_give = exchange_near(*grad_pieces)
    attend_zero.step(small=small)
    feed_one.step(attend_one)
    feed_zero.step()
    line.pin(grad_near)
    attend_zero.step()
    feed_zero.step()
    feed_one.step()
    attend_zero.step()
    grad_across = over_section(grad_give, 2)
    line.pin(grad_across)
    feed_zero.step(attend_zero)
    outputs = finish_rows(line, out_own, out_near, out_across, "finish_outputs")
    input_grad = finish_rows(line, grad_own, grad_near, grad_across, "finish_input_grad")
    share_one = feed_one.last()
    share_zero = feed_zero.last()

    weight_grads = [
        shape((2, WIDTH // shards, FF), FLOAT), shape((2, FF // shards, WIDTH), FLOAT),
        shape((2, WIDTH // shards, 3 * WIDTH), FLOAT), shape((2, WIDTH // shards, WIDTH), FLOAT),
    ]
    stages = [vmem(out.shape[1:], FLOAT) for out in weight_grads]
    stages += [vmem((4, 16, WIDTH), FLOAT), pltpu.SemaphoreType.DMA((4,))]
    weight_first = line.call(
        functools.partial(finish_one, shards), weight_grads, there(*over_all_sections(share_one)),
        stages, 1.9, "finish_one", out_specs=[ANY] * 4,
    )
    vector = shape((2, WIDTH // shards), FLOAT)
    vectors = [vector] * 5 + [shape((2, FF // shards), FLOAT), vector]
    finished = line.call(
        functools.partial(finish_zero, shards), weight_grads + vectors,
        there(*over_all_sections(share_zero)) + [(ANY, array) for array in weight_first],
        stages, 3.0, "finish_zero", out_specs=[ANY] * 4 + [VMEM] * 7, aliases={4 + k: k for k in range(4)},
    )
    up_grad, down_grad, proj_grad, back_grad, gain_a, bias_a, bias_o, gain_f, bias_f, bias_u, bias_d = finished
    return (outputs, input_grad, gain_a, bias_a, proj_grad, back_grad, bias_o, gain_f, bias_f, up_grad, bias_u,
            down_grad, bias_d)


def solution(mesh):
    batch = P("dp", None, None)
    split = P("dp", None, "section")
    vector, matrix = P(None, "dp"), P(None, "dp", None)
    return jax.shard_map(
        local,
        mesh=mesh,
        in_specs=(batch, P("dp")) + (P(),) * 11 + (batch,),
        out_specs=(split, split, vector, vector, matrix, matrix, vector, vector, vector, matrix, vector, matrix, vector),
        check_vma=False,
    )
```

```python
import functools

import jax
import jax.numpy as jnp
from jax import lax
from jax.experimental import pallas as pl
from jax.experimental.pallas import tpu as pltpu
from jax.sharding import PartitionSpec as P

FLOAT = jnp.float32
BRAIN = jnp.bfloat16
NORM_EPS = 1e-05
MASK_FILL = -1000000000.0
WIDTH = 512
TOKENS = 512
FF = 2048
GROUP = 64
GROUPS = TOKENS // GROUP
LEVELS = 5
KEYS = GROUP + 32 + 16 * (LEVELS - 1)
HALF = 256
QROWS = 4 * GROUP
TILE = 256
TILES = TOKENS // TILE
LEVEL_AT = (0, 128, 192, 224, 240)
USED = 248
MIB = 1024 * 1024
FEED_ORDERS = ((("x", 1, 0, 2), (1, 0, "x", 2)), (("x", 0, 1, 2), (0, 1, 2, "x")))
ATTEND_ORDERS = ((("x", 0, 1, 2), (0, "x", 1, 2)), (("x", 0, 1, 2), (1, 0, 2, "x")))
COST = 1 * 10**9

NN = (((1,), (0,)), ((), ()))
NT = (((1,), (1,)), ((), ()))
TN = (((0,), (0,)), ((), ()))


def dot(left, right, dims=NN):
    return lax.dot_general(left, right, dims, preferred_element_type=FLOAT)


def iota(shape, dim):
    return lax.broadcasted_iota(jnp.int32, shape, dim)


def normalise(rows):
    mean = jnp.mean(rows, axis=-1, keepdims=True)
    centred = rows - mean
    scale = lax.rsqrt(jnp.mean(centred * centred, axis=-1, keepdims=True) + NORM_EPS)
    return centred * scale, scale


def norm_into(source, gain, bias, target):
    for start in range(0, TOKENS, 64):
        rows = slice(start, start + 64)
        unit, _ = normalise(source[rows, :].astype(FLOAT))
        target[rows, :] = (unit * gain + bias).astype(BRAIN)


def norm_back(source, gain, grad_ref, through_ref, target, gain_out, bias_out):
    gain_sum = jnp.zeros((1, WIDTH), FLOAT)
    bias_sum = jnp.zeros((1, WIDTH), FLOAT)
    for start in range(0, TOKENS, 64):
        rows = slice(start, start + 64)
        unit, scale = normalise(source[rows, :].astype(FLOAT))
        grad = grad_ref[rows, :]
        gain_sum = gain_sum + jnp.sum(grad * unit, axis=0, keepdims=True)
        bias_sum = bias_sum + jnp.sum(grad, axis=0, keepdims=True)
        inner = grad * gain
        inner_mean = jnp.mean(inner, axis=-1, keepdims=True)
        slope = jnp.mean(inner * unit, axis=-1, keepdims=True)
        back = scale * (inner - inner_mean - unit * slope)
        target[rows, :] = (through_ref[rows, :].astype(FLOAT) + back).astype(BRAIN)
    gain_out[...] = gain_sum
    bias_out[...] = bias_sum


def span_of(row):
    level = 1 + sum((row >= at).astype(jnp.int32) for at in LEVEL_AT[1:])
    at = sum(jnp.where(level == k + 1, at, 0) for k, at in enumerate(LEVEL_AT))
    return level, (row - at) << level


def pool_matrix(tile, live, transposed):
    dims = (TILE, TILE)
    row, token = iota(dims, int(transposed)), iota(dims, 1 - int(transposed))
    level, first = span_of(row)
    inside = (token >= first) & (token < first + (1 << level)) & (token < live - tile * TILE) & (row < USED)
    return inside.astype(FLOAT).astype(BRAIN)


def counts(tile, live, columns):
    level, first = span_of(iota((TILE, columns), 0))
    return jnp.clip(live - tile * TILE - first, 0, 1 << level)


def far_counts(live, columns):
    return jnp.clip(live - (iota((16, columns), 0) << LEVELS), 0, 1 << LEVELS)


def inverse(number):
    return 1.0 / jnp.maximum(number, 1).astype(FLOAT)


def log_count(number):
    return jnp.where(number > 0, jnp.log(jnp.maximum(number, 1).astype(FLOAT)), MASK_FILL)


def project(normed, weight, target, start, stop, target_start=None):
    shift = 0 if target_start is None else target_start - start
    for column in range(start, stop, 256):
        target[:, column + shift : column + shift + 256] = dot(
            normed[...], weight[:, column : column + 256]
        ).astype(BRAIN)


def pool_keys(qkv, live, coarse, pooled):
    matrix = [pool_matrix(tile, live, False) for tile in range(TILES)]
    share = [inverse(counts(tile, live, TILE)) for tile in range(TILES)]
    for column in range(0, 2 * WIDTH, TILE):
        columns = slice(column, column + TILE)
        last = []
        for tile in range(TILES):
            rows = slice(tile * TILE, (tile + 1) * TILE)
            mean = dot(matrix[tile], qkv[rows, WIDTH + column : WIDTH + column + TILE]) * share[tile]
            coarse[rows, columns] = mean.astype(BRAIN)
            last.append(mean[LEVEL_AT[4] : USED])
        pooled[:, columns] = jnp.concatenate(last, axis=0).astype(BRAIN)


def project_far(normed, weight, live, pooled):
    key, token = iota((16, TOKENS), 0), iota((16, TOKENS), 1)
    matrix = ((token >> LEVELS == key) & (token < live)).astype(FLOAT).astype(BRAIN)
    mean = dot(matrix, normed[...]) * inverse(far_counts(live, WIDTH))
    high = mean.astype(BRAIN)
    both = jnp.concatenate([high, (mean - high.astype(FLOAT)).astype(BRAIN)], axis=0)
    for column in range(0, 2 * WIDTH, 256):
        product = dot(both, weight[:, WIDTH + column : WIDTH + column + 256])
        pooled[:, column : column + 256] = (product[0:16] + product[16:32]).astype(BRAIN)


def key_bias(live, other_live, bias):
    for tile in range(TILES):
        bias[tile * TILE : (tile + 1) * TILE, :] = log_count(counts(tile, live, 128))
    bias[TOKENS:, :] = log_count(far_counts(other_live, 128))


def head_mask(value):
    dims = (QROWS, HALF)
    return jnp.where(iota(dims, 0) // GROUP == iota(dims, 1) // 64, value, 0.0).astype(BRAIN)


def pair_mask():
    own_key, own_query = iota((GROUP, QROWS), 0) // 32, iota((GROUP, QROWS), 1) % GROUP // 32
    near_key, near_query = iota((32, QROWS), 0) // 16, iota((32, QROWS), 1) % GROUP // 32
    own = jnp.where(own_key == own_query, 0.0, MASK_FILL)
    near = jnp.where(near_key != near_query, 0.0, MASK_FILL)
    return jnp.concatenate([own, near], axis=0)


def spread(rows, mask):
    return jnp.concatenate([rows] * 4, axis=0) * mask


def gather_heads(wide):
    left = iota((GROUP, 128), 1) < 64
    pairs = [wide[k * GROUP : (k + 1) * GROUP, k // 2 * 128 : k // 2 * 128 + 128] for k in range(4)]
    return jnp.concatenate([jnp.where(left, pairs[0], pairs[1]), jnp.where(left, pairs[2], pairs[3])], axis=1)


def group_rows(group):
    at = [(group // 4 * TILE + group % 4 * 32, 32)]
    for level in range(2, LEVELS):
        block = (group >> (level - 2)) ^ 1
        per_tile = TILE // (16 << level)
        at.append((block // per_tile * TILE + LEVEL_AT[level - 1] + block % per_tile * 16, 16))
    return at


def key_block(qkv, coarse, far, group, part, half):
    column = WIDTH * (part + 1) + HALF * half
    columns = slice(WIDTH * part + HALF * half, WIDTH * part + HALF * (half + 1))
    pieces = [qkv[group * GROUP : (group + 1) * GROUP, column : column + HALF]]
    pieces += [coarse[at : at + size, columns] for at, size in group_rows(group)]
    return jnp.concatenate(pieces + [far[:, columns]], axis=0)


def hier_forward(qkv, coarse, far, bias, prob, attended, exact, live):
    mask = head_mask(0.125)
    pairs = pair_mask()
    for group in range(GROUPS):
        rows = slice(group * GROUP, (group + 1) * GROUP)
        own_bias = jnp.where(group * GROUP + iota((GROUP, QROWS), 0) < live, 0.0, MASK_FILL)
        coarse_bias = jnp.concatenate(
            [bias[at : at + size, :] for at, size in group_rows(group)] + [bias[TOKENS:, :]], axis=0
        )
        added_bias = jnp.concatenate([own_bias, jnp.concatenate([coarse_bias] * 2, axis=1)], axis=0)
        added_bias = jnp.concatenate([added_bias[: GROUP + 32] + pairs, added_bias[GROUP + 32 :]], axis=0)
        query_live = (group * GROUP + iota((GROUP, HALF), 0) < live).astype(FLOAT)
        for half in range(2):
            columns = slice(half * HALF, (half + 1) * HALF)
            queries = spread(qkv[rows, columns], mask)
            scores = dot(key_block(qkv, coarse, far, group, 0, half), queries, NT) + added_bias
            weights = jnp.exp(scores - jnp.max(scores, axis=0, keepdims=True))
            weights = weights * (1.0 / jnp.sum(weights, axis=0, keepdims=True))
            weights = weights.astype(BRAIN)
            prob[group, half, :, :] = weights
            output = dot(weights, key_block(qkv, coarse, far, group, 1, half), TN)
            output = gather_heads(output) * query_live
            exact[rows, columns] = output
            attended[rows, columns] = output.astype(BRAIN)


def far_backward(qkv, far, prob, exact, grad_out, grad_far, dots):
    weights = []
    for half in range(2):
        for head in range(4):
            parts = [prob[g, half, KEYS - 16 :, head * 64 : head * 64 + 64] for g in range(GROUPS)]
            weights.append(jnp.concatenate(parts, axis=1))
    weights = jnp.concatenate(weights, axis=0)
    dims = (128, WIDTH)
    mask = jnp.where(iota(dims, 0) // 16 == iota(dims, 1) // 64, 1.0, 0.0).astype(BRAIN)
    values = jnp.concatenate([far[:, WIDTH:]] * 8, axis=0) * mask
    both = exact[...] * grad_out[...].astype(FLOAT)
    high = both.astype(BRAIN)
    total = dot(mask, high, NT) + dot(mask, (both - high.astype(FLOAT)).astype(BRAIN), NT)
    score_grad = (weights.astype(FLOAT) * (dot(values, grad_out[...], NT) - total)).astype(BRAIN)
    left = iota((16, 128), 1) < 64
    for part, wide in enumerate((dot(score_grad, qkv[:, 0:WIDTH]) * 0.125, dot(weights, grad_out[...]))):
        for pair in range(4):
            block = wide[32 * pair : 32 * pair + 32, 128 * pair : 128 * pair + 128]
            to = part * WIDTH + 128 * pair
            grad_far[:, to : to + 128] = jnp.where(left, block[0:16], block[16:32])
    for group in range(GROUPS):
        for half in range(2):
            rows = [half * 64 + head * 16 for head in range(4)]
            dots[group, half, 0:1, :] = jnp.concatenate(
                [total[row : row + 1, group * GROUP : (group + 1) * GROUP] for row in rows], axis=1)


def hier_backward(qkv, coarse, far, prob, grad_out, dots, grad_q, grad_kv, grad_coarse):
    mask_q, mask_o = head_mask(0.125), head_mask(1.0)
    for group in range(GROUPS):
        own = slice(group * GROUP, (group + 1) * GROUP)
        for half in range(2):
            columns = slice(half * HALF, (half + 1) * HALF)
            queries = spread(qkv[own, columns], mask_q)
            grads = spread(grad_out[own, columns], mask_o)
            keys = key_block(qkv, coarse, far, group, 0, half)
            values = key_block(qkv, coarse, far, group, 1, half)
            weights = prob[group, half, :, :]
            score_grad = weights.astype(FLOAT) * (dot(values, grads, NT) - dots[group, half, 0:1, :])
            score_grad = score_grad.astype(BRAIN)
            grad_q[own, columns] = (gather_heads(dot(score_grad, keys, TN)) * 0.125).astype(BRAIN)
            for part, block in enumerate((dot(score_grad, queries), dot(weights, grads))):
                to = slice(part * WIDTH + half * HALF, part * WIDTH + (half + 1) * HALF)
                grad_kv[own, to] = block[0:GROUP]
                start = GROUP
                for level, (at, size) in enumerate(group_rows(group)):
                    piece = block[start : start + size]
                    start += size
                    if level < 2 or group % (1 << (level - 1)) == 0:
                        grad_coarse[at : at + size, to] = piece
                    else:
                        grad_coarse[at : at + size, to] += piece


def add_projected(stream, source, weight, bias, target):
    for column in range(0, WIDTH, 256):
        columns = slice(column, column + 256)
        total = dot(source[...], weight[:, columns])
        target[:, columns] = (stream[:, columns].astype(FLOAT) + total + bias[:, columns]).astype(
            BRAIN
        )


def feed_hidden(normed, weight, bias, hidden, slope):
    scale, cubic = 0.7978845608, 0.7978845608 * 0.044715
    for start in range(0, TOKENS, 256):
        rows = slice(start, start + 256)
        for column in range(0, FF, 256):
            columns = slice(column, column + 256)
            pre = dot(normed[rows, :], weight[:, columns]) + bias[:, columns]
            square = pre * pre
            share = 0.5 * jnp.tanh(pre * (scale + cubic * square)) + 0.5
            value = pre * share
            hidden[rows, columns] = value.astype(BRAIN)
            slope[rows, columns] = (
                share + value * ((1.0 - share) * (2 * scale + 6 * cubic * square))
            ).astype(BRAIN)


def feed_through(normed, stream, w_up, up_bias, w_down, down_bias, hidden, slope, target, total):
    scale, cubic = 0.7978845608, 0.7978845608 * 0.044715
    for start in range(0, TOKENS, 256):
        rows = slice(start, start + 256)
        for column in range(0, FF, 256):
            columns = slice(column, column + 256)
            pre = dot(normed[rows, :], w_up[:, columns]) + up_bias[:, columns]
            square = pre * pre
            share = 0.5 * jnp.tanh(pre * (scale + cubic * square)) + 0.5
            value = pre * share
            value_low = value.astype(BRAIN)
            hidden[rows, columns] = value_low
            slope[rows, columns] = (
                share + value * ((1.0 - share) * (2 * scale + 6 * cubic * square))
            ).astype(BRAIN)
            part = dot(value_low, w_down[columns, :])
            if column == 0:
                total[rows, :] = part
            else:
                total[rows, :] += part
        target[rows, :] = (stream[rows, :].astype(FLOAT) + total[rows, :] + down_bias).astype(BRAIN)


def projected_grad(qkv_grad, grad_kv, grad_coarse, grad_far, live):
    for tile in range(TILES):
        rows = slice(tile * TILE, (tile + 1) * TILE)
        matrix = pool_matrix(tile, live, True)
        share = inverse(counts(tile, live, TILE))
        for column in range(0, 2 * WIDTH, TILE):
            columns = slice(column, column + TILE)
            spans = jnp.concatenate(
                [grad_coarse[tile * TILE : tile * TILE + LEVEL_AT[4], columns],
                 grad_far[8 * tile : 8 * tile + 8, columns], jnp.zeros((8, TILE), FLOAT)], axis=0)
            total = grad_kv[rows, columns] + dot(matrix, (spans * share).astype(BRAIN))
            qkv_grad[rows, WIDTH + column : WIDTH + column + TILE] = total.astype(BRAIN)


def fetch(source, target, sem):
    copy = pltpu.make_async_copy(source, target, sem)
    copy.start()
    return copy


def reversed_bits(value, bits):
    return sum(((value >> k) & 1) << (bits - 1 - k) for k in range(bits))


def axes_of(order, bits):
    known = [axis for axis in order if axis == "x" or axis < bits]
    return known + [bit for bit in range(bits) if bit not in known]


def block_index(info, owner_core, rel_x, shard, bits, orders):
    index = []
    for order in orders:
        total = 0
        for axis in axes_of(order, bits):
            rel = rel_x if axis == "x" else ((shard >> axis) & 1) ^ ((info[5] >> axis) & 1)
            total = total * 2 + rel
        index.append(total)
    return jnp.where(owner_core == 0, index[0], index[1])


def pair_columns(ref, section, rel_core, width):
    both = []
    for rel_x in range(2):
        quarter = section ^ (2 * rel_x + rel_core)
        both.append(ref[:, pl.ds(pl.multiple_of(quarter * width, 128), width)])
    return jnp.concatenate(both, axis=1)


def feed_weight_grads(info, orders, rel_core, normed, pre_grad, hidden, grad, up, down, shards):
    bits = shards.bit_length() - 1
    section = info[4]
    owner = (section & 1) ^ rel_core
    rows = WIDTH // shards
    wide = FF // shards
    where = [[block_index(info, owner, rel_x, shard, bits, orders) for shard in range(shards)] for rel_x in range(2)]
    for rel_x in range(2):
        quarter = section ^ (2 * rel_x + rel_core)
        for part in range(2):
            at = pl.multiple_of(quarter * 512 + 256 * part, 256)
            block = dot(normed[...], pre_grad[:, pl.ds(at, 256)], TN).astype(BRAIN)
            for shard in range(shards):
                up[where[rel_x][shard], :, 256 * part : 256 * part + 256] = block[shard * rows : (shard + 1) * rows]
    some_grad = pair_columns(grad, section, rel_core, 128)
    for start in range(0, FF, 256):
        block = dot(hidden[:, start : start + 256], some_grad, TN).astype(BRAIN)
        for at in range(0, 256, rows):
            shard, part = (start + at) // wide, (start + at) % wide // rows
            for rel_x in range(2):
                down[where[rel_x][shard], :, 128 * part : 128 * part + 128] = block[
                    at : at + rows, 128 * rel_x : 128 * rel_x + 128]


def attend_weight_grads(info, orders, rel_core, normed, qkv_grad, att, grad, first, second, shards):
    bits = shards.bit_length() - 1
    section = info[4]
    owner = (section & 1) ^ rel_core
    rows = WIDTH // shards
    left = dot(normed[...], pair_columns(qkv_grad, section, rel_core, 384), TN).astype(BRAIN)
    right = dot(att[...], pair_columns(grad, section, rel_core, 128), TN).astype(BRAIN)
    for rel_x in range(2):
        for shard in range(shards):
            where = block_index(info, owner, rel_x, shard, bits, orders)
            mine = slice(shard * rows, (shard + 1) * rows)
            first[where, :, :] = left[mine, 384 * rel_x : 384 * rel_x + 256]
            second[where, :, 0:128] = left[mine, 384 * rel_x + 256 : 384 * rel_x + 384]
            second[where, :, 128:256] = right[mine, 128 * rel_x : 128 * rel_x + 128]


ANY = pl.BlockSpec(memory_space=pl.ANY)
VMEM = pl.BlockSpec(memory_space=pltpu.VMEM)
SMEM = pl.BlockSpec(memory_space=pltpu.SMEM)


def shape(dims, dtype=BRAIN):
    return jax.ShapeDtypeStruct(dims, dtype)


def vmem(dims, dtype=BRAIN):
    return pltpu.VMEM(dims, dtype)


def facts(ids, lengths, shards):
    section, dp = ids[0], ids[1]
    seq, half = section >> 1, section & 1
    length = lengths[seq]

    def inside(value):
        return jnp.minimum(jnp.maximum(value, 0), TOKENS)

    reverse = reversed_bits(dp, shards.bit_length() - 1)
    return seq, half, inside(length - half * TOKENS), inside(length - (1 - half) * TOKENS), section, dp, reverse


class Line:
    def __init__(self):
        self.known, self.last, self.pinned = None, None, []

    def pin(self, *arrays):
        self.pinned += arrays

    def call(self, body, outs, args, scratch, us, name, limit=16, out_specs=None, aliases=None):
        known = [] if self.known is None else [pltpu.with_memory_space_constraint(self.known, pltpu.SMEM)]
        first = len(known)
        count = first + len(args)
        after = there(*([] if self.last is None else [self.last]), *self.pinned)
        self.pinned = []

        def kernel(*refs):
            info = [refs[0][k] for k in range(7)] if known else None
            body(info, *refs[first:count], *refs[count + len(after) :])

        result = pl.pallas_call(
            kernel,
            out_shape=outs,
            in_specs=[SMEM] * first + [spec for spec, _ in args + after],
            out_specs=out_specs or [VMEM] * len(outs),
            scratch_shapes=scratch,
            input_output_aliases={first + k: v for k, v in (aliases or {}).items()},
            compiler_params=pltpu.CompilerParams(vmem_limit_bytes=limit * MIB),
            cost_estimate=pl.CostEstimate(flops=int(us * COST), bytes_accessed=1024, transcendentals=0),
            name=name,
        )(*known, *[array for _, array in args + after])
        if out_specs is None:
            self.last = result[-1]
        return result


def first_kernel(shards, _info, ids, lengths_in, inputs, hag, hab, hob, hfg, hfb, hub, hdb, hwp, hwo, hwu, hwd,
                 ag, ab, ob, fg, fb, ub, db, wp, wo, wu, wd,
                 qkv, coarse, far, prob, att, exact, mine, mid, hidden, slope, out, qkv_next, coarse_next, info_out, pooled,
                 other, normed, bias, total, lengths, sems):
    seq, half = ids[0] >> 1, ids[0] & 1
    get_lengths = fetch(lengths_in, lengths, sems.at[17])
    get_mine = fetch(inputs.at[seq, pl.ds(half * TOKENS, TOKENS)], mine, sems.at[0])
    small = [fetch(source, target, sems.at[2 + k]) for k, (source, target) in enumerate(
        ((hag, ag), (hab, ab), (hob, ob), (hfg, fg), (hfb, fb), (hub, ub), (hdb, db)))]
    get_wp = fetch(hwp.at[0], wp.at[0], sems.at[9])
    get_other = fetch(inputs.at[seq, pl.ds((1 - half) * TOKENS, TOKENS)], other, sems.at[1])
    large = [fetch(source.at[0], target.at[0], sems.at[10 + k]) for k, (source, target) in enumerate(
        ((hwo, wo), (hwu, wu), (hwd, wd)))]
    later = [fetch(source.at[1], target.at[1], sems.at[13 + k]) for k, (source, target) in enumerate(
        ((hwp, wp), (hwo, wo), (hwu, wu), (hwd, wd)))]
    get_lengths.wait()
    info = facts(ids, lengths, shards)
    for k, value in enumerate(info):
        info_out[k] = value
    live, other_live = info[2], info[3]
    key_bias(live, other_live, bias)
    for copy in small:
        copy.wait()
    get_mine.wait()
    norm_into(mine, ag[0:1, :], ab[0:1, :], normed)
    get_wp.wait()
    project(normed, wp.at[0], qkv, 0, 3 * WIDTH)
    get_other.wait()
    norm_into(other, ag[0:1, :], ab[0:1, :], normed)
    project_far(normed, wp.at[0], other_live, far)
    pool_keys(qkv, live, coarse, pooled)
    hier_forward(qkv, coarse, far, bias, prob, att, exact, live)
    large[0].wait()
    add_projected(mine, att, wo.at[0], ob[0:1, :], mid)
    norm_into(mid, fg[0:1, :], fb[0:1, :], normed)
    large[1].wait()
    large[2].wait()
    feed_through(normed, mid, wu.at[0], ub[0:1, :], wd.at[0], db[0:1, :], hidden, slope, out, total)
    norm_into(out, ag[1:2, :], ab[1:2, :], normed)
    later[0].wait()
    project(normed, wp.at[1], qkv_next, 0, 3 * WIDTH)
    pool_keys(qkv_next, live, coarse_next, pooled)
    for copy in later[1:]:
        copy.wait()


def second_kernel(info, cotangent, qkv, coarse, far, stream, ob, fg, fb, ub, wo, wu,
                  prob, att, exact, mid, normed, hidden, slope, grad, bias, sem):
    live, other_live = info[2], info[3]
    get_grad = fetch(cotangent.at[info[0], pl.ds(pl.multiple_of(info[1] * TOKENS, TOKENS), TOKENS)], grad, sem)
    key_bias(live, other_live, bias)
    hier_forward(qkv, coarse, far, bias, prob, att, exact, live)
    add_projected(stream, att, wo.at[1], ob[1:2, :], mid)
    norm_into(mid, fg[1:2, :], fb[1:2, :], normed)
    feed_hidden(normed, wu.at[1], ub[1:2, :], hidden, slope)
    get_grad.wait()


def feed_back_send(layer, shards, take_norm, info, grad, hidden, slope, wd, *refs):
    if take_norm:
        stream, gain, shift, pre_grad, sums, send_up, send_down, normed = refs
        norm_into(stream, gain[layer : layer + 1, :], shift[layer : layer + 1, :], normed)
    else:
        normed, pre_grad, sums, send_up, send_down = refs
    for column in range(0, FF, 256):
        columns = slice(column, column + 256)
        back = dot(grad[...], wd[layer, columns, :], NT) * slope[:, columns].astype(FLOAT)
        back = back.astype(BRAIN)
        pre_grad[:, columns] = back
        sums[3 + column // 512 : 4 + column // 512, column % 512 : column % 512 + 256] = jnp.sum(
            back.astype(FLOAT), axis=0, keepdims=True
        )
    feed_weight_grads(info, FEED_ORDERS[layer], 1, normed, pre_grad, hidden, grad, send_up, send_down, shards)
    sums[0:2, :] = jnp.zeros((2, WIDTH), FLOAT)
    sums[2:3, :] = jnp.sum(grad[...].astype(FLOAT), axis=0, keepdims=True)
    sums[7:8, :] = jnp.zeros((1, WIDTH), FLOAT)


def feed_back_keep(layer, shards, info, grad, normed, pre_grad, hidden, stream, gain, wu, sums_in, wo, qkv, far, prob, exact,
                   target, sums, keep_up, keep_down, grad_out, dots, grad_far, norm_grad):
    feed_weight_grads(info, FEED_ORDERS[layer], 0, normed, pre_grad, hidden, grad, keep_up, keep_down, shards)
    for column in range(0, WIDTH, 256):
        norm_grad[:, column : column + 256] = dot(pre_grad[...], wu[layer, column : column + 256, :], NT)
    sums[...] = sums_in[...]
    norm_back(stream, gain[layer : layer + 1, :], norm_grad, grad, target, sums.at[0:1, :], sums.at[1:2, :])
    for column in range(0, WIDTH, 256):
        back = dot(target[...], wo[layer, column : column + 256, :], NT)
        back = back * (iota((TOKENS, 256), 0) < info[2]).astype(FLOAT)
        grad_out[:, column : column + 256] = back.astype(BRAIN)
    far_backward(qkv, far, prob, exact, grad_out, grad_far, dots)


def split_pieces(rows, section, own, far, near):
    targets = {0: own, 2: far}
    for k in range(4):
        piece = rows[:, pl.ds(pl.multiple_of((section ^ k) * 128, 128), 128)]
        if k % 2 == 0:
            targets[k][...] = piece
        else:
            near[k // 2, :, :] = piece


def last_output(layer, info, mid, hidden, wd, db, own, far, near, final):
    for column in range(0, WIDTH, 256):
        columns = slice(column, column + 256)
        total = dot(hidden[...], wd[layer, :, columns])
        final[:, columns] = (mid[:, columns].astype(FLOAT) + total + db[layer : layer + 1, columns]).astype(BRAIN)
    split_pieces(final, info[4], own, far, near)


def attend_back(info, qkv, coarse, far, prob, grad_out, dots, grad_q, grad_kv, grad_coarse):
    hier_backward(qkv, coarse, far, prob, grad_out, dots, grad_q, grad_kv, grad_coarse)


def project_back(layer, shards, info, grad, stream, att, grad_q, grad_kv, grad_coarse, grad_far, gain, shift,
                 qkv_grad, send, send_more, keep, keep_more, normed):
    norm_into(stream, gain[layer : layer + 1, :], shift[layer : layer + 1, :], normed)
    qkv_grad[:, 0:WIDTH] = grad_q[...]
    projected_grad(qkv_grad, grad_kv, grad_coarse, grad_far, info[2])
    attend_weight_grads(info, ATTEND_ORDERS[layer], 1, normed, qkv_grad, att, grad, send, send_more, shards)
    attend_weight_grads(info, ATTEND_ORDERS[layer], 0, normed, qkv_grad, att, grad, keep, keep_more, shards)


def project_back_norm(layer, last, info, grad, stream, qkv_grad, gain, wp, *refs):
    section = info[4]
    refs = list(refs)
    if last:
        earlier = refs[:3]
        del refs[:3]
        own, far, near, small, norm_grad, target, sums = refs
    else:
        mid, hidden, wd, db, target, sums, own, far, near, norm_grad, final = refs
        last_output(layer, info, mid, hidden, wd, db, own, far, near, final)
    for column in range(0, WIDTH, 256):
        norm_grad[:, column : column + 256] = dot(qkv_grad[...], wp[layer, column : column + 256, :], NT)
    norm_back(stream, gain[layer : layer + 1, :], norm_grad, grad, target, sums.at[0:1, :], sums.at[1:2, :])
    if last:
        split_pieces(target, section, own, far, near)
    sums[2:3, :] = jnp.sum(grad[...].astype(FLOAT), axis=0, keepdims=True)
    sums[3:8, :] = jnp.zeros((5, WIDTH), FLOAT)
    if last:
        feed_one, attend_one, feed_zero = earlier
        for k, sublayer in enumerate((sums, feed_zero, attend_one, feed_one)):
            up = feed_zero if k < 2 else feed_one
            small[k, 0:3, :] = sublayer[0:3, :]
            small[k, 3:5, :] = up[3 + k % 2 * 2 : 5 + k % 2 * 2, :]
            small[k, 5:, :] = jnp.zeros((11, WIDTH), FLOAT)


def beside(pairs):
    row = column = 0
    for mine, came in zip(pairs[::2], pairs[1::2]):
        rows, columns = mine.shape[1:]
        yield mine, came, slice(row, row + rows), slice(column, column + columns)
        column = (column + columns) % WIDTH
        row += rows if column == 0 else 0


def add_halves(info, *refs):
    *pairs, give, kept = refs
    half = give.shape[0]

    def body(k, carry):
        for mine, came, rows, columns in beside(pairs):
            give[k, rows, columns] = mine[half + k] + came[half + k]
            kept[k, rows, columns] = mine[k] + came[k]
        return carry

    lax.fori_loop(0, half, body, 0)


def add_last(info, *refs):
    *pairs, total = refs
    for mine, came, rows, columns in beside(pairs):
        total[rows, columns] = mine[0] + came[0]


def add_first(x_bits, info, *refs):
    *pairs, small, small_came, give, kept = refs
    half, height = give.shape[0], give.shape[1] - small.shape[1]
    core = info[4] & 1

    def body(k, carry):
        for target, block in ((give, half + k), (kept, k)):
            for mine, came, rows, columns in beside(pairs):
                target[k, rows, columns] = mine[block] + came[block]
            rel_x = (block >> jnp.where(core == 0, x_bits[0], x_bits[1])) & 1
            quarter = info[4] ^ (2 * rel_x)
            target[k, height:, :] = (small[quarter] + small_came[quarter]).astype(BRAIN)
        return carry

    lax.fori_loop(0, half, body, 0)


def place_shares(layer, shards, section, pieces, outs, stages, sems):
    up, down, proj, back = stages
    rows = WIDTH // shards
    for k in range(4):
        owner = section ^ k
        piece = pieces[k]
        up[:, pl.ds(pl.multiple_of(owner * 512, 512), 512)] = piece[0:rows, :].astype(FLOAT)
        for part in range(FF // WIDTH):
            down[part * rows : (part + 1) * rows, pl.ds(pl.multiple_of(owner * 128, 128), 128)] = piece[
                rows : 2 * rows, 128 * part : 128 * part + 128].astype(FLOAT)
        proj[:, pl.ds(pl.multiple_of(owner * 384, 128), 384)] = piece[2 * rows : 3 * rows, 0:384].astype(FLOAT)
        back[:, pl.ds(pl.multiple_of(owner * 128, 128), 128)] = piece[2 * rows : 3 * rows, 384:].astype(FLOAT)
    return [fetch(stage, out.at[layer], sems.at[k]) for k, (stage, out) in enumerate(zip(stages, outs))]


def finish_tokens(info, own, near, across, target, done, sems):
    section = info[4]
    copies = []
    for k, piece in enumerate((own, near.at[0], across.at[0], across.at[1])):
        owner = section ^ k
        to = target.at[owner >> 1, pl.ds(pl.multiple_of((owner & 1) * TOKENS, TOKENS), TOKENS)]
        copies.append(fetch(piece, to, sems.at[k]))
    done[...] = jnp.zeros((8, 128), FLOAT)
    for copy in copies:
        copy.wait()


def finish_one(shards, info, own, near, across, beyond, up, down, proj, back, *scratch):
    section, sems = info[4], scratch[-1]
    copies = place_shares(1, shards, section, (own, near, across, beyond), (up, down, proj, back), scratch[:4], sems)
    for copy in copies:
        copy.wait()


def finish_zero(shards, info, own, near, across, beyond, _up, _down, _proj, _back,
                up, down, proj, back, gain_a, bias_a, bias_o, gain_f, bias_f, bias_u, bias_d, *scratch):
    section, dp, small, sems = info[4], info[5], scratch[-2], scratch[-1]
    pieces = (own, near, across, beyond)
    copies = place_shares(0, shards, section, pieces, (up, down, proj, back), scratch[:4], sems)
    width = WIDTH // shards
    for k in range(4):
        small[section ^ k, :, :] = pieces[k][3 * width :, :].astype(FLOAT)
    total = jnp.concatenate([small[k, 0:8, :] for k in range(4)], axis=0)

    def taken(start, columns):
        pick = (iota((WIDTH, columns), 0) == start + iota((WIDTH, columns), 1)).astype(FLOAT)
        return lax.dot_general(total, pick, NN, precision=lax.Precision.HIGHEST, preferred_element_type=FLOAT)

    part = taken(dp * width, width)
    for layer in range(2):
        attend, feed = 16 * layer, 16 * layer + 8
        for start, outs in ((attend, (gain_a, bias_a, bias_o)), (feed, (gain_f, bias_f, bias_d))):
            for k, out in enumerate(outs):
                out[layer : layer + 1, :] = part[start + k : start + k + 1]
    wide = FF // shards
    per_row = WIDTH // wide
    part = taken(dp % per_row * wide, wide)
    for layer in range(2):
        row = part[16 * layer + 3 : 16 * layer + 4]
        for k in range(1, 4):
            at = 16 * layer + 8 * (k // 2) + 3 + k % 2
            row = jnp.where(dp // per_row == k, part[at : at + 1], row)
        bias_u[layer : layer + 1, :] = row
    for copy in copies:
        copy.wait()


def swap(block, partner):
    sections = lax.axis_size("section")
    pairs = []
    for dp in range(lax.axis_size("dp")):
        for section in range(sections):
            to_dp, to_section = partner(dp, section)
            pairs.append((dp * sections + section, to_dp * sections + to_section))
    return lax.ppermute(block, ("dp", "section"), pairs)


def over_section(block, bits):
    return swap(block, lambda dp, section: (dp, section ^ bits))


def there(*arrays):
    return [(VMEM, pltpu.with_memory_space_constraint(array, pltpu.VMEM)) for array in arrays]


def in_hbm(*arrays):
    return [(ANY, pltpu.with_memory_space_constraint(array, pltpu.HBM)) for array in arrays]


class Reduction:
    def __init__(self, line, name, orders, *send):
        self.line, self.name = line, name
        self.bits = lax.axis_size("dp").bit_length() - 1
        self.orders = [axes_of(order, self.bits) for order in orders]
        self.came = [over_section(part, 1) for part in send]
        self.done = 0

    def partner(self, dp, section):
        axis = self.orders[section & 1][self.done]
        return (dp, section ^ 2) if axis == "x" else (dp ^ (1 << axis), section)

    def keep(self, *blocks):
        self.mine = list(blocks)

    def height(self, other):
        arrays = self.mine + (other.mine if other is not None else [])
        return sum(array.shape[1] * array.shape[2] for array in arrays) // WIDTH

    def pairs(self):
        return [pair for mine, came in zip(self.mine, self.came) for pair in there(mine, came)]

    def step(self, other=None, small=None):
        pairs = self.pairs() + (other.pairs() if other is not None else [])
        dims = [self.mine[0].shape[0] // 2, self.height(other), WIDTH]
        body = add_halves
        if small is not None:
            body = functools.partial(add_first, [self.bits - order.index("x") for order in self.orders])
            pairs += there(small, over_section(small, 1))
            dims[1] += small.shape[1]
        give, mine = self.line.call(body, [vmem(dims)] * 2, pairs, [], 0.2, self.name + str(self.done))
        self.mine, self.came = [mine], [swap(give, self.partner)]
        self.done += 1

    def last(self, other=None):
        while self.done <= self.bits:
            self.step(other)
            other = None
        pairs = self.pairs() + (other.pairs() if other is not None else [])
        rows = self.height(other)
        (total,) = self.line.call(add_last, [vmem((rows, WIDTH))], pairs, [], 0.1, self.name + "_last")
        return total


def over_all_sections(share):
    across = over_section(share, 2)
    return share, over_section(share, 1), across, over_section(across, 1)


def exchange_near(own, far, near):
    came = over_section(near, 1)
    return own, came, jnp.concatenate([far[None], came[1:]], axis=0)


def finish_rows(line, own, near, across, name):
    outs = [shape((2, 2 * TOKENS, 128)), vmem((8, 128), FLOAT)]
    target, line.last = line.call(
        finish_tokens, outs, [(ANY, array) for array in (own, near, across)],
        [pltpu.SemaphoreType.DMA((4,))], 1.2, name, out_specs=[ANY, VMEM],
    )
    return target


def local(inputs, lengths, ag, ab, wp, wo, ob, fg, fb, wu, ub, wd, db, cotangent):
    shards = lax.axis_size("dp")
    ids = jnp.stack([lax.axis_index("section"), lax.axis_index("dp")]).astype(jnp.int32)
    line = Line()

    rows, wide, tall = vmem((TOKENS, WIDTH)), vmem((TOKENS, FF)), vmem((TOKENS, 3 * WIDTH))
    rows_float, double_float = vmem((TOKENS, WIDTH), FLOAT), vmem((TOKENS, 2 * WIDTH), FLOAT)
    coarse_shape, far_shape = vmem((TOKENS, 2 * WIDTH)), vmem((16, 2 * WIDTH))
    prob_shape = vmem((GROUPS, 2, KEYS, QROWS))
    bias_shape = vmem((TOKENS + 16, 128), FLOAT)
    sums_shape = vmem((8, WIDTH), FLOAT)
    piece, two_pieces = vmem((TOKENS, 128)), vmem((2, TOKENS, 128))
    params = (ag, ab, ob, fg, fb, ub, db, wp, wo, wu, wd)
    (ag, ab, ob, fg, fb, ub, db, wp, wo, wu, wd,
     qkv0, coarse0, far0, prob0, att0, exact0, stream0, mid0, hidden0, slope0, stream1, qkv1, coarse1, info, pooled) = line.call(
        functools.partial(first_kernel, shards),
        [vmem(array.shape, array.dtype) for array in params]
        + [tall, coarse_shape, far_shape, prob_shape, rows, rows_float, rows, rows, wide, wide, rows, tall, coarse_shape,
           pltpu.SMEM((8,), jnp.int32), far_shape],
        [(SMEM, ids)] + in_hbm(lengths, inputs, *params),
        [rows, rows, bias_shape, rows_float, pltpu.SMEM((2,), jnp.int32), pltpu.SemaphoreType.DMA((18,))],
        13.5, "layer_zero_forward", out_specs=[VMEM] * 24 + [SMEM, VMEM],
    )
    line.known, line.last = info, pooled
    far1 = over_section(pooled, 1)
    prob1, att1, exact1, mid1, normed1, hidden1, slope1, grad_last = line.call(
        second_kernel, [prob_shape, rows, rows_float, rows, rows, wide, wide, rows],
        in_hbm(cotangent) + there(qkv1, coarse1, far1, stream1, ob, fg, fb, ub, wo, wu),
        [bias_shape, pltpu.SemaphoreType.DMA],
        6.8, "layer_one_forward",
    )

    blocks = vmem((2 * shards, WIDTH // shards, WIDTH))

    dots_shape = vmem((GROUPS, 2, 8, QROWS), FLOAT)
    far_float = vmem((16, 2 * WIDTH), FLOAT)

    pre_grad, sums_f1, send_up, send_down = line.call(
        functools.partial(feed_back_send, 1, shards, False), [wide, sums_shape, blocks, blocks],
        there(grad_last, hidden1, slope1, wd, normed1), [], 3.2, "feed_back_send_1",
    )
    feed_one = Reduction(line, "feed_one_", FEED_ORDERS[1], send_up, send_down)
    grad3, sums_f1, keep_up, keep_down, grad_out, dots, grad_far = line.call(
        functools.partial(feed_back_keep, 1, shards),
        [rows, sums_shape, blocks, blocks, rows, dots_shape, far_float],
        there(grad_last, normed1, pre_grad, hidden1, mid1, fg, wu, sums_f1, wo, qkv1, far1, prob1, exact1), [rows_float],
        5.5, "feed_back_keep_1",
    )
    grad_far = over_section(grad_far, 1)
    feed_one.keep(keep_up, keep_down)
    feed_one.step()
    grad_q, grad_kv, grad_coarse = line.call(
        attend_back, [rows, double_float, double_float],
        there(qkv1, coarse1, far1, prob1, grad_out, dots), [], 4.3, "attend_back_1",
    )
    qkv_grad, *both = line.call(
        functools.partial(project_back, 1, shards), [tall] + [vmem((2 * shards, WIDTH // shards, WIDTH // 2))] * 4,
        there(grad3, stream1, att1, grad_q, grad_kv, grad_coarse, grad_far, ag, ab), [rows], 3.4, "project_back_1",
    )
    attend_one = Reduction(line, "attend_one_", ATTEND_ORDERS[1], *both[:2])
    attend_one.keep(*both[2:])
    grad2, sums_a1, *out_pieces = line.call(
        functools.partial(project_back_norm, 1, False), [rows, sums_shape, piece, piece, two_pieces],
        there(grad3, stream1, qkv_grad, ag, wp, mid1, hidden1, wd, db), [rows_float, rows], 3.0, "project_back_norm_1",
    )
    out_own, out_near, out_give = exchange_near(*out_pieces)
    out_across = over_section(out_give, 2)
    pre_grad, sums_f0, send_up, send_down, normed = line.call(
        functools.partial(feed_back_send, 0, shards, True), [wide, sums_shape, blocks, blocks, rows],
        there(grad2, hidden0, slope0, wd, mid0, fg, fb), [], 3.7, "feed_back_send_0",
    )
    feed_zero = Reduction(line, "feed_zero_", FEED_ORDERS[0], send_up, send_down)
    line.pin(out_near)
    feed_one.step()
    attend_one.step()
    grad1, sums_f0, keep_up, keep_down, grad_out, dots, grad_far = line.call(
        functools.partial(feed_back_keep, 0, shards),
        [rows, sums_shape, blocks, blocks, rows, dots_shape, far_float],
        there(grad2, normed, pre_grad, hidden0, mid0, fg, wu, sums_f0, wo, qkv0, far0, prob0, exact0), [rows_float],
        5.5, "feed_back_keep_0",
    )
    grad_far = over_section(grad_far, 1)
    feed_zero.keep(keep_up, keep_down)
    line.pin(out_across)
    feed_zero.step()
    grad_q, grad_kv, grad_coarse = line.call(
        attend_back, [rows, double_float, double_float],
        there(qkv0, coarse0, far0, prob0, grad_out, dots), [], 4.3, "attend_back_0",
    )
    attend_one.step()
    line.pin(*feed_one.came)
    qkv_grad, *both = line.call(
        functools.partial(project_back, 0, shards), [tall] + [vmem((2 * shards, WIDTH // shards, WIDTH // 2))] * 4,
        there(grad1, stream0, att0, grad_q, grad_kv, grad_coarse, grad_far, ag, ab), [rows], 0.5, "project_back_0",
    )
    attend_zero = Reduction(line, "attend_zero_", ATTEND_ORDERS[0], *both[:2])
    attend_zero.keep(*both[2:])
    *grad_pieces, small = line.call(
        functools.partial(project_back_norm, 0, True), [piece, piece, two_pieces, vmem((4, 16, WIDTH), FLOAT)],
        there(grad1, stream0, qkv_grad, ag, wp, sums_f1, sums_a1, sums_f0), [rows_float, rows, sums_shape], 5.0,
        "project_back_norm_0",
    )
    grad_own, grad_near, grad_give = exchange_near(*grad_pieces)
    line.pin(*attend_one.came)
    attend_zero.step(small=small)
    feed_one.step(attend_one)
    feed_zero.step()
    line.pin(grad_near)
    attend_zero.step()
    feed_zero.step()
    feed_one.step()
    attend_zero.step()
    grad_across = over_section(grad_give, 2)
    line.pin(grad_across)
    feed_zero.step(attend_zero)
    outputs = finish_rows(line, out_own, out_near, out_across, "finish_outputs")
    input_grad = finish_rows(line, grad_own, grad_near, grad_across, "finish_input_grad")
    share_one = feed_one.last()
    share_zero = feed_zero.last()

    weight_grads = [
        shape((2, WIDTH // shards, FF), FLOAT), shape((2, FF // shards, WIDTH), FLOAT),
        shape((2, WIDTH // shards, 3 * WIDTH), FLOAT), shape((2, WIDTH // shards, WIDTH), FLOAT),
    ]
    stages = [vmem(out.shape[1:], FLOAT) for out in weight_grads]
    stages += [vmem((4, 16, WIDTH), FLOAT), pltpu.SemaphoreType.DMA((4,))]
    weight_first = line.call(
        functools.partial(finish_one, shards), weight_grads, there(*over_all_sections(share_one)),
        stages, 1.9, "finish_one", out_specs=[ANY] * 4,
    )
    vector = shape((2, WIDTH // shards), FLOAT)
    vectors = [vector] * 5 + [shape((2, FF // shards), FLOAT), vector]
    finished = line.call(
        functools.partial(finish_zero, shards), weight_grads + vectors,
        there(*over_all_sections(share_zero)) + [(ANY, array) for array in weight_first],
        stages, 3.0, "finish_zero", out_specs=[ANY] * 4 + [VMEM] * 7, aliases={4 + k: k for k in range(4)},
    )
    up_grad, down_grad, proj_grad, back_grad, gain_a, bias_a, bias_o, gain_f, bias_f, bias_u, bias_d = finished
    return (outputs, input_grad, gain_a, bias_a, proj_grad, back_grad, bias_o, gain_f, bias_f, up_grad, bias_u,
            down_grad, bias_d)


def solution(mesh):
    batch = P("dp", None, None)
    split = P("dp", None, "section")
    vector, matrix = P(None, "dp"), P(None, "dp", None)
    return jax.shard_map(
        local,
        mesh=mesh,
        in_specs=(batch, P("dp")) + (P(),) * 11 + (batch,),
        out_specs=(split, split, vector, vector, matrix, matrix, vector, vector, vector, matrix, vector, matrix, vector),
        check_vma=False,
    )
```

```python
import functools

import jax
import jax.numpy as jnp
from jax import lax
from jax.experimental import pallas as pl
from jax.experimental.pallas import tpu as pltpu
from jax.sharding import PartitionSpec as P

FLOAT = jnp.float32
BRAIN = jnp.bfloat16
NORM_EPS = 1e-05
MASK_FILL = -1000000000.0
WIDTH = 512
TOKENS = 512
FF = 2048
GROUP = 64
GROUPS = TOKENS // GROUP
LEVELS = 5
KEYS = GROUP + 32 + 16 * (LEVELS - 1)
HALF = 256
QROWS = 4 * GROUP
TILE = 256
TILES = TOKENS // TILE
LEVEL_AT = (0, 128, 192, 224, 240)
USED = 248
MIB = 1024 * 1024
FEED_ORDERS = ((("x", 1, 0, 2), (1, 0, "x", 2)), (("x", 0, 1, 2), (0, 1, 2, "x")))
ATTEND_ORDERS = ((("x", 0, 1, 2), (0, "x", 1, 2)), (("x", 0, 1, 2), (1, 0, 2, "x")))
COST = 1 * 10**9

NN = (((1,), (0,)), ((), ()))
NT = (((1,), (1,)), ((), ()))
TN = (((0,), (0,)), ((), ()))


def dot(left, right, dims=NN):
    return lax.dot_general(left, right, dims, preferred_element_type=FLOAT)


def iota(shape, dim):
    return lax.broadcasted_iota(jnp.int32, shape, dim)


def normalise(rows):
    mean = jnp.mean(rows, axis=-1, keepdims=True)
    centred = rows - mean
    scale = lax.rsqrt(jnp.mean(centred * centred, axis=-1, keepdims=True) + NORM_EPS)
    return centred * scale, scale


def norm_into(source, gain, bias, target):
    for start in range(0, TOKENS, 64):
        rows = slice(start, start + 64)
        unit, _ = normalise(source[rows, :].astype(FLOAT))
        target[rows, :] = (unit * gain + bias).astype(BRAIN)


def norm_back(source, gain, grad_ref, through_ref, target, gain_out, bias_out):
    gain_sum = jnp.zeros((1, WIDTH), FLOAT)
    bias_sum = jnp.zeros((1, WIDTH), FLOAT)
    for start in range(0, TOKENS, 64):
        rows = slice(start, start + 64)
        unit, scale = normalise(source[rows, :].astype(FLOAT))
        grad = grad_ref[rows, :]
        gain_sum = gain_sum + jnp.sum(grad * unit, axis=0, keepdims=True)
        bias_sum = bias_sum + jnp.sum(grad, axis=0, keepdims=True)
        inner = grad * gain
        inner_mean = jnp.mean(inner, axis=-1, keepdims=True)
        slope = jnp.mean(inner * unit, axis=-1, keepdims=True)
        back = scale * (inner - inner_mean - unit * slope)
        target[rows, :] = (through_ref[rows, :].astype(FLOAT) + back).astype(BRAIN)
    gain_out[...] = gain_sum
    bias_out[...] = bias_sum


def span_of(row):
    level = 1 + sum((row >= at).astype(jnp.int32) for at in LEVEL_AT[1:])
    at = sum(jnp.where(level == k + 1, at, 0) for k, at in enumerate(LEVEL_AT))
    return level, (row - at) << level


def pool_matrix(tile, live, transposed):
    dims = (TILE, TILE)
    row, token = iota(dims, int(transposed)), iota(dims, 1 - int(transposed))
    level, first = span_of(row)
    inside = (token >= first) & (token < first + (1 << level)) & (token < live - tile * TILE) & (row < USED)
    return inside.astype(FLOAT).astype(BRAIN)


def counts(tile, live, columns):
    level, first = span_of(iota((TILE, columns), 0))
    return jnp.clip(live - tile * TILE - first, 0, 1 << level)


def far_counts(live, columns):
    return jnp.clip(live - (iota((16, columns), 0) << LEVELS), 0, 1 << LEVELS)


def inverse(number):
    return 1.0 / jnp.maximum(number, 1).astype(FLOAT)


def log_count(number):
    return jnp.where(number > 0, jnp.log(jnp.maximum(number, 1).astype(FLOAT)), MASK_FILL)


def project(normed, weight, target, start, stop, target_start=None):
    shift = 0 if target_start is None else target_start - start
    for column in range(start, stop, 256):
        target[:, column + shift : column + shift + 256] = dot(
            normed[...], weight[:, column : column + 256]
        ).astype(BRAIN)


def pool_keys(qkv, live, coarse, pooled):
    matrix = [pool_matrix(tile, live, False) for tile in range(TILES)]
    share = [inverse(counts(tile, live, TILE)) for tile in range(TILES)]
    for column in range(0, 2 * WIDTH, TILE):
        columns = slice(column, column + TILE)
        last = []
        for tile in range(TILES):
            rows = slice(tile * TILE, (tile + 1) * TILE)
            mean = dot(matrix[tile], qkv[rows, WIDTH + column : WIDTH + column + TILE]) * share[tile]
            coarse[rows, columns] = mean.astype(BRAIN)
            last.append(mean[LEVEL_AT[4] : USED])
        pooled[:, columns] = jnp.concatenate(last, axis=0).astype(BRAIN)


def project_far(normed, weight, live, pooled):
    key, token = iota((16, TOKENS), 0), iota((16, TOKENS), 1)
    matrix = ((token >> LEVELS == key) & (token < live)).astype(FLOAT).astype(BRAIN)
    mean = dot(matrix, normed[...]) * inverse(far_counts(live, WIDTH))
    high = mean.astype(BRAIN)
    both = jnp.concatenate([high, (mean - high.astype(FLOAT)).astype(BRAIN)], axis=0)
    for column in range(0, 2 * WIDTH, 256):
        product = dot(both, weight[:, WIDTH + column : WIDTH + column + 256])
        pooled[:, column : column + 256] = (product[0:16] + product[16:32]).astype(BRAIN)


def key_bias(live, other_live, bias):
    for tile in range(TILES):
        bias[tile * TILE : (tile + 1) * TILE, :] = log_count(counts(tile, live, 128))
    bias[TOKENS:, :] = log_count(far_counts(other_live, 128))


def head_mask(value):
    dims = (QROWS, HALF)
    return jnp.where(iota(dims, 0) // GROUP == iota(dims, 1) // 64, value, 0.0).astype(BRAIN)


def pair_mask():
    own_key, own_query = iota((GROUP, QROWS), 0) // 32, iota((GROUP, QROWS), 1) % GROUP // 32
    near_key, near_query = iota((32, QROWS), 0) // 16, iota((32, QROWS), 1) % GROUP // 32
    own = jnp.where(own_key == own_query, 0.0, MASK_FILL)
    near = jnp.where(near_key != near_query, 0.0, MASK_FILL)
    return jnp.concatenate([own, near], axis=0)


def spread(rows, mask):
    return jnp.concatenate([rows] * 4, axis=0) * mask


def gather_heads(wide):
    left = iota((GROUP, 128), 1) < 64
    pairs = [wide[k * GROUP : (k + 1) * GROUP, k // 2 * 128 : k // 2 * 128 + 128] for k in range(4)]
    return jnp.concatenate([jnp.where(left, pairs[0], pairs[1]), jnp.where(left, pairs[2], pairs[3])], axis=1)


def group_rows(group):
    at = [(group // 4 * TILE + group % 4 * 32, 32)]
    for level in range(2, LEVELS):
        block = (group >> (level - 2)) ^ 1
        per_tile = TILE // (16 << level)
        at.append((block // per_tile * TILE + LEVEL_AT[level - 1] + block % per_tile * 16, 16))
    return at


def key_block(qkv, coarse, far, group, part, half):
    column = WIDTH * (part + 1) + HALF * half
    columns = slice(WIDTH * part + HALF * half, WIDTH * part + HALF * (half + 1))
    pieces = [qkv[group * GROUP : (group + 1) * GROUP, column : column + HALF]]
    pieces += [coarse[at : at + size, columns] for at, size in group_rows(group)]
    return jnp.concatenate(pieces + [far[:, columns]], axis=0)


def hier_forward(qkv, coarse, far, bias, prob, attended, exact, live):
    mask = head_mask(0.125)
    pairs = pair_mask()
    for group in range(GROUPS):
        rows = slice(group * GROUP, (group + 1) * GROUP)
        own_bias = jnp.where(group * GROUP + iota((GROUP, QROWS), 0) < live, 0.0, MASK_FILL)
        coarse_bias = jnp.concatenate(
            [bias[at : at + size, :] for at, size in group_rows(group)] + [bias[TOKENS:, :]], axis=0
        )
        added_bias = jnp.concatenate([own_bias, jnp.concatenate([coarse_bias] * 2, axis=1)], axis=0)
        added_bias = jnp.concatenate([added_bias[: GROUP + 32] + pairs, added_bias[GROUP + 32 :]], axis=0)
        query_live = (group * GROUP + iota((GROUP, HALF), 0) < live).astype(FLOAT)
        for half in range(2):
            columns = slice(half * HALF, (half + 1) * HALF)
            queries = spread(qkv[rows, columns], mask)
            scores = dot(key_block(qkv, coarse, far, group, 0, half), queries, NT) + added_bias
            weights = jnp.exp(scores - jnp.max(scores, axis=0, keepdims=True))
            weights = weights * (1.0 / jnp.sum(weights, axis=0, keepdims=True))
            weights = weights.astype(BRAIN)
            prob[group, half, :, :] = weights
            output = dot(weights, key_block(qkv, coarse, far, group, 1, half), TN)
            output = gather_heads(output) * query_live
            exact[rows, columns] = output
            attended[rows, columns] = output.astype(BRAIN)


def far_backward(qkv, far, prob, exact, grad_out, grad_far, dots):
    weights = []
    for half in range(2):
        for head in range(4):
            parts = [prob[g, half, KEYS - 16 :, head * 64 : head * 64 + 64] for g in range(GROUPS)]
            weights.append(jnp.concatenate(parts, axis=1))
    weights = jnp.concatenate(weights, axis=0)
    dims = (128, WIDTH)
    mask = jnp.where(iota(dims, 0) // 16 == iota(dims, 1) // 64, 1.0, 0.0).astype(BRAIN)
    values = jnp.concatenate([far[:, WIDTH:]] * 8, axis=0) * mask
    both = exact[...] * grad_out[...].astype(FLOAT)
    high = both.astype(BRAIN)
    total = dot(mask, high, NT) + dot(mask, (both - high.astype(FLOAT)).astype(BRAIN), NT)
    score_grad = (weights.astype(FLOAT) * (dot(values, grad_out[...], NT) - total)).astype(BRAIN)
    left = iota((16, 128), 1) < 64
    for part, wide in enumerate((dot(score_grad, qkv[:, 0:WIDTH]) * 0.125, dot(weights, grad_out[...]))):
        for pair in range(4):
            block = wide[32 * pair : 32 * pair + 32, 128 * pair : 128 * pair + 128]
            to = part * WIDTH + 128 * pair
            grad_far[:, to : to + 128] = jnp.where(left, block[0:16], block[16:32])
    for group in range(GROUPS):
        for half in range(2):
            rows = [half * 64 + head * 16 for head in range(4)]
            dots[group, half, 0:1, :] = jnp.concatenate(
                [total[row : row + 1, group * GROUP : (group + 1) * GROUP] for row in rows], axis=1)


def hier_backward(qkv, coarse, far, prob, grad_out, dots, grad_q, grad_kv, grad_coarse):
    mask_q, mask_o = head_mask(0.125), head_mask(1.0)
    for group in range(GROUPS):
        own = slice(group * GROUP, (group + 1) * GROUP)
        for half in range(2):
            columns = slice(half * HALF, (half + 1) * HALF)
            queries = spread(qkv[own, columns], mask_q)
            grads = spread(grad_out[own, columns], mask_o)
            keys = key_block(qkv, coarse, far, group, 0, half)
            values = key_block(qkv, coarse, far, group, 1, half)
            weights = prob[group, half, :, :]
            score_grad = weights.astype(FLOAT) * (dot(values, grads, NT) - dots[group, half, 0:1, :])
            score_grad = score_grad.astype(BRAIN)
            grad_q[own, columns] = (gather_heads(dot(score_grad, keys, TN)) * 0.125).astype(BRAIN)
            for part, block in enumerate((dot(score_grad, queries), dot(weights, grads))):
                to = slice(part * WIDTH + half * HALF, part * WIDTH + (half + 1) * HALF)
                grad_kv[own, to] = block[0:GROUP]
                start = GROUP
                for level, (at, size) in enumerate(group_rows(group)):
                    piece = block[start : start + size]
                    start += size
                    if level < 2 or group % (1 << (level - 1)) == 0:
                        grad_coarse[at : at + size, to] = piece
                    else:
                        grad_coarse[at : at + size, to] += piece


def add_projected(stream, source, weight, bias, target):
    for column in range(0, WIDTH, 256):
        columns = slice(column, column + 256)
        total = dot(source[...], weight[:, columns])
        target[:, columns] = (stream[:, columns].astype(FLOAT) + total + bias[:, columns]).astype(
            BRAIN
        )


def feed_hidden(normed, weight, bias, hidden, slope):
    scale, cubic = 0.7978845608, 0.7978845608 * 0.044715
    for start in range(0, TOKENS, 256):
        rows = slice(start, start + 256)
        for column in range(0, FF, 256):
            columns = slice(column, column + 256)
            pre = dot(normed[rows, :], weight[:, columns]) + bias[:, columns]
            square = pre * pre
            share = 0.5 * jnp.tanh(pre * (scale + cubic * square)) + 0.5
            value = pre * share
            hidden[rows, columns] = value.astype(BRAIN)
            slope[rows, columns] = (
                share + value * ((1.0 - share) * (2 * scale + 6 * cubic * square))
            ).astype(BRAIN)


def feed_through(normed, stream, w_up, up_bias, w_down, down_bias, hidden, slope, target, total):
    scale, cubic = 0.7978845608, 0.7978845608 * 0.044715
    for start in range(0, TOKENS, 256):
        rows = slice(start, start + 256)
        for column in range(0, FF, 256):
            columns = slice(column, column + 256)
            pre = dot(normed[rows, :], w_up[:, columns]) + up_bias[:, columns]
            square = pre * pre
            share = 0.5 * jnp.tanh(pre * (scale + cubic * square)) + 0.5
            value = pre * share
            value_low = value.astype(BRAIN)
            hidden[rows, columns] = value_low
            slope[rows, columns] = (
                share + value * ((1.0 - share) * (2 * scale + 6 * cubic * square))
            ).astype(BRAIN)
            part = dot(value_low, w_down[columns, :])
            if column == 0:
                total[rows, :] = part
            else:
                total[rows, :] += part
        target[rows, :] = (stream[rows, :].astype(FLOAT) + total[rows, :] + down_bias).astype(BRAIN)


def projected_grad(qkv_grad, grad_kv, grad_coarse, grad_far, live):
    for tile in range(TILES):
        rows = slice(tile * TILE, (tile + 1) * TILE)
        matrix = pool_matrix(tile, live, True)
        share = inverse(counts(tile, live, TILE))
        for column in range(0, 2 * WIDTH, TILE):
            columns = slice(column, column + TILE)
            spans = jnp.concatenate(
                [grad_coarse[tile * TILE : tile * TILE + LEVEL_AT[4], columns],
                 grad_far[8 * tile : 8 * tile + 8, columns], jnp.zeros((8, TILE), FLOAT)], axis=0)
            total = grad_kv[rows, columns] + dot(matrix, (spans * share).astype(BRAIN))
            qkv_grad[rows, WIDTH + column : WIDTH + column + TILE] = total.astype(BRAIN)


def fetch(source, target, sem):
    copy = pltpu.make_async_copy(source, target, sem)
    copy.start()
    return copy


def reversed_bits(value, bits):
    return sum(((value >> k) & 1) << (bits - 1 - k) for k in range(bits))


def axes_of(order, bits):
    known = [axis for axis in order if axis == "x" or axis < bits]
    return known + [bit for bit in range(bits) if bit not in known]


def block_index(info, owner_core, rel_x, shard, bits, orders):
    index = []
    for order in orders:
        total = 0
        for axis in axes_of(order, bits):
            rel = rel_x if axis == "x" else ((shard >> axis) & 1) ^ ((info[5] >> axis) & 1)
            total = total * 2 + rel
        index.append(total)
    return jnp.where(owner_core == 0, index[0], index[1])


def pair_columns(ref, section, rel_core, width):
    both = []
    for rel_x in range(2):
        quarter = section ^ (2 * rel_x + rel_core)
        both.append(ref[:, pl.ds(pl.multiple_of(quarter * width, 128), width)])
    return jnp.concatenate(both, axis=1)


def feed_weight_grads(info, orders, rel_core, normed, pre_grad, hidden, grad, up, down, shards):
    bits = shards.bit_length() - 1
    section = info[4]
    owner = (section & 1) ^ rel_core
    rows = WIDTH // shards
    wide = FF // shards
    where = [[block_index(info, owner, rel_x, shard, bits, orders) for shard in range(shards)] for rel_x in range(2)]
    for rel_x in range(2):
        quarter = section ^ (2 * rel_x + rel_core)
        for part in range(2):
            at = pl.multiple_of(quarter * 512 + 256 * part, 256)
            block = dot(normed[...], pre_grad[:, pl.ds(at, 256)], TN).astype(BRAIN)
            for shard in range(shards):
                up[where[rel_x][shard], :, 256 * part : 256 * part + 256] = block[shard * rows : (shard + 1) * rows]
    some_grad = pair_columns(grad, section, rel_core, 128)
    for start in range(0, FF, 256):
        block = dot(hidden[:, start : start + 256], some_grad, TN).astype(BRAIN)
        for at in range(0, 256, rows):
            shard, part = (start + at) // wide, (start + at) % wide // rows
            for rel_x in range(2):
                down[where[rel_x][shard], :, 128 * part : 128 * part + 128] = block[
                    at : at + rows, 128 * rel_x : 128 * rel_x + 128]


def attend_weight_grads(info, orders, rel_core, normed, qkv_grad, att, grad, first, second, shards):
    bits = shards.bit_length() - 1
    section = info[4]
    owner = (section & 1) ^ rel_core
    rows = WIDTH // shards
    left = dot(normed[...], pair_columns(qkv_grad, section, rel_core, 384), TN).astype(BRAIN)
    right = dot(att[...], pair_columns(grad, section, rel_core, 128), TN).astype(BRAIN)
    for rel_x in range(2):
        for shard in range(shards):
            where = block_index(info, owner, rel_x, shard, bits, orders)
            mine = slice(shard * rows, (shard + 1) * rows)
            first[where, :, :] = left[mine, 384 * rel_x : 384 * rel_x + 256]
            second[where, :, 0:128] = left[mine, 384 * rel_x + 256 : 384 * rel_x + 384]
            second[where, :, 128:256] = right[mine, 128 * rel_x : 128 * rel_x + 128]


ANY = pl.BlockSpec(memory_space=pl.ANY)
VMEM = pl.BlockSpec(memory_space=pltpu.VMEM)
SMEM = pl.BlockSpec(memory_space=pltpu.SMEM)


def shape(dims, dtype=BRAIN):
    return jax.ShapeDtypeStruct(dims, dtype)


def vmem(dims, dtype=BRAIN):
    return pltpu.VMEM(dims, dtype)


def facts(ids, lengths, shards):
    section, dp = ids[0], ids[1]
    seq, half = section >> 1, section & 1
    length = lengths[seq]

    def inside(value):
        return jnp.minimum(jnp.maximum(value, 0), TOKENS)

    reverse = reversed_bits(dp, shards.bit_length() - 1)
    return seq, half, inside(length - half * TOKENS), inside(length - (1 - half) * TOKENS), section, dp, reverse


class Line:
    def __init__(self):
        self.known, self.last, self.pinned = None, None, []

    def pin(self, *arrays):
        self.pinned += arrays

    def call(self, body, outs, args, scratch, us, name, limit=16, out_specs=None, aliases=None):
        known = [] if self.known is None else [pltpu.with_memory_space_constraint(self.known, pltpu.SMEM)]
        first = len(known)
        count = first + len(args)
        after = there(*([] if self.last is None else [self.last]), *self.pinned)
        self.pinned = []

        def kernel(*refs):
            info = [refs[0][k] for k in range(7)] if known else None
            body(info, *refs[first:count], *refs[count + len(after) :])

        result = pl.pallas_call(
            kernel,
            out_shape=outs,
            in_specs=[SMEM] * first + [spec for spec, _ in args + after],
            out_specs=out_specs or [VMEM] * len(outs),
            scratch_shapes=scratch,
            input_output_aliases={first + k: v for k, v in (aliases or {}).items()},
            compiler_params=pltpu.CompilerParams(vmem_limit_bytes=limit * MIB),
            cost_estimate=pl.CostEstimate(flops=int(us * COST), bytes_accessed=1024, transcendentals=0),
            name=name,
        )(*known, *[array for _, array in args + after])
        if out_specs is None:
            self.last = result[-1]
        return result


def first_kernel(shards, _info, ids, lengths_in, inputs, hag, hab, hob, hfg, hfb, hub, hdb, hwp, hwo, hwu, hwd,
                 ag, ab, ob, fg, fb, ub, db, wp, wo, wu, wd,
                 qkv, coarse, far, prob, att, exact, mine, mid, hidden, slope, out, qkv_next, coarse_next, info_out, pooled,
                 other, normed, bias, total, lengths, sems):
    seq, half = ids[0] >> 1, ids[0] & 1
    get_lengths = fetch(lengths_in, lengths, sems.at[17])
    get_mine = fetch(inputs.at[seq, pl.ds(half * TOKENS, TOKENS)], mine, sems.at[0])
    small = [fetch(source, target, sems.at[2 + k]) for k, (source, target) in enumerate(
        ((hag, ag), (hab, ab), (hob, ob), (hfg, fg), (hfb, fb), (hub, ub), (hdb, db)))]
    get_wp = fetch(hwp.at[0], wp.at[0], sems.at[9])
    get_other = fetch(inputs.at[seq, pl.ds((1 - half) * TOKENS, TOKENS)], other, sems.at[1])
    large = [fetch(source.at[0], target.at[0], sems.at[10 + k]) for k, (source, target) in enumerate(
        ((hwo, wo), (hwu, wu), (hwd, wd)))]
    later = [fetch(source.at[1], target.at[1], sems.at[13 + k]) for k, (source, target) in enumerate(
        ((hwp, wp), (hwo, wo), (hwu, wu), (hwd, wd)))]
    get_lengths.wait()
    info = facts(ids, lengths, shards)
    for k, value in enumerate(info):
        info_out[k] = value
    live, other_live = info[2], info[3]
    key_bias(live, other_live, bias)
    for copy in small:
        copy.wait()
    get_mine.wait()
    norm_into(mine, ag[0:1, :], ab[0:1, :], normed)
    get_wp.wait()
    project(normed, wp.at[0], qkv, 0, 3 * WIDTH)
    get_other.wait()
    norm_into(other, ag[0:1, :], ab[0:1, :], normed)
    project_far(normed, wp.at[0], other_live, far)
    pool_keys(qkv, live, coarse, pooled)
    hier_forward(qkv, coarse, far, bias, prob, att, exact, live)
    large[0].wait()
    add_projected(mine, att, wo.at[0], ob[0:1, :], mid)
    norm_into(mid, fg[0:1, :], fb[0:1, :], normed)
    large[1].wait()
    large[2].wait()
    feed_through(normed, mid, wu.at[0], ub[0:1, :], wd.at[0], db[0:1, :], hidden, slope, out, total)
    norm_into(out, ag[1:2, :], ab[1:2, :], normed)
    later[0].wait()
    project(normed, wp.at[1], qkv_next, 0, 3 * WIDTH)
    pool_keys(qkv_next, live, coarse_next, pooled)
    for copy in later[1:]:
        copy.wait()


def second_kernel(info, cotangent, qkv, coarse, far, stream, ob, fg, fb, ub, wo, wu,
                  prob, att, exact, mid, normed, hidden, slope, grad, bias, sem):
    live, other_live = info[2], info[3]
    get_grad = fetch(cotangent.at[info[0], pl.ds(pl.multiple_of(info[1] * TOKENS, TOKENS), TOKENS)], grad, sem)
    key_bias(live, other_live, bias)
    hier_forward(qkv, coarse, far, bias, prob, att, exact, live)
    add_projected(stream, att, wo.at[1], ob[1:2, :], mid)
    norm_into(mid, fg[1:2, :], fb[1:2, :], normed)
    feed_hidden(normed, wu.at[1], ub[1:2, :], hidden, slope)
    get_grad.wait()


def feed_back_send(layer, shards, take_norm, info, grad, hidden, slope, wd, *refs):
    if take_norm:
        stream, gain, shift, pre_grad, sums, send_up, send_down, normed = refs
        norm_into(stream, gain[layer : layer + 1, :], shift[layer : layer + 1, :], normed)
    else:
        normed, pre_grad, sums, send_up, send_down = refs
    for column in range(0, FF, 256):
        columns = slice(column, column + 256)
        back = dot(grad[...], wd[layer, columns, :], NT) * slope[:, columns].astype(FLOAT)
        back = back.astype(BRAIN)
        pre_grad[:, columns] = back
        sums[3 + column // 512 : 4 + column // 512, column % 512 : column % 512 + 256] = jnp.sum(
            back.astype(FLOAT), axis=0, keepdims=True
        )
    feed_weight_grads(info, FEED_ORDERS[layer], 1, normed, pre_grad, hidden, grad, send_up, send_down, shards)
    sums[0:2, :] = jnp.zeros((2, WIDTH), FLOAT)
    sums[2:3, :] = jnp.sum(grad[...].astype(FLOAT), axis=0, keepdims=True)
    sums[7:8, :] = jnp.zeros((1, WIDTH), FLOAT)


def feed_back_keep(layer, shards, info, grad, normed, pre_grad, hidden, stream, gain, wu, sums_in, wo, qkv, far, prob, exact,
                   target, sums, keep_up, keep_down, grad_out, dots, grad_far, norm_grad):
    feed_weight_grads(info, FEED_ORDERS[layer], 0, normed, pre_grad, hidden, grad, keep_up, keep_down, shards)
    for column in range(0, WIDTH, 256):
        norm_grad[:, column : column + 256] = dot(pre_grad[...], wu[layer, column : column + 256, :], NT)
    sums[...] = sums_in[...]
    norm_back(stream, gain[layer : layer + 1, :], norm_grad, grad, target, sums.at[0:1, :], sums.at[1:2, :])
    for column in range(0, WIDTH, 256):
        back = dot(target[...], wo[layer, column : column + 256, :], NT)
        back = back * (iota((TOKENS, 256), 0) < info[2]).astype(FLOAT)
        grad_out[:, column : column + 256] = back.astype(BRAIN)
    far_backward(qkv, far, prob, exact, grad_out, grad_far, dots)


def split_pieces(rows, section, own, far, near):
    targets = {0: own, 2: far}
    for k in range(4):
        piece = rows[:, pl.ds(pl.multiple_of((section ^ k) * 128, 128), 128)]
        if k % 2 == 0:
            targets[k][...] = piece
        else:
            near[k // 2, :, :] = piece


def last_output(layer, info, mid, hidden, wd, db, own, far, near, final):
    for column in range(0, WIDTH, 256):
        columns = slice(column, column + 256)
        total = dot(hidden[...], wd[layer, :, columns])
        final[:, columns] = (mid[:, columns].astype(FLOAT) + total + db[layer : layer + 1, columns]).astype(BRAIN)
    split_pieces(final, info[4], own, far, near)


def attend_back(info, qkv, coarse, far, prob, grad_out, dots, grad_q, grad_kv, grad_coarse):
    hier_backward(qkv, coarse, far, prob, grad_out, dots, grad_q, grad_kv, grad_coarse)


def project_back(layer, shards, info, grad, stream, att, grad_q, grad_kv, grad_coarse, grad_far, gain, shift,
                 qkv_grad, send, send_more, keep, keep_more, normed):
    norm_into(stream, gain[layer : layer + 1, :], shift[layer : layer + 1, :], normed)
    qkv_grad[:, 0:WIDTH] = grad_q[...]
    projected_grad(qkv_grad, grad_kv, grad_coarse, grad_far, info[2])
    attend_weight_grads(info, ATTEND_ORDERS[layer], 1, normed, qkv_grad, att, grad, send, send_more, shards)
    attend_weight_grads(info, ATTEND_ORDERS[layer], 0, normed, qkv_grad, att, grad, keep, keep_more, shards)


def project_back_norm(layer, last, info, grad, stream, qkv_grad, gain, wp, *refs):
    section = info[4]
    refs = list(refs)
    if last:
        earlier = refs[:3]
        del refs[:3]
        own, far, near, small, norm_grad, target, sums = refs
    else:
        mid, hidden, wd, db, target, sums, own, far, near, norm_grad, final = refs
        last_output(layer, info, mid, hidden, wd, db, own, far, near, final)
    for column in range(0, WIDTH, 256):
        norm_grad[:, column : column + 256] = dot(qkv_grad[...], wp[layer, column : column + 256, :], NT)
    norm_back(stream, gain[layer : layer + 1, :], norm_grad, grad, target, sums.at[0:1, :], sums.at[1:2, :])
    if last:
        split_pieces(target, section, own, far, near)
    sums[2:3, :] = jnp.sum(grad[...].astype(FLOAT), axis=0, keepdims=True)
    sums[3:8, :] = jnp.zeros((5, WIDTH), FLOAT)
    if last:
        feed_one, attend_one, feed_zero = earlier
        for k, sublayer in enumerate((sums, feed_zero, attend_one, feed_one)):
            up = feed_zero if k < 2 else feed_one
            small[k, 0:3, :] = sublayer[0:3, :]
            small[k, 3:5, :] = up[3 + k % 2 * 2 : 5 + k % 2 * 2, :]
            small[k, 5:, :] = jnp.zeros((11, WIDTH), FLOAT)


def beside(pairs):
    row = column = 0
    for mine, came in zip(pairs[::2], pairs[1::2]):
        rows, columns = mine.shape[1:]
        yield mine, came, slice(row, row + rows), slice(column, column + columns)
        column = (column + columns) % WIDTH
        row += rows if column == 0 else 0


def add_halves(info, *refs):
    *pairs, give, kept = refs
    half = give.shape[0]

    def body(k, carry):
        for mine, came, rows, columns in beside(pairs):
            give[k, rows, columns] = mine[half + k] + came[half + k]
            kept[k, rows, columns] = mine[k] + came[k]
        return carry

    lax.fori_loop(0, half, body, 0)


def add_last(info, *refs):
    *pairs, total = refs
    for mine, came, rows, columns in beside(pairs):
        total[rows, columns] = mine[0] + came[0]


def add_first(x_bits, info, *refs):
    *pairs, small, small_came, give, kept = refs
    half, height = give.shape[0], give.shape[1] - small.shape[1]
    core = info[4] & 1

    def body(k, carry):
        for target, block in ((give, half + k), (kept, k)):
            for mine, came, rows, columns in beside(pairs):
                target[k, rows, columns] = mine[block] + came[block]
            rel_x = (block >> jnp.where(core == 0, x_bits[0], x_bits[1])) & 1
            quarter = info[4] ^ (2 * rel_x)
            target[k, height:, :] = (small[quarter] + small_came[quarter]).astype(BRAIN)
        return carry

    lax.fori_loop(0, half, body, 0)


def place_shares(layer, shards, section, pieces, outs, stages, sems):
    up, down, proj, back = stages
    rows = WIDTH // shards
    for k in range(4):
        owner = section ^ k
        piece = pieces[k]
        up[:, pl.ds(pl.multiple_of(owner * 512, 512), 512)] = piece[0:rows, :].astype(FLOAT)
        for part in range(FF // WIDTH):
            down[part * rows : (part + 1) * rows, pl.ds(pl.multiple_of(owner * 128, 128), 128)] = piece[
                rows : 2 * rows, 128 * part : 128 * part + 128].astype(FLOAT)
        proj[:, pl.ds(pl.multiple_of(owner * 384, 128), 384)] = piece[2 * rows : 3 * rows, 0:384].astype(FLOAT)
        back[:, pl.ds(pl.multiple_of(owner * 128, 128), 128)] = piece[2 * rows : 3 * rows, 384:].astype(FLOAT)
    return [fetch(stage, out.at[layer], sems.at[k]) for k, (stage, out) in enumerate(zip(stages, outs))]


def finish_tokens(info, own, near, across, target, done, sems):
    section = info[4]
    copies = []
    for k, piece in enumerate((own, near.at[0], across.at[0], across.at[1])):
        owner = section ^ k
        to = target.at[owner >> 1, pl.ds(pl.multiple_of((owner & 1) * TOKENS, TOKENS), TOKENS)]
        copies.append(fetch(piece, to, sems.at[k]))
    done[...] = jnp.zeros((8, 128), FLOAT)
    for copy in copies:
        copy.wait()


def finish_one(shards, info, own, near, across, beyond, up, down, proj, back, *scratch):
    section, sems = info[4], scratch[-1]
    copies = place_shares(1, shards, section, (own, near, across, beyond), (up, down, proj, back), scratch[:4], sems)
    for copy in copies:
        copy.wait()


def finish_zero(shards, info, own, near, across, beyond, _up, _down, _proj, _back,
                up, down, proj, back, *refs):
    section, dp = info[4], info[5]
    vectors, vector_stages, stages = refs[:7], refs[7:14], refs[14:18]
    small, sems, vector_sems = refs[18:]
    pieces = (own, near, across, beyond)
    copies = place_shares(0, shards, section, pieces, (up, down, proj, back), stages, sems)
    width = WIDTH // shards
    for k in range(4):
        small[section ^ k, :, :] = pieces[k][3 * width :, :]
    total = jnp.concatenate([small[k, :, :] for k in range(4)], axis=0)

    def taken(start, columns):
        pick = (iota((WIDTH, columns), 0) == start + iota((WIDTH, columns), 1)).astype(FLOAT).astype(BRAIN)
        return dot(total, pick)

    gain_a, bias_a, bias_o, gain_f, bias_f, bias_u, bias_d = vector_stages
    part = taken(dp * width, width)
    for layer in range(2):
        attend, feed = 32 * layer, 32 * layer + 16
        for start, outs in ((attend, (gain_a, bias_a, bias_o)), (feed, (gain_f, bias_f, bias_d))):
            for k, out in enumerate(outs):
                out[layer : layer + 1, :] = part[start + k : start + k + 1]
    wide = FF // shards
    per_row = WIDTH // wide
    part = taken(dp % per_row * wide, wide)
    for layer in range(2):
        row = part[32 * layer + 3 : 32 * layer + 4]
        for k in range(1, 4):
            at = 32 * layer + 16 * (k // 2) + 3 + k % 2
            row = jnp.where(dp // per_row == k, part[at : at + 1], row)
        bias_u[layer : layer + 1, :] = row
    copies += [fetch(stage, out, vector_sems.at[k]) for k, (stage, out) in enumerate(zip(vector_stages, vectors))]
    for copy in copies:
        copy.wait()


def swap(block, partner):
    sections = lax.axis_size("section")
    pairs = []
    for dp in range(lax.axis_size("dp")):
        for section in range(sections):
            to_dp, to_section = partner(dp, section)
            pairs.append((dp * sections + section, to_dp * sections + to_section))
    return lax.ppermute(block, ("dp", "section"), pairs)


def over_section(block, bits):
    return swap(block, lambda dp, section: (dp, section ^ bits))


def there(*arrays):
    return [(VMEM, pltpu.with_memory_space_constraint(array, pltpu.VMEM)) for array in arrays]


def in_hbm(*arrays):
    return [(ANY, pltpu.with_memory_space_constraint(array, pltpu.HBM)) for array in arrays]


class Reduction:
    def __init__(self, line, name, orders, *send):
        self.line, self.name = line, name
        self.bits = lax.axis_size("dp").bit_length() - 1
        self.orders = [axes_of(order, self.bits) for order in orders]
        self.came = [over_section(part, 1) for part in send]
        self.done = 0

    def partner(self, dp, section):
        axis = self.orders[section & 1][self.done]
        return (dp, section ^ 2) if axis == "x" else (dp ^ (1 << axis), section)

    def keep(self, *blocks):
        self.mine = list(blocks)

    def height(self, other):
        arrays = self.mine + (other.mine if other is not None else [])
        return sum(array.shape[1] * array.shape[2] for array in arrays) // WIDTH

    def pairs(self):
        return [pair for mine, came in zip(self.mine, self.came) for pair in there(mine, came)]

    def step(self, other=None, small=None):
        pairs = self.pairs() + (other.pairs() if other is not None else [])
        dims = [self.mine[0].shape[0] // 2, self.height(other), WIDTH]
        body = add_halves
        if small is not None:
            body = functools.partial(add_first, [self.bits - order.index("x") for order in self.orders])
            pairs += there(small, over_section(small, 1))
            dims[1] += small.shape[1]
        give, mine = self.line.call(body, [vmem(dims)] * 2, pairs, [], 0.2, self.name + str(self.done))
        self.mine, self.came = [mine], [swap(give, self.partner)]
        self.done += 1

    def last(self, other=None):
        while self.done <= self.bits:
            self.step(other)
            other = None
        pairs = self.pairs() + (other.pairs() if other is not None else [])
        rows = self.height(other)
        (total,) = self.line.call(add_last, [vmem((rows, WIDTH))], pairs, [], 0.1, self.name + "_last")
        return total


def over_all_sections(share):
    across = over_section(share, 2)
    return share, over_section(share, 1), across, over_section(across, 1)


def exchange_near(own, far, near):
    came = over_section(near, 1)
    return own, came, jnp.concatenate([far[None], came[1:]], axis=0)


def finish_rows(line, own, near, across, name):
    outs = [shape((2, 2 * TOKENS, 128)), vmem((8, 128), FLOAT)]
    target, line.last = line.call(
        finish_tokens, outs, [(ANY, array) for array in (own, near, across)],
        [pltpu.SemaphoreType.DMA((4,))], 1.2, name, out_specs=[ANY, VMEM],
    )
    return target


def local(inputs, lengths, ag, ab, wp, wo, ob, fg, fb, wu, ub, wd, db, cotangent):
    shards = lax.axis_size("dp")
    ids = jnp.stack([lax.axis_index("section"), lax.axis_index("dp")]).astype(jnp.int32)
    line = Line()

    rows, wide, tall = vmem((TOKENS, WIDTH)), vmem((TOKENS, FF)), vmem((TOKENS, 3 * WIDTH))
    rows_float, double_float = vmem((TOKENS, WIDTH), FLOAT), vmem((TOKENS, 2 * WIDTH), FLOAT)
    coarse_shape, far_shape = vmem((TOKENS, 2 * WIDTH)), vmem((16, 2 * WIDTH))
    prob_shape = vmem((GROUPS, 2, KEYS, QROWS))
    bias_shape = vmem((TOKENS + 16, 128), FLOAT)
    sums_shape = vmem((8, WIDTH), FLOAT)
    piece, two_pieces = vmem((TOKENS, 128)), vmem((2, TOKENS, 128))
    params = (ag, ab, ob, fg, fb, ub, db, wp, wo, wu, wd)
    (ag, ab, ob, fg, fb, ub, db, wp, wo, wu, wd,
     qkv0, coarse0, far0, prob0, att0, exact0, stream0, mid0, hidden0, slope0, stream1, qkv1, coarse1, info, pooled) = line.call(
        functools.partial(first_kernel, shards),
        [vmem(array.shape, array.dtype) for array in params]
        + [tall, coarse_shape, far_shape, prob_shape, rows, rows_float, rows, rows, wide, wide, rows, tall, coarse_shape,
           pltpu.SMEM((8,), jnp.int32), far_shape],
        [(SMEM, ids)] + in_hbm(lengths, inputs, *params),
        [rows, rows, bias_shape, rows_float, pltpu.SMEM((2,), jnp.int32), pltpu.SemaphoreType.DMA((18,))],
        13.5, "layer_zero_forward", out_specs=[VMEM] * 24 + [SMEM, VMEM],
    )
    line.known, line.last = info, pooled
    far1 = over_section(pooled, 1)
    prob1, att1, exact1, mid1, normed1, hidden1, slope1, grad_last = line.call(
        second_kernel, [prob_shape, rows, rows_float, rows, rows, wide, wide, rows],
        in_hbm(cotangent) + there(qkv1, coarse1, far1, stream1, ob, fg, fb, ub, wo, wu),
        [bias_shape, pltpu.SemaphoreType.DMA],
        6.8, "layer_one_forward",
    )

    blocks = vmem((2 * shards, WIDTH // shards, WIDTH))

    dots_shape = vmem((GROUPS, 2, 8, QROWS), FLOAT)
    far_float = vmem((16, 2 * WIDTH), FLOAT)

    pre_grad, sums_f1, send_up, send_down = line.call(
        functools.partial(feed_back_send, 1, shards, False), [wide, sums_shape, blocks, blocks],
        there(grad_last, hidden1, slope1, wd, normed1), [], 3.2, "feed_back_send_1",
    )
    feed_one = Reduction(line, "feed_one_", FEED_ORDERS[1], send_up, send_down)
    grad3, sums_f1, keep_up, keep_down, grad_out, dots, grad_far = line.call(
        functools.partial(feed_back_keep, 1, shards),
        [rows, sums_shape, blocks, blocks, rows, dots_shape, far_float],
        there(grad_last, normed1, pre_grad, hidden1, mid1, fg, wu, sums_f1, wo, qkv1, far1, prob1, exact1), [rows_float],
        5.5, "feed_back_keep_1",
    )
    grad_far = over_section(grad_far, 1)
    feed_one.keep(keep_up, keep_down)
    feed_one.step()
    grad_q, grad_kv, grad_coarse = line.call(
        attend_back, [rows, double_float, double_float],
        there(qkv1, coarse1, far1, prob1, grad_out, dots), [], 4.3, "attend_back_1",
    )
    qkv_grad, *both = line.call(
        functools.partial(project_back, 1, shards), [tall] + [vmem((2 * shards, WIDTH // shards, WIDTH // 2))] * 4,
        there(grad3, stream1, att1, grad_q, grad_kv, grad_coarse, grad_far, ag, ab), [rows], 3.4, "project_back_1",
    )
    attend_one = Reduction(line, "attend_one_", ATTEND_ORDERS[1], *both[:2])
    attend_one.keep(*both[2:])
    grad2, sums_a1, *out_pieces = line.call(
        functools.partial(project_back_norm, 1, False), [rows, sums_shape, piece, piece, two_pieces],
        there(grad3, stream1, qkv_grad, ag, wp, mid1, hidden1, wd, db), [rows_float, rows], 3.0, "project_back_norm_1",
    )
    out_own, out_near, out_give = exchange_near(*out_pieces)
    out_across = over_section(out_give, 2)
    pre_grad, sums_f0, send_up, send_down, normed = line.call(
        functools.partial(feed_back_send, 0, shards, True), [wide, sums_shape, blocks, blocks, rows],
        there(grad2, hidden0, slope0, wd, mid0, fg, fb), [], 3.7, "feed_back_send_0",
    )
    feed_zero = Reduction(line, "feed_zero_", FEED_ORDERS[0], send_up, send_down)
    line.pin(out_near)
    feed_one.step()
    attend_one.step()
    grad1, sums_f0, keep_up, keep_down, grad_out, dots, grad_far = line.call(
        functools.partial(feed_back_keep, 0, shards),
        [rows, sums_shape, blocks, blocks, rows, dots_shape, far_float],
        there(grad2, normed, pre_grad, hidden0, mid0, fg, wu, sums_f0, wo, qkv0, far0, prob0, exact0), [rows_float],
        5.5, "feed_back_keep_0",
    )
    grad_far = over_section(grad_far, 1)
    feed_zero.keep(keep_up, keep_down)
    line.pin(out_across)
    feed_zero.step()
    grad_q, grad_kv, grad_coarse = line.call(
        attend_back, [rows, double_float, double_float],
        there(qkv0, coarse0, far0, prob0, grad_out, dots), [], 4.3, "attend_back_0",
    )
    attend_one.step()
    line.pin(*feed_one.came)
    qkv_grad, *both = line.call(
        functools.partial(project_back, 0, shards), [tall] + [vmem((2 * shards, WIDTH // shards, WIDTH // 2))] * 4,
        there(grad1, stream0, att0, grad_q, grad_kv, grad_coarse, grad_far, ag, ab), [rows], 0.5, "project_back_0",
    )
    attend_zero = Reduction(line, "attend_zero_", ATTEND_ORDERS[0], *both[:2])
    attend_zero.keep(*both[2:])
    *grad_pieces, small = line.call(
        functools.partial(project_back_norm, 0, True), [piece, piece, two_pieces, vmem((4, 16, WIDTH), FLOAT)],
        there(grad1, stream0, qkv_grad, ag, wp, sums_f1, sums_a1, sums_f0), [rows_float, rows, sums_shape], 5.0,
        "project_back_norm_0",
    )
    grad_own, grad_near, grad_give = exchange_near(*grad_pieces)
    line.pin(*attend_one.came)
    attend_zero.step(small=small)
    feed_one.step(attend_one)
    feed_zero.step()
    line.pin(grad_near)
    attend_zero.step()
    feed_zero.step()
    feed_one.step()
    attend_zero.step()
    grad_across = over_section(grad_give, 2)
    line.pin(grad_across)
    feed_zero.step(attend_zero)
    outputs = finish_rows(line, out_own, out_near, out_across, "finish_outputs")
    input_grad = finish_rows(line, grad_own, grad_near, grad_across, "finish_input_grad")
    share_one = feed_one.last()
    share_zero = feed_zero.last()

    weight_grads = [
        shape((2, WIDTH // shards, FF), FLOAT), shape((2, FF // shards, WIDTH), FLOAT),
        shape((2, WIDTH // shards, 3 * WIDTH), FLOAT), shape((2, WIDTH // shards, WIDTH), FLOAT),
    ]
    stages = [vmem(out.shape[1:], FLOAT) for out in weight_grads]
    stages += [vmem((4, 16, WIDTH)), pltpu.SemaphoreType.DMA((4,))]
    weight_first = line.call(
        functools.partial(finish_one, shards), weight_grads, there(*over_all_sections(share_one)),
        stages, 1.9, "finish_one", out_specs=[ANY] * 4,
    )
    vector = shape((2, WIDTH // shards), FLOAT)
    vectors = [vector] * 5 + [shape((2, FF // shards), FLOAT), vector]
    finished = line.call(
        functools.partial(finish_zero, shards), weight_grads + vectors,
        there(*over_all_sections(share_zero)) + [(ANY, array) for array in weight_first],
        [vmem(out.shape, FLOAT) for out in vectors] + stages + [pltpu.SemaphoreType.DMA((7,))], 3.0, "finish_zero",
        out_specs=[ANY] * 11, aliases={4 + k: k for k in range(4)},
    )
    up_grad, down_grad, proj_grad, back_grad, gain_a, bias_a, bias_o, gain_f, bias_f, bias_u, bias_d = finished
    return (outputs, input_grad, gain_a, bias_a, proj_grad, back_grad, bias_o, gain_f, bias_f, up_grad, bias_u,
            down_grad, bias_d)


def solution(mesh):
    batch = P("dp", None, None)
    split = P("dp", None, "section")
    vector, matrix = P(None, "dp"), P(None, "dp", None)
    return jax.shard_map(
        local,
        mesh=mesh,
        in_specs=(batch, P("dp")) + (P(),) * 11 + (batch,),
        out_specs=(split, split, vector, vector, matrix, matrix, vector, vector, vector, matrix, vector, matrix, vector),
        check_vma=False,
    )
```

```python
import functools

import jax
import jax.numpy as jnp
from jax import lax
from jax.experimental import pallas as pl
from jax.experimental.pallas import tpu as pltpu
from jax.sharding import PartitionSpec as P

FLOAT = jnp.float32
BRAIN = jnp.bfloat16
NORM_EPS = 1e-05
MASK_FILL = -1000000000.0
WIDTH = 512
TOKENS = 512
FF = 2048
GROUP = 64
GROUPS = TOKENS // GROUP
LEVELS = 5
KEYS = GROUP + 32 + 16 * (LEVELS - 1)
HALF = 256
QROWS = 4 * GROUP
TILE = 256
TILES = TOKENS // TILE
LEVEL_AT = (0, 128, 192, 224, 240)
USED = 248
MIB = 1024 * 1024
FEED_ORDERS = ((("x", 1, 0, 2), (1, 0, "x", 2)), (("x", 0, 1, 2), (0, 1, 2, "x")))
ATTEND_ORDERS = ((("x", 0, 1, 2), (0, "x", 1, 2)), (("x", 0, 1, 2), (1, 0, 2, "x")))
COST = 1 * 10**9

NN = (((1,), (0,)), ((), ()))
NT = (((1,), (1,)), ((), ()))
TN = (((0,), (0,)), ((), ()))


def dot(left, right, dims=NN):
    return lax.dot_general(left, right, dims, preferred_element_type=FLOAT)


def iota(shape, dim):
    return lax.broadcasted_iota(jnp.int32, shape, dim)


def normalise(rows):
    mean = jnp.mean(rows, axis=-1, keepdims=True)
    centred = rows - mean
    scale = lax.rsqrt(jnp.mean(centred * centred, axis=-1, keepdims=True) + NORM_EPS)
    return centred * scale, scale


def norm_into(source, gain, bias, target):
    for start in range(0, TOKENS, 64):
        rows = slice(start, start + 64)
        unit, _ = normalise(source[rows, :].astype(FLOAT))
        target[rows, :] = (unit * gain + bias).astype(BRAIN)


def norm_back(source, gain, grad_ref, through_ref, target, gain_out, bias_out):
    gain_sum = jnp.zeros((1, WIDTH), FLOAT)
    bias_sum = jnp.zeros((1, WIDTH), FLOAT)
    for start in range(0, TOKENS, 64):
        rows = slice(start, start + 64)
        unit, scale = normalise(source[rows, :].astype(FLOAT))
        grad = grad_ref[rows, :]
        gain_sum = gain_sum + jnp.sum(grad * unit, axis=0, keepdims=True)
        bias_sum = bias_sum + jnp.sum(grad, axis=0, keepdims=True)
        inner = grad * gain
        inner_mean = jnp.mean(inner, axis=-1, keepdims=True)
        slope = jnp.mean(inner * unit, axis=-1, keepdims=True)
        back = scale * (inner - inner_mean - unit * slope)
        target[rows, :] = (through_ref[rows, :].astype(FLOAT) + back).astype(BRAIN)
    gain_out[...] = gain_sum
    bias_out[...] = bias_sum


def span_of(row):
    level = 1 + sum((row >= at).astype(jnp.int32) for at in LEVEL_AT[1:])
    at = sum(jnp.where(level == k + 1, at, 0) for k, at in enumerate(LEVEL_AT))
    return level, (row - at) << level


def pool_matrix(tile, live, transposed):
    dims = (TILE, TILE)
    row, token = iota(dims, int(transposed)), iota(dims, 1 - int(transposed))
    level, first = span_of(row)
    inside = (token >= first) & (token < first + (1 << level)) & (token < live - tile * TILE) & (row < USED)
    return inside.astype(FLOAT).astype(BRAIN)


def counts(tile, live, columns):
    level, first = span_of(iota((TILE, columns), 0))
    return jnp.clip(live - tile * TILE - first, 0, 1 << level)


def far_counts(live, columns):
    return jnp.clip(live - (iota((16, columns), 0) << LEVELS), 0, 1 << LEVELS)


def inverse(number):
    return 1.0 / jnp.maximum(number, 1).astype(FLOAT)


def log_count(number):
    return jnp.where(number > 0, jnp.log(jnp.maximum(number, 1).astype(FLOAT)), MASK_FILL)


def project(normed, weight, target, start, stop, target_start=None):
    shift = 0 if target_start is None else target_start - start
    for column in range(start, stop, 256):
        target[:, column + shift : column + shift + 256] = dot(
            normed[...], weight[:, column : column + 256]
        ).astype(BRAIN)


def pool_keys(qkv, live, coarse, pooled):
    matrix = [pool_matrix(tile, live, False) for tile in range(TILES)]
    share = [inverse(counts(tile, live, TILE)) for tile in range(TILES)]
    for column in range(0, 2 * WIDTH, TILE):
        columns = slice(column, column + TILE)
        last = []
        for tile in range(TILES):
            rows = slice(tile * TILE, (tile + 1) * TILE)
            mean = dot(matrix[tile], qkv[rows, WIDTH + column : WIDTH + column + TILE]) * share[tile]
            coarse[rows, columns] = mean.astype(BRAIN)
            last.append(mean[LEVEL_AT[4] : USED])
        pooled[:, columns] = jnp.concatenate(last, axis=0).astype(BRAIN)


def project_far(normed, weight, live, pooled):
    key, token = iota((16, TOKENS), 0), iota((16, TOKENS), 1)
    matrix = ((token >> LEVELS == key) & (token < live)).astype(FLOAT).astype(BRAIN)
    mean = dot(matrix, normed[...]) * inverse(far_counts(live, WIDTH))
    high = mean.astype(BRAIN)
    both = jnp.concatenate([high, (mean - high.astype(FLOAT)).astype(BRAIN)], axis=0)
    for column in range(0, 2 * WIDTH, 256):
        product = dot(both, weight[:, WIDTH + column : WIDTH + column + 256])
        pooled[:, column : column + 256] = (product[0:16] + product[16:32]).astype(BRAIN)


def key_bias(live, other_live, bias):
    for tile in range(TILES):
        bias[tile * TILE : (tile + 1) * TILE, :] = log_count(counts(tile, live, 128))
    bias[TOKENS:, :] = log_count(far_counts(other_live, 128))


def head_mask(value):
    dims = (QROWS, HALF)
    return jnp.where(iota(dims, 0) // GROUP == iota(dims, 1) // 64, value, 0.0).astype(BRAIN)


def pair_mask():
    own_key, own_query = iota((GROUP, QROWS), 0) // 32, iota((GROUP, QROWS), 1) % GROUP // 32
    near_key, near_query = iota((32, QROWS), 0) // 16, iota((32, QROWS), 1) % GROUP // 32
    own = jnp.where(own_key == own_query, 0.0, MASK_FILL)
    near = jnp.where(near_key != near_query, 0.0, MASK_FILL)
    return jnp.concatenate([own, near], axis=0)


def spread(rows, mask):
    return jnp.concatenate([rows] * 4, axis=0) * mask


def gather_heads(wide):
    left = iota((GROUP, 128), 1) < 64
    pairs = [wide[k * GROUP : (k + 1) * GROUP, k // 2 * 128 : k // 2 * 128 + 128] for k in range(4)]
    return jnp.concatenate([jnp.where(left, pairs[0], pairs[1]), jnp.where(left, pairs[2], pairs[3])], axis=1)


def group_rows(group):
    at = [(group // 4 * TILE + group % 4 * 32, 32)]
    for level in range(2, LEVELS):
        block = (group >> (level - 2)) ^ 1
        per_tile = TILE // (16 << level)
        at.append((block // per_tile * TILE + LEVEL_AT[level - 1] + block % per_tile * 16, 16))
    return at


def key_block(qkv, coarse, far, group, part, half):
    column = WIDTH * (part + 1) + HALF * half
    columns = slice(WIDTH * part + HALF * half, WIDTH * part + HALF * (half + 1))
    pieces = [qkv[group * GROUP : (group + 1) * GROUP, column : column + HALF]]
    pieces += [coarse[at : at + size, columns] for at, size in group_rows(group)]
    return jnp.concatenate(pieces + [far[:, columns]], axis=0)


def hier_forward(qkv, coarse, far, bias, prob, attended, exact, live):
    mask = head_mask(0.125)
    pairs = pair_mask()
    for group in range(GROUPS):
        rows = slice(group * GROUP, (group + 1) * GROUP)
        own_bias = jnp.where(group * GROUP + iota((GROUP, QROWS), 0) < live, 0.0, MASK_FILL)
        coarse_bias = jnp.concatenate(
            [bias[at : at + size, :] for at, size in group_rows(group)] + [bias[TOKENS:, :]], axis=0
        )
        added_bias = jnp.concatenate([own_bias, jnp.concatenate([coarse_bias] * 2, axis=1)], axis=0)
        added_bias = jnp.concatenate([added_bias[: GROUP + 32] + pairs, added_bias[GROUP + 32 :]], axis=0)
        query_live = (group * GROUP + iota((GROUP, HALF), 0) < live).astype(FLOAT)
        for half in range(2):
            columns = slice(half * HALF, (half + 1) * HALF)
            queries = spread(qkv[rows, columns], mask)
            scores = dot(key_block(qkv, coarse, far, group, 0, half), queries, NT) + added_bias
            weights = jnp.exp(scores - jnp.max(scores, axis=0, keepdims=True))
            weights = weights * (1.0 / jnp.sum(weights, axis=0, keepdims=True))
            weights = weights.astype(BRAIN)
            prob[group, half, :, :] = weights
            output = dot(weights, key_block(qkv, coarse, far, group, 1, half), TN)
            output = gather_heads(output) * query_live
            exact[rows, columns] = output
            attended[rows, columns] = output.astype(BRAIN)


def far_backward(qkv, far, prob, exact, grad_out, grad_far, dots):
    weights = []
    for half in range(2):
        for head in range(4):
            parts = [prob[g, half, KEYS - 16 :, head * 64 : head * 64 + 64] for g in range(GROUPS)]
            weights.append(jnp.concatenate(parts, axis=1))
    weights = jnp.concatenate(weights, axis=0)
    dims = (128, WIDTH)
    mask = jnp.where(iota(dims, 0) // 16 == iota(dims, 1) // 64, 1.0, 0.0).astype(BRAIN)
    values = jnp.concatenate([far[:, WIDTH:]] * 8, axis=0) * mask
    both = exact[...] * grad_out[...].astype(FLOAT)
    high = both.astype(BRAIN)
    total = dot(mask, high, NT) + dot(mask, (both - high.astype(FLOAT)).astype(BRAIN), NT)
    score_grad = (weights.astype(FLOAT) * (dot(values, grad_out[...], NT) - total)).astype(BRAIN)
    left = iota((16, 128), 1) < 64
    for part, wide in enumerate((dot(score_grad, qkv[:, 0:WIDTH]) * 0.125, dot(weights, grad_out[...]))):
        for pair in range(4):
            block = wide[32 * pair : 32 * pair + 32, 128 * pair : 128 * pair + 128]
            to = part * WIDTH + 128 * pair
            grad_far[:, to : to + 128] = jnp.where(left, block[0:16], block[16:32])
    for group in range(GROUPS):
        for half in range(2):
            rows = [half * 64 + head * 16 for head in range(4)]
            dots[group, half, 0:1, :] = jnp.concatenate(
                [total[row : row + 1, group * GROUP : (group + 1) * GROUP] for row in rows], axis=1)


def hier_backward(qkv, coarse, far, prob, grad_out, dots, grad_q, grad_kv, grad_coarse):
    mask_q, mask_o = head_mask(0.125), head_mask(1.0)
    for group in range(GROUPS):
        own = slice(group * GROUP, (group + 1) * GROUP)
        for half in range(2):
            columns = slice(half * HALF, (half + 1) * HALF)
            queries = spread(qkv[own, columns], mask_q)
            grads = spread(grad_out[own, columns], mask_o)
            keys = key_block(qkv, coarse, far, group, 0, half)
            values = key_block(qkv, coarse, far, group, 1, half)
            weights = prob[group, half, :, :]
            score_grad = weights.astype(FLOAT) * (dot(values, grads, NT) - dots[group, half, 0:1, :])
            score_grad = score_grad.astype(BRAIN)
            grad_q[own, columns] = (gather_heads(dot(score_grad, keys, TN)) * 0.125).astype(BRAIN)
            for part, block in enumerate((dot(score_grad, queries), dot(weights, grads))):
                to = slice(part * WIDTH + half * HALF, part * WIDTH + (half + 1) * HALF)
                grad_kv[own, to] = block[0:GROUP]
                start = GROUP
                for level, (at, size) in enumerate(group_rows(group)):
                    piece = block[start : start + size]
                    start += size
                    if level < 2 or group % (1 << (level - 1)) == 0:
                        grad_coarse[at : at + size, to] = piece
                    else:
                        grad_coarse[at : at + size, to] += piece


def add_projected(stream, source, weight, bias, target):
    for column in range(0, WIDTH, 256):
        columns = slice(column, column + 256)
        total = dot(source[...], weight[:, columns])
        target[:, columns] = (stream[:, columns].astype(FLOAT) + total + bias[:, columns]).astype(
            BRAIN
        )


def feed_hidden(normed, weight, bias, hidden, slope):
    scale, cubic = 0.7978845608, 0.7978845608 * 0.044715
    for start in range(0, TOKENS, 256):
        rows = slice(start, start + 256)
        for column in range(0, FF, 256):
            columns = slice(column, column + 256)
            pre = dot(normed[rows, :], weight[:, columns]) + bias[:, columns]
            square = pre * pre
            share = 0.5 * jnp.tanh(pre * (scale + cubic * square)) + 0.5
            value = pre * share
            hidden[rows, columns] = value.astype(BRAIN)
            slope[rows, columns] = (
                share + value * ((1.0 - share) * (2 * scale + 6 * cubic * square))
            ).astype(BRAIN)


def feed_through(normed, stream, w_up, up_bias, w_down, down_bias, hidden, slope, target, total):
    scale, cubic = 0.7978845608, 0.7978845608 * 0.044715
    for start in range(0, TOKENS, 256):
        rows = slice(start, start + 256)
        for column in range(0, FF, 256):
            columns = slice(column, column + 256)
            pre = dot(normed[rows, :], w_up[:, columns]) + up_bias[:, columns]
            square = pre * pre
            share = 0.5 * jnp.tanh(pre * (scale + cubic * square)) + 0.5
            value = pre * share
            value_low = value.astype(BRAIN)
            hidden[rows, columns] = value_low
            slope[rows, columns] = (
                share + value * ((1.0 - share) * (2 * scale + 6 * cubic * square))
            ).astype(BRAIN)
            part = dot(value_low, w_down[columns, :])
            if column == 0:
                total[rows, :] = part
            else:
                total[rows, :] += part
        target[rows, :] = (stream[rows, :].astype(FLOAT) + total[rows, :] + down_bias).astype(BRAIN)


def projected_grad(qkv_grad, grad_kv, grad_coarse, grad_far, live):
    for tile in range(TILES):
        rows = slice(tile * TILE, (tile + 1) * TILE)
        matrix = pool_matrix(tile, live, True)
        share = inverse(counts(tile, live, TILE))
        for column in range(0, 2 * WIDTH, TILE):
            columns = slice(column, column + TILE)
            spans = jnp.concatenate(
                [grad_coarse[tile * TILE : tile * TILE + LEVEL_AT[4], columns],
                 grad_far[8 * tile : 8 * tile + 8, columns], jnp.zeros((8, TILE), FLOAT)], axis=0)
            total = grad_kv[rows, columns] + dot(matrix, (spans * share).astype(BRAIN))
            qkv_grad[rows, WIDTH + column : WIDTH + column + TILE] = total.astype(BRAIN)


def fetch(source, target, sem):
    copy = pltpu.make_async_copy(source, target, sem)
    copy.start()
    return copy


def reversed_bits(value, bits):
    return sum(((value >> k) & 1) << (bits - 1 - k) for k in range(bits))


def axes_of(order, bits):
    known = [axis for axis in order if axis == "x" or axis < bits]
    return known + [bit for bit in range(bits) if bit not in known]


def block_index(info, owner_core, rel_x, shard, bits, orders):
    index = []
    for order in orders:
        total = 0
        for axis in axes_of(order, bits):
            rel = rel_x if axis == "x" else ((shard >> axis) & 1) ^ ((info[5] >> axis) & 1)
            total = total * 2 + rel
        index.append(total)
    return jnp.where(owner_core == 0, index[0], index[1])


def pair_columns(ref, section, rel_core, width):
    both = []
    for rel_x in range(2):
        quarter = section ^ (2 * rel_x + rel_core)
        both.append(ref[:, pl.ds(pl.multiple_of(quarter * width, 128), width)])
    return jnp.concatenate(both, axis=1)


def feed_weight_grads(info, orders, rel_core, normed, pre_grad, hidden, grad, up, down, shards):
    bits = shards.bit_length() - 1
    section = info[4]
    owner = (section & 1) ^ rel_core
    rows = WIDTH // shards
    wide = FF // shards
    where = [[block_index(info, owner, rel_x, shard, bits, orders) for shard in range(shards)] for rel_x in range(2)]
    for rel_x in range(2):
        quarter = section ^ (2 * rel_x + rel_core)
        for part in range(2):
            at = pl.multiple_of(quarter * 512 + 256 * part, 256)
            block = dot(normed[...], pre_grad[:, pl.ds(at, 256)], TN).astype(BRAIN)
            for shard in range(shards):
                up[where[rel_x][shard], :, 256 * part : 256 * part + 256] = block[shard * rows : (shard + 1) * rows]
    some_grad = pair_columns(grad, section, rel_core, 128)
    for start in range(0, FF, 256):
        block = dot(hidden[:, start : start + 256], some_grad, TN).astype(BRAIN)
        for at in range(0, 256, rows):
            shard, part = (start + at) // wide, (start + at) % wide // rows
            for rel_x in range(2):
                down[where[rel_x][shard], :, 128 * part : 128 * part + 128] = block[
                    at : at + rows, 128 * rel_x : 128 * rel_x + 128]


def attend_weight_grads(info, orders, rel_core, normed, qkv_grad, att, grad, first, second, shards):
    bits = shards.bit_length() - 1
    section = info[4]
    owner = (section & 1) ^ rel_core
    rows = WIDTH // shards
    left = dot(normed[...], pair_columns(qkv_grad, section, rel_core, 384), TN).astype(BRAIN)
    right = dot(att[...], pair_columns(grad, section, rel_core, 128), TN).astype(BRAIN)
    for rel_x in range(2):
        for shard in range(shards):
            where = block_index(info, owner, rel_x, shard, bits, orders)
            mine = slice(shard * rows, (shard + 1) * rows)
            first[where, :, :] = left[mine, 384 * rel_x : 384 * rel_x + 256]
            second[where, :, 0:128] = left[mine, 384 * rel_x + 256 : 384 * rel_x + 384]
            second[where, :, 128:256] = right[mine, 128 * rel_x : 128 * rel_x + 128]


ANY = pl.BlockSpec(memory_space=pl.ANY)
VMEM = pl.BlockSpec(memory_space=pltpu.VMEM)
SMEM = pl.BlockSpec(memory_space=pltpu.SMEM)


def shape(dims, dtype=BRAIN):
    return jax.ShapeDtypeStruct(dims, dtype)


def vmem(dims, dtype=BRAIN):
    return pltpu.VMEM(dims, dtype)


def facts(ids, lengths, shards):
    section, dp = ids[0], ids[1]
    seq, half = section >> 1, section & 1
    length = lengths[seq]

    def inside(value):
        return jnp.minimum(jnp.maximum(value, 0), TOKENS)

    reverse = reversed_bits(dp, shards.bit_length() - 1)
    return seq, half, inside(length - half * TOKENS), inside(length - (1 - half) * TOKENS), section, dp, reverse


class Line:
    def __init__(self):
        self.known, self.last, self.pinned = None, None, []

    def pin(self, *arrays):
        self.pinned += arrays

    def call(self, body, outs, args, scratch, us, name, limit=16, out_specs=None, aliases=None):
        known = [] if self.known is None else [pltpu.with_memory_space_constraint(self.known, pltpu.SMEM)]
        first = len(known)
        count = first + len(args)
        after = there(*([] if self.last is None else [self.last]), *self.pinned)
        self.pinned = []

        def kernel(*refs):
            info = [refs[0][k] for k in range(7)] if known else None
            body(info, *refs[first:count], *refs[count + len(after) :])

        result = pl.pallas_call(
            kernel,
            out_shape=outs,
            in_specs=[SMEM] * first + [spec for spec, _ in args + after],
            out_specs=out_specs or [VMEM] * len(outs),
            scratch_shapes=scratch,
            input_output_aliases={first + k: v for k, v in (aliases or {}).items()},
            compiler_params=pltpu.CompilerParams(vmem_limit_bytes=limit * MIB),
            cost_estimate=pl.CostEstimate(flops=int(us * COST), bytes_accessed=1024, transcendentals=0),
            name=name,
        )(*known, *[array for _, array in args + after])
        if out_specs is None:
            self.last = result[-1]
        return result


def first_kernel(shards, _info, ids, lengths_in, inputs, hag, hab, hob, hfg, hfb, hub, hdb, hwp, hwo, hwu, hwd,
                 ag, ab, ob, fg, fb, ub, db, wp, wo, wu, wd,
                 qkv, coarse, far, prob, att, exact, mine, mid, hidden, slope, out, qkv_next, coarse_next, norm_zero, norm_feed, norm_one, bias, info_out, pooled,
                 other, normed, total, lengths, sems):
    seq, half = ids[0] >> 1, ids[0] & 1
    get_lengths = fetch(lengths_in, lengths, sems.at[17])
    get_mine = fetch(inputs.at[seq, pl.ds(half * TOKENS, TOKENS)], mine, sems.at[0])
    small = [fetch(source, target, sems.at[2 + k]) for k, (source, target) in enumerate(
        ((hag, ag), (hab, ab), (hob, ob), (hfg, fg), (hfb, fb), (hub, ub), (hdb, db)))]
    get_wp = fetch(hwp.at[0], wp.at[0], sems.at[9])
    get_other = fetch(inputs.at[seq, pl.ds((1 - half) * TOKENS, TOKENS)], other, sems.at[1])
    large = [fetch(source.at[0], target.at[0], sems.at[10 + k]) for k, (source, target) in enumerate(
        ((hwo, wo), (hwu, wu), (hwd, wd)))]
    later = [fetch(source.at[1], target.at[1], sems.at[13 + k]) for k, (source, target) in enumerate(
        ((hwp, wp), (hwo, wo), (hwu, wu), (hwd, wd)))]
    get_lengths.wait()
    info = facts(ids, lengths, shards)
    for k, value in enumerate(info):
        info_out[k] = value
    live, other_live = info[2], info[3]
    key_bias(live, other_live, bias)
    for copy in small:
        copy.wait()
    get_mine.wait()
    norm_into(mine, ag[0:1, :], ab[0:1, :], norm_zero)
    get_wp.wait()
    project(norm_zero, wp.at[0], qkv, 0, 3 * WIDTH)
    get_other.wait()
    norm_into(other, ag[0:1, :], ab[0:1, :], normed)
    project_far(normed, wp.at[0], other_live, far)
    pool_keys(qkv, live, coarse, pooled)
    hier_forward(qkv, coarse, far, bias, prob, att, exact, live)
    large[0].wait()
    add_projected(mine, att, wo.at[0], ob[0:1, :], mid)
    norm_into(mid, fg[0:1, :], fb[0:1, :], norm_feed)
    large[1].wait()
    large[2].wait()
    feed_through(norm_feed, mid, wu.at[0], ub[0:1, :], wd.at[0], db[0:1, :], hidden, slope, out, total)
    norm_into(out, ag[1:2, :], ab[1:2, :], norm_one)
    later[0].wait()
    project(norm_one, wp.at[1], qkv_next, 0, 3 * WIDTH)
    pool_keys(qkv_next, live, coarse_next, pooled)
    for copy in later[1:]:
        copy.wait()


def second_kernel(info, cotangent, qkv, coarse, far, bias, stream, ob, fg, fb, ub, wo, wu,
                  prob, att, exact, mid, normed, hidden, slope, grad, sem):
    live = info[2]
    get_grad = fetch(cotangent.at[info[0], pl.ds(pl.multiple_of(info[1] * TOKENS, TOKENS), TOKENS)], grad, sem)
    hier_forward(qkv, coarse, far, bias, prob, att, exact, live)
    add_projected(stream, att, wo.at[1], ob[1:2, :], mid)
    norm_into(mid, fg[1:2, :], fb[1:2, :], normed)
    feed_hidden(normed, wu.at[1], ub[1:2, :], hidden, slope)
    get_grad.wait()


def feed_back_send(layer, shards, info, grad, hidden, slope, wd, normed, pre_grad, sums, send_up, send_down):
    for column in range(0, FF, 256):
        columns = slice(column, column + 256)
        back = dot(grad[...], wd[layer, columns, :], NT) * slope[:, columns].astype(FLOAT)
        back = back.astype(BRAIN)
        pre_grad[:, columns] = back
        sums[3 + column // 512 : 4 + column // 512, column % 512 : column % 512 + 256] = jnp.sum(
            back.astype(FLOAT), axis=0, keepdims=True
        )
    feed_weight_grads(info, FEED_ORDERS[layer], 1, normed, pre_grad, hidden, grad, send_up, send_down, shards)
    sums[0:2, :] = jnp.zeros((2, WIDTH), FLOAT)
    sums[2:3, :] = jnp.sum(grad[...].astype(FLOAT), axis=0, keepdims=True)
    sums[7:8, :] = jnp.zeros((1, WIDTH), FLOAT)


def feed_back_keep(layer, shards, info, grad, normed, pre_grad, hidden, stream, gain, wu, sums_in, wo, qkv, far, prob, exact,
                   target, sums, keep_up, keep_down, grad_out, dots, grad_far, norm_grad):
    feed_weight_grads(info, FEED_ORDERS[layer], 0, normed, pre_grad, hidden, grad, keep_up, keep_down, shards)
    for column in range(0, WIDTH, 256):
        norm_grad[:, column : column + 256] = dot(pre_grad[...], wu[layer, column : column + 256, :], NT)
    sums[...] = sums_in[...]
    norm_back(stream, gain[layer : layer + 1, :], norm_grad, grad, target, sums.at[0:1, :], sums.at[1:2, :])
    for column in range(0, WIDTH, 256):
        back = dot(target[...], wo[layer, column : column + 256, :], NT)
        back = back * (iota((TOKENS, 256), 0) < info[2]).astype(FLOAT)
        grad_out[:, column : column + 256] = back.astype(BRAIN)
    far_backward(qkv, far, prob, exact, grad_out, grad_far, dots)


def split_pieces(rows, section, own, far, near):
    targets = {0: own, 2: far}
    for k in range(4):
        piece = rows[:, pl.ds(pl.multiple_of((section ^ k) * 128, 128), 128)]
        if k % 2 == 0:
            targets[k][...] = piece
        else:
            near[k // 2, :, :] = piece


def last_output(layer, info, mid, hidden, wd, db, own, far, near, final):
    for column in range(0, WIDTH, 256):
        columns = slice(column, column + 256)
        total = dot(hidden[...], wd[layer, :, columns])
        final[:, columns] = (mid[:, columns].astype(FLOAT) + total + db[layer : layer + 1, columns]).astype(BRAIN)
    split_pieces(final, info[4], own, far, near)


def attend_back(info, qkv, coarse, far, prob, grad_out, dots, grad_q, grad_kv, grad_coarse):
    hier_backward(qkv, coarse, far, prob, grad_out, dots, grad_q, grad_kv, grad_coarse)


def project_back(layer, shards, info, grad, normed, att, grad_q, grad_kv, grad_coarse, grad_far,
                 qkv_grad, send, send_more, keep, keep_more):
    qkv_grad[:, 0:WIDTH] = grad_q[...]
    projected_grad(qkv_grad, grad_kv, grad_coarse, grad_far, info[2])
    attend_weight_grads(info, ATTEND_ORDERS[layer], 1, normed, qkv_grad, att, grad, send, send_more, shards)
    attend_weight_grads(info, ATTEND_ORDERS[layer], 0, normed, qkv_grad, att, grad, keep, keep_more, shards)


def project_back_norm(layer, last, info, grad, stream, qkv_grad, gain, wp, *refs):
    section = info[4]
    refs = list(refs)
    if last:
        earlier = refs[:3]
        del refs[:3]
        own, far, near, small, norm_grad, target, sums = refs
    else:
        mid, hidden, wd, db, target, sums, own, far, near, norm_grad, final = refs
        last_output(layer, info, mid, hidden, wd, db, own, far, near, final)
    for column in range(0, WIDTH, 256):
        norm_grad[:, column : column + 256] = dot(qkv_grad[...], wp[layer, column : column + 256, :], NT)
    norm_back(stream, gain[layer : layer + 1, :], norm_grad, grad, target, sums.at[0:1, :], sums.at[1:2, :])
    if last:
        split_pieces(target, section, own, far, near)
    sums[2:3, :] = jnp.sum(grad[...].astype(FLOAT), axis=0, keepdims=True)
    sums[3:8, :] = jnp.zeros((5, WIDTH), FLOAT)
    if last:
        feed_one, attend_one, feed_zero = earlier
        for k, sublayer in enumerate((sums, feed_zero, attend_one, feed_one)):
            up = feed_zero if k < 2 else feed_one
            small[k, 0:3, :] = sublayer[0:3, :]
            small[k, 3:5, :] = up[3 + k % 2 * 2 : 5 + k % 2 * 2, :]
            small[k, 5:, :] = jnp.zeros((11, WIDTH), FLOAT)


def beside(pairs):
    row = column = 0
    for mine, came in zip(pairs[::2], pairs[1::2]):
        rows, columns = mine.shape[1:]
        yield mine, came, slice(row, row + rows), slice(column, column + columns)
        column = (column + columns) % WIDTH
        row += rows if column == 0 else 0


def add_halves(info, *refs):
    *pairs, give, kept = refs
    half = give.shape[0]

    def body(k, carry):
        for mine, came, rows, columns in beside(pairs):
            give[k, rows, columns] = mine[half + k] + came[half + k]
            kept[k, rows, columns] = mine[k] + came[k]
        return carry

    lax.fori_loop(0, half, body, 0)


def add_last(info, *refs):
    *pairs, total = refs
    for mine, came, rows, columns in beside(pairs):
        total[rows, columns] = mine[0] + came[0]


def add_first(x_bits, info, *refs):
    *pairs, small, small_came, give, kept = refs
    half, height = give.shape[0], give.shape[1] - small.shape[1]
    core = info[4] & 1

    def body(k, carry):
        for target, block in ((give, half + k), (kept, k)):
            for mine, came, rows, columns in beside(pairs):
                target[k, rows, columns] = mine[block] + came[block]
            rel_x = (block >> jnp.where(core == 0, x_bits[0], x_bits[1])) & 1
            quarter = info[4] ^ (2 * rel_x)
            target[k, height:, :] = (small[quarter] + small_came[quarter]).astype(BRAIN)
        return carry

    lax.fori_loop(0, half, body, 0)


def place_shares(layer, shards, section, pieces, outs, stages, sems):
    up, down, proj, back = stages
    rows = WIDTH // shards
    for k in range(4):
        owner = section ^ k
        piece = pieces[k]
        up[:, pl.ds(pl.multiple_of(owner * 512, 512), 512)] = piece[0:rows, :].astype(FLOAT)
        for part in range(FF // WIDTH):
            down[part * rows : (part + 1) * rows, pl.ds(pl.multiple_of(owner * 128, 128), 128)] = piece[
                rows : 2 * rows, 128 * part : 128 * part + 128].astype(FLOAT)
        proj[:, pl.ds(pl.multiple_of(owner * 384, 128), 384)] = piece[2 * rows : 3 * rows, 0:384].astype(FLOAT)
        back[:, pl.ds(pl.multiple_of(owner * 128, 128), 128)] = piece[2 * rows : 3 * rows, 384:].astype(FLOAT)
    return [fetch(stage, out.at[layer], sems.at[k]) for k, (stage, out) in enumerate(zip(stages, outs))]


def finish_tokens(info, own, near, across, target, done, sems):
    section = info[4]
    copies = []
    for k, piece in enumerate((own, near.at[0], across.at[0], across.at[1])):
        owner = section ^ k
        to = target.at[owner >> 1, pl.ds(pl.multiple_of((owner & 1) * TOKENS, TOKENS), TOKENS)]
        copies.append(fetch(piece, to, sems.at[k]))
    done[...] = jnp.zeros((8, 128), FLOAT)
    for copy in copies:
        copy.wait()


def finish_one(shards, info, own, near, across, beyond, up, down, proj, back, *scratch):
    section, sems = info[4], scratch[-1]
    copies = place_shares(1, shards, section, (own, near, across, beyond), (up, down, proj, back), scratch[:4], sems)
    for copy in copies:
        copy.wait()


def finish_zero(shards, info, own, near, across, beyond, _up, _down, _proj, _back,
                up, down, proj, back, *refs):
    section, dp = info[4], info[5]
    vectors, vector_stages, stages = refs[:7], refs[7:14], refs[14:18]
    small, sems, vector_sems = refs[18:]
    pieces = (own, near, across, beyond)
    copies = place_shares(0, shards, section, pieces, (up, down, proj, back), stages, sems)
    width = WIDTH // shards
    for k in range(4):
        small[section ^ k, :, :] = pieces[k][3 * width :, :]
    total = jnp.concatenate([small[k, :, :] for k in range(4)], axis=0)

    def taken(start, columns):
        pick = (iota((WIDTH, columns), 0) == start + iota((WIDTH, columns), 1)).astype(FLOAT).astype(BRAIN)
        return dot(total, pick)

    gain_a, bias_a, bias_o, gain_f, bias_f, bias_u, bias_d = vector_stages
    part = taken(dp * width, width)
    for layer in range(2):
        attend, feed = 32 * layer, 32 * layer + 16
        for start, outs in ((attend, (gain_a, bias_a, bias_o)), (feed, (gain_f, bias_f, bias_d))):
            for k, out in enumerate(outs):
                out[layer : layer + 1, :] = part[start + k : start + k + 1]
    wide = FF // shards
    per_row = WIDTH // wide
    part = taken(dp % per_row * wide, wide)
    for layer in range(2):
        row = part[32 * layer + 3 : 32 * layer + 4]
        for k in range(1, 4):
            at = 32 * layer + 16 * (k // 2) + 3 + k % 2
            row = jnp.where(dp // per_row == k, part[at : at + 1], row)
        bias_u[layer : layer + 1, :] = row
    copies += [fetch(stage, out, vector_sems.at[k]) for k, (stage, out) in enumerate(zip(vector_stages, vectors))]
    for copy in copies:
        copy.wait()


def swap(block, partner):
    sections = lax.axis_size("section")
    pairs = []
    for dp in range(lax.axis_size("dp")):
        for section in range(sections):
            to_dp, to_section = partner(dp, section)
            pairs.append((dp * sections + section, to_dp * sections + to_section))
    return lax.ppermute(block, ("dp", "section"), pairs)


def over_section(block, bits):
    return swap(block, lambda dp, section: (dp, section ^ bits))


def there(*arrays):
    return [(VMEM, pltpu.with_memory_space_constraint(array, pltpu.VMEM)) for array in arrays]


def in_hbm(*arrays):
    return [(ANY, pltpu.with_memory_space_constraint(array, pltpu.HBM)) for array in arrays]


class Reduction:
    def __init__(self, line, name, orders, *send):
        self.line, self.name = line, name
        self.bits = lax.axis_size("dp").bit_length() - 1
        self.orders = [axes_of(order, self.bits) for order in orders]
        self.came = [over_section(part, 1) for part in send]
        self.done = 0

    def partner(self, dp, section):
        axis = self.orders[section & 1][self.done]
        return (dp, section ^ 2) if axis == "x" else (dp ^ (1 << axis), section)

    def keep(self, *blocks):
        self.mine = list(blocks)

    def height(self, other):
        arrays = self.mine + (other.mine if other is not None else [])
        return sum(array.shape[1] * array.shape[2] for array in arrays) // WIDTH

    def pairs(self):
        return [pair for mine, came in zip(self.mine, self.came) for pair in there(mine, came)]

    def step(self, other=None, small=None):
        pairs = self.pairs() + (other.pairs() if other is not None else [])
        dims = [self.mine[0].shape[0] // 2, self.height(other), WIDTH]
        body = add_halves
        if small is not None:
            body = functools.partial(add_first, [self.bits - order.index("x") for order in self.orders])
            pairs += there(small, over_section(small, 1))
            dims[1] += small.shape[1]
        give, mine = self.line.call(body, [vmem(dims)] * 2, pairs, [], 0.2, self.name + str(self.done))
        self.mine, self.came = [mine], [swap(give, self.partner)]
        self.done += 1

    def last(self, other=None):
        while self.done <= self.bits:
            self.step(other)
            other = None
        pairs = self.pairs() + (other.pairs() if other is not None else [])
        rows = self.height(other)
        (total,) = self.line.call(add_last, [vmem((rows, WIDTH))], pairs, [], 0.1, self.name + "_last")
        return total


def over_all_sections(share):
    across = over_section(share, 2)
    return share, over_section(share, 1), across, over_section(across, 1)


def exchange_near(own, far, near):
    came = over_section(near, 1)
    return own, came, jnp.concatenate([far[None], came[1:]], axis=0)


def finish_rows(line, own, near, across, name):
    outs = [shape((2, 2 * TOKENS, 128)), vmem((8, 128), FLOAT)]
    target, line.last = line.call(
        finish_tokens, outs, [(ANY, array) for array in (own, near, across)],
        [pltpu.SemaphoreType.DMA((4,))], 1.2, name, out_specs=[ANY, VMEM],
    )
    return target


def local(inputs, lengths, ag, ab, wp, wo, ob, fg, fb, wu, ub, wd, db, cotangent):
    shards = lax.axis_size("dp")
    ids = jnp.stack([lax.axis_index("section"), lax.axis_index("dp")]).astype(jnp.int32)
    line = Line()

    rows, wide, tall = vmem((TOKENS, WIDTH)), vmem((TOKENS, FF)), vmem((TOKENS, 3 * WIDTH))
    rows_float, double_float = vmem((TOKENS, WIDTH), FLOAT), vmem((TOKENS, 2 * WIDTH), FLOAT)
    coarse_shape, far_shape = vmem((TOKENS, 2 * WIDTH)), vmem((16, 2 * WIDTH))
    prob_shape = vmem((GROUPS, 2, KEYS, QROWS))
    bias_shape = vmem((TOKENS + 16, 128), FLOAT)
    sums_shape = vmem((8, WIDTH), FLOAT)
    piece, two_pieces = vmem((TOKENS, 128)), vmem((2, TOKENS, 128))
    params = (ag, ab, ob, fg, fb, ub, db, wp, wo, wu, wd)
    (ag, ab, ob, fg, fb, ub, db, wp, wo, wu, wd,
     qkv0, coarse0, far0, prob0, att0, exact0, stream0, mid0, hidden0, slope0, stream1, qkv1, coarse1,
     norm_a0, norm_f0, norm_a1, bias, info, pooled) = line.call(
        functools.partial(first_kernel, shards),
        [vmem(array.shape, array.dtype) for array in params]
        + [tall, coarse_shape, far_shape, prob_shape, rows, rows_float, rows, rows, wide, wide, rows, tall, coarse_shape,
           rows, rows, rows, bias_shape, pltpu.SMEM((8,), jnp.int32), far_shape],
        [(SMEM, ids)] + in_hbm(lengths, inputs, *params),
        [rows, rows, rows_float, pltpu.SMEM((2,), jnp.int32), pltpu.SemaphoreType.DMA((18,))],
        13.5, "layer_zero_forward", out_specs=[VMEM] * 28 + [SMEM, VMEM],
    )
    line.known, line.last = info, pooled
    far1 = over_section(pooled, 1)
    prob1, att1, exact1, mid1, normed1, hidden1, slope1, grad_last = line.call(
        second_kernel, [prob_shape, rows, rows_float, rows, rows, wide, wide, rows],
        in_hbm(cotangent) + there(qkv1, coarse1, far1, bias, stream1, ob, fg, fb, ub, wo, wu),
        [pltpu.SemaphoreType.DMA],
        6.8, "layer_one_forward",
    )

    blocks = vmem((2 * shards, WIDTH // shards, WIDTH))

    dots_shape = vmem((GROUPS, 2, 8, QROWS), FLOAT)
    far_float = vmem((16, 2 * WIDTH), FLOAT)

    pre_grad, sums_f1, send_up, send_down = line.call(
        functools.partial(feed_back_send, 1, shards), [wide, sums_shape, blocks, blocks],
        there(grad_last, hidden1, slope1, wd, normed1), [], 3.2, "feed_back_send_1",
    )
    feed_one = Reduction(line, "feed_one_", FEED_ORDERS[1], send_up, send_down)
    grad3, sums_f1, keep_up, keep_down, grad_out, dots, grad_far = line.call(
        functools.partial(feed_back_keep, 1, shards),
        [rows, sums_shape, blocks, blocks, rows, dots_shape, far_float],
        there(grad_last, normed1, pre_grad, hidden1, mid1, fg, wu, sums_f1, wo, qkv1, far1, prob1, exact1), [rows_float],
        5.5, "feed_back_keep_1",
    )
    grad_far = over_section(grad_far, 1)
    feed_one.keep(keep_up, keep_down)
    feed_one.step()
    grad_q, grad_kv, grad_coarse = line.call(
        attend_back, [rows, double_float, double_float],
        there(qkv1, coarse1, far1, prob1, grad_out, dots), [], 4.3, "attend_back_1",
    )
    qkv_grad, *both = line.call(
        functools.partial(project_back, 1, shards), [tall] + [vmem((2 * shards, WIDTH // shards, WIDTH // 2))] * 4,
        there(grad3, norm_a1, att1, grad_q, grad_kv, grad_coarse, grad_far), [], 3.4, "project_back_1",
    )
    attend_one = Reduction(line, "attend_one_", ATTEND_ORDERS[1], *both[:2])
    attend_one.keep(*both[2:])
    grad2, sums_a1, *out_pieces = line.call(
        functools.partial(project_back_norm, 1, False), [rows, sums_shape, piece, piece, two_pieces],
        there(grad3, stream1, qkv_grad, ag, wp, mid1, hidden1, wd, db), [rows_float, rows], 3.0, "project_back_norm_1",
    )
    out_own, out_near, out_give = exchange_near(*out_pieces)
    out_across = over_section(out_give, 2)
    pre_grad, sums_f0, send_up, send_down = line.call(
        functools.partial(feed_back_send, 0, shards), [wide, sums_shape, blocks, blocks],
        there(grad2, hidden0, slope0, wd, norm_f0), [], 3.7, "feed_back_send_0",
    )
    feed_zero = Reduction(line, "feed_zero_", FEED_ORDERS[0], send_up, send_down)
    line.pin(out_near)
    feed_one.step()
    attend_one.step()
    grad1, sums_f0, keep_up, keep_down, grad_out, dots, grad_far = line.call(
        functools.partial(feed_back_keep, 0, shards),
        [rows, sums_shape, blocks, blocks, rows, dots_shape, far_float],
        there(grad2, norm_f0, pre_grad, hidden0, mid0, fg, wu, sums_f0, wo, qkv0, far0, prob0, exact0), [rows_float],
        5.5, "feed_back_keep_0",
    )
    grad_far = over_section(grad_far, 1)
    feed_zero.keep(keep_up, keep_down)
    line.pin(out_across)
    feed_zero.step()
    grad_q, grad_kv, grad_coarse = line.call(
        attend_back, [rows, double_float, double_float],
        there(qkv0, coarse0, far0, prob0, grad_out, dots), [], 4.3, "attend_back_0",
    )
    attend_one.step()
    line.pin(*feed_one.came)
    qkv_grad, *both = line.call(
        functools.partial(project_back, 0, shards), [tall] + [vmem((2 * shards, WIDTH // shards, WIDTH // 2))] * 4,
        there(grad1, norm_a0, att0, grad_q, grad_kv, grad_coarse, grad_far), [], 0.5, "project_back_0",
    )
    attend_zero = Reduction(line, "attend_zero_", ATTEND_ORDERS[0], *both[:2])
    attend_zero.keep(*both[2:])
    *grad_pieces, small = line.call(
        functools.partial(project_back_norm, 0, True), [piece, piece, two_pieces, vmem((4, 16, WIDTH), FLOAT)],
        there(grad1, stream0, qkv_grad, ag, wp, sums_f1, sums_a1, sums_f0), [rows_float, rows, sums_shape], 5.0,
        "project_back_norm_0",
    )
    grad_own, grad_near, grad_give = exchange_near(*grad_pieces)
    line.pin(*attend_one.came)
    attend_zero.step(small=small)
    feed_one.step(attend_one)
    feed_zero.step()
    line.pin(grad_near)
    attend_zero.step()
    feed_zero.step()
    feed_one.step()
    attend_zero.step()
    grad_across = over_section(grad_give, 2)
    line.pin(grad_across)
    feed_zero.step(attend_zero)
    outputs = finish_rows(line, out_own, out_near, out_across, "finish_outputs")
    input_grad = finish_rows(line, grad_own, grad_near, grad_across, "finish_input_grad")
    share_one = feed_one.last()
    share_zero = feed_zero.last()

    weight_grads = [
        shape((2, WIDTH // shards, FF), FLOAT), shape((2, FF // shards, WIDTH), FLOAT),
        shape((2, WIDTH // shards, 3 * WIDTH), FLOAT), shape((2, WIDTH // shards, WIDTH), FLOAT),
    ]
    stages = [vmem(out.shape[1:], FLOAT) for out in weight_grads]
    stages += [vmem((4, 16, WIDTH)), pltpu.SemaphoreType.DMA((4,))]
    weight_first = line.call(
        functools.partial(finish_one, shards), weight_grads, there(*over_all_sections(share_one)),
        stages, 1.9, "finish_one", out_specs=[ANY] * 4,
    )
    vector = shape((2, WIDTH // shards), FLOAT)
    vectors = [vector] * 5 + [shape((2, FF // shards), FLOAT), vector]
    finished = line.call(
        functools.partial(finish_zero, shards), weight_grads + vectors,
        there(*over_all_sections(share_zero)) + [(ANY, array) for array in weight_first],
        [vmem(out.shape, FLOAT) for out in vectors] + stages + [pltpu.SemaphoreType.DMA((7,))], 3.0, "finish_zero",
        out_specs=[ANY] * 11, aliases={4 + k: k for k in range(4)},
    )
    up_grad, down_grad, proj_grad, back_grad, gain_a, bias_a, bias_o, gain_f, bias_f, bias_u, bias_d = finished
    return (outputs, input_grad, gain_a, bias_a, proj_grad, back_grad, bias_o, gain_f, bias_f, up_grad, bias_u,
            down_grad, bias_d)


def solution(mesh):
    batch = P("dp", None, None)
    split = P("dp", None, "section")
    vector, matrix = P(None, "dp"), P(None, "dp", None)
    return jax.shard_map(
        local,
        mesh=mesh,
        in_specs=(batch, P("dp")) + (P(),) * 11 + (batch,),
        out_specs=(split, split, vector, vector, matrix, matrix, vector, vector, vector, matrix, vector, matrix, vector),
        check_vma=False,
    )
```
